32 devices in a mesh: section: 2 (over core), dp: 4 (over y, x), seq: 4 (over z).
Axes of the slice: x: 2, y: 2, z: 4, core: 2. Of those that a mesh axis runs over, the one named last changes fastest.
Arguments:
- inputs: bfloat16 [16, 2048, 768], P('dp', 'seq'), may hold values from -80 to 80
- shifts: int32 [16], P('dp'), may hold values from -3 to 3, as said below
- flips: int32 [16], P('dp'), may hold values from 0 to 1, as said below
- norm1_gain: float32 [768], replicated, may hold values from 0.25 to 1.75
- norm1_bias: float32 [768], replicated, may hold values from -2.5 to 2.5
- conv1_weight: bfloat16 [5, 768, 768], replicated, may hold values from -0.09375 to 0.09375
- norm2_gain: float32 [768], replicated, may hold values from 0.25 to 1.75
- norm2_bias: float32 [768], replicated, may hold values from -2.5 to 2.5
- dilated_conv2_weight: bfloat16 [3, 768, 384], replicated, may hold values from -0.125 to 0.125
- norm3_gain: float32 [384], replicated, may hold values from 0.25 to 1.75
- norm3_bias: float32 [384], replicated, may hold values from -2.5 to 2.5
- conv3_weight: bfloat16 [384, 768], replicated, may hold values from -0.3125 to 0.3125
- out_grad: bfloat16 [16, 1024, 768], P('dp', 'seq'), may hold values from -6 to 6
Outputs:
- result: bfloat16 [16, 1024, 768], P('dp', 'seq', 'section')
- input_grad: bfloat16 [16, 2048, 768], P('dp', 'seq', 'section')
- conv1_grad: float32 [5, 768, 768], replicated
- norm1_gain_grad: float32 [768], replicated
- norm1_bias_grad: float32 [768], replicated
- conv2_grad: float32 [3, 768, 384], replicated
- norm2_gain_grad: float32 [768], replicated
- norm2_bias_grad: float32 [768], replicated
- conv3_grad: float32 [384, 768], replicated
- norm3_gain_grad: float32 [384], replicated
- norm3_bias_grad: float32 [384], replicated
The draws below stay inside these ranges and needn't reach their ends.
Inputs may be any that keep to these rules, and one draw needn't show every extreme that they name: `shifts`: 3 and -3 both occur. `flips`: both values occur.
All inputs are finite; a program needn't handle non-finite values.
Results may differ from the reference program's by a relative error of at most 0.012.
The reference program's roundings to bfloat16 on the way count: a program that leaves them out, or rounds other values in their place, can miss the bound.
Values may be sent and summed in bfloat16 or wider, within the bound.
A program may use at most 192 MiB of HBM per device.

```python
import math
import jax
import jax.numpy as jnp
from jax import lax

C = 768
H = 384
K1 = 5
K2 = 3
DILATION_SIZE = 11
SHIFT_MAX = 3
MB = 4
SEQ_MB = 1
LIN = 2048
SEQS = 16
POOL = 1024
N_DP = 4


def draw_inputs(key, part):
    subkeys = jax.random.split(jax.random.fold_in(key, 3), 3)
    chan_scale = jnp.exp(jax.random.uniform(subkeys[1], (C,), jnp.float32, math.log(0.3), math.log(3.0)))
    chan_mean = jax.random.uniform(subkeys[2], (C,), jnp.float32, -1.0, 1.0)
    seq_place = jnp.arange(SEQS, dtype=jnp.float32) / max(SEQS - 1, 1)
    bin_place = jnp.arange(LIN, dtype=jnp.float32) / (LIN - 1)
    growth = jnp.exp(0.5 * math.log(3.0) * (seq_place[:, None] + bin_place[None, :]))
    noise_draw = jnp.clip(jax.random.normal(subkeys[0], (SEQS, LIN, C), jnp.float32), -6.0, 6.0)
    return ((noise_draw + chan_mean) * chan_scale * growth[:, :, None]).astype(jnp.bfloat16)


def pick_two(key):
    subkeys = jax.random.split(key, 2)
    first_seq = jax.random.randint(subkeys[0], (), 0, SEQS, jnp.int32)
    second_seq = (first_seq + 1 + jax.random.randint(subkeys[1], (), 0, SEQS - 1, jnp.int32)) % SEQS
    return (first_seq, second_seq)


def draw_shifts(key, part):
    subkeys = jax.random.split(jax.random.fold_in(key, 5), 2)
    amounts = jax.random.randint(subkeys[0], (SEQS,), -SHIFT_MAX, SHIFT_MAX + 1, jnp.int32)
    first_seq, second_seq = pick_two(subkeys[1])
    return amounts.at[first_seq].set(SHIFT_MAX).at[second_seq].set(-SHIFT_MAX)


def draw_flips(key, part):
    subkeys = jax.random.split(jax.random.fold_in(key, 7), 2)
    marks = jax.random.randint(subkeys[0], (SEQS,), 0, 2, jnp.int32)
    first_seq, second_seq = pick_two(subkeys[1])
    return marks.at[first_seq].set(1).at[second_seq].set(0)


def level_of(key, shape, cuts, smallest, largest):
    def one(axis_at, parts):
        draws = jax.random.uniform(jax.random.fold_in(jax.random.fold_in(key, 6), axis_at), (parts,), jnp.float32, smallest / len(cuts), largest / len(cuts))
        return jnp.repeat(jnp.exp(draws), shape[axis_at] // parts).reshape((-1,) + (1,) * (len(shape) - axis_at - 1))

    level = one(*cuts[0])
    for cut in cuts[1:]:
        level = level * one(*cut)
    return level


def normal_values(stream_key, shape, width, most, shards=(), kind=jnp.bfloat16):
    loudness = level_of(stream_key, shape, shards, -0.22, 0.18) if shards else 1.0
    drawn = jax.random.normal(stream_key, shape, jnp.float32) * width * loudness
    return jnp.minimum(jnp.maximum(drawn, -most), most).astype(kind)


def setup_inputs(seed: int = 0) -> dict:
    splits = jax.random.split(jax.random.key(seed), 14)
    inputs = draw_inputs(jax.random.fold_in(splits[13], 71), 0)
    shifts = draw_shifts(jax.random.fold_in(splits[13], 71), 0)
    flips = draw_flips(jax.random.fold_in(splits[13], 71), 0)
    norm1_gain = jnp.clip(1.0 + 0.15 * jax.random.normal(splits[3], (C,), jnp.float32), 0.25, 1.75)
    norm1_bias = normal_values(splits[4], (C,), 0.5, 2.5, (), jnp.float32)
    conv1_weight = normal_values(splits[5], (K1, C, C), (K1 * C) ** -0.5, 0.09375)
    norm2_gain = jnp.clip(1.0 + 0.15 * jax.random.normal(splits[6], (C,), jnp.float32), 0.25, 1.75)
    norm2_bias = normal_values(splits[7], (C,), 0.5, 2.5, (), jnp.float32)
    dilated_conv2_weight = normal_values(splits[8], (K2, C, H), (K2 * C) ** -0.5, 0.125)
    norm3_gain = jnp.clip(1.0 + 0.15 * jax.random.normal(splits[9], (H,), jnp.float32), 0.25, 1.75)
    norm3_bias = normal_values(splits[10], (H,), 0.5, 2.5, (), jnp.float32)
    conv3_weight = normal_values(splits[11], (H, C), H ** -0.5, 0.3125)
    out_grad = normal_values(splits[12], (SEQS, POOL, C), 1.0, 6.0, ((0, 4), (1, 4)))
    return dict(inputs=inputs, shifts=shifts, flips=flips, norm1_gain=norm1_gain, norm1_bias=norm1_bias, conv1_weight=conv1_weight, norm2_gain=norm2_gain, norm2_bias=norm2_bias, dilated_conv2_weight=dilated_conv2_weight, norm3_gain=norm3_gain, norm3_bias=norm3_bias, conv3_weight=conv3_weight, out_grad=out_grad)


EPSILON = 0.001
PRECISE = lax.Precision.HIGHEST

@jax.custom_vjp
def low(v):
    return lax.optimization_barrier(v.astype(jnp.bfloat16)).astype(jnp.float32)

@jax.custom_vjp
def lower_backward(v):
    return v

def low_keep(v):
    return (low(v), None)

def low_pass(kept, grad):
    return (grad,)

def back_keep(v):
    return (v, None)

def back_low(kept, grad):
    return (low(grad),)
low.defvjp(low_keep, low_pass)
lower_backward.defvjp(back_keep, back_low)

def gelu_apply(values):
    return jax.nn.gelu(values, approximate=True)

def batch_norm(values, gain, bias):
    average = lax.optimization_barrier(jnp.mean(values, axis=(0, 1)))
    centred = values - average
    spread = lax.optimization_barrier(jnp.mean(centred * centred, axis=(0, 1)))
    return gain * (centred * lax.rsqrt(spread + EPSILON)) + bias

def apply_kernel_taps(source, weight, stride):
    tap_count = weight.shape[0]
    border_width = (tap_count - 1) // 2 * stride
    extent = source.shape[1]
    padded = jnp.pad(source, ((0, 0), (border_width, border_width), (0, 0)))
    running = jnp.zeros(source.shape[:2] + (weight.shape[2],), jnp.float32)
    for tap_index in range(tap_count):
        window = padded[:, tap_index * stride:tap_index * stride + extent]
        running = running + jnp.einsum('slc,co->slo', window, weight[tap_index], precision=PRECISE)
    return running

def permute(inputs_block, shift_block, flip_block):
    extent = inputs_block.shape[1]
    places = jnp.arange(extent, dtype=jnp.int32)

    def one_row(seq_row, offset, flipped):
        viewed = jnp.where(flipped == 1, extent - 1 - places, places)
        source = jnp.mod(viewed - offset, extent).astype(jnp.int32)
        return jnp.take(seq_row, source, axis=0)
    return jax.vmap(one_row)(inputs_block, shift_block, flip_block)

def micro_batch(weights, inputs_block, shift_block, flip_block):
    gain_one, bias_one, weight_one, gain_two, bias_two, second_weight_matrix, gain_three, bias_three, weight_three = weights
    shifted = lower_backward(permute(inputs_block, shift_block, flip_block))
    first_act = low(gelu_apply(batch_norm(shifted, gain_one, bias_one)))
    wide_out = lower_backward(apply_kernel_taps(first_act, weight_one, 1))
    pair_view = wide_out.reshape(wide_out.shape[0], wide_out.shape[1] // 2, 2, wide_out.shape[2])
    pooled = low(lower_backward(jnp.logaddexp(pair_view[:, :, 0], pair_view[:, :, 1])))
    second_activation = low(gelu_apply(batch_norm(pooled, gain_two, bias_two)))
    narrow_output = lower_backward(apply_kernel_taps(second_activation, second_weight_matrix, DILATION_SIZE))
    third_act = low(gelu_apply(batch_norm(narrow_output, gain_three, bias_three)))
    return pooled + jnp.einsum('slh,hc->slc', third_act, weight_three, precision=PRECISE)

def group_batches(values):
    shaped = values.reshape((N_DP, MB, SEQ_MB) + values.shape[1:])
    return jnp.swapaxes(shaped, 0, 1).reshape((MB, N_DP * SEQ_MB) + values.shape[1:])

def split_batches(values):
    shaped = values.reshape((MB, N_DP, SEQ_MB) + values.shape[2:])
    return jnp.swapaxes(shaped, 0, 1).reshape((N_DP * MB * SEQ_MB,) + values.shape[2:])

def reference(inputs, shifts, flips, norm1_gain, norm1_bias, conv1_weight, norm2_gain, norm2_bias, dilated_conv2_weight, norm3_gain, norm3_bias, conv3_weight, out_grad):
    params = (norm1_gain, norm1_bias, conv1_weight.astype(jnp.float32), norm2_gain, norm2_bias, dilated_conv2_weight.astype(jnp.float32), norm3_gain, norm3_bias, conv3_weight.astype(jnp.float32))
    grouped_shifts = group_batches(shifts)
    grouped_flips = group_batches(flips)

    def forward(values, weights):
        grouped = group_batches(values)

        def one_batch(pieces):
            return micro_batch(weights, pieces[0], pieces[1], pieces[2])
        outputs = lax.map(jax.checkpoint(one_batch), (grouped, grouped_shifts, grouped_flips))
        return split_batches(outputs)
    result, pullback = jax.vjp(forward, inputs.astype(jnp.float32), params)
    input_grad, weight_grads = pullback(out_grad.astype(jnp.float32))
    return (result.astype(jnp.bfloat16), input_grad.astype(jnp.bfloat16), weight_grads[2], weight_grads[0], weight_grads[1], weight_grads[5], weight_grads[3], weight_grads[4], weight_grads[8], weight_grads[6], weight_grads[7])
```

```python
import functools

import jax
import jax.numpy as jnp
from jax import lax
from jax.experimental import pallas as pl
from jax.experimental.pallas import tpu as pltpu
from jax.sharding import PartitionSpec as P

DILATION_SIZE = 11
EPSILON = 0.001
EDGE = 16
MESH = pl.DeviceIdType.MESH
F32 = jnp.float32
BF16 = jnp.bfloat16
SCALE = 0.7978845608028654
CUBIC = 0.044715
TN = (((0,), (0,)), ((), ()))
NT = (((1,), (1,)), ((), ()))


def gelu(u):
    return 0.5 * u * (1.0 + jnp.tanh(SCALE * u * (1.0 + CUBIC * (u * u))))


def gelu_slope(u):
    square = u * u
    t = jnp.tanh(SCALE * u * (1.0 + CUBIC * square))
    return 0.5 * (1.0 + t) + (0.5 * SCALE) * u * (1.0 - t * t) * (1.0 + (3.0 * CUBIC) * square)


def chunks(count, body, carry=0, unroll=1):
    def step(i, carry):
        return body(pl.multiple_of(i * EDGE, EDGE), carry)

    return lax.fori_loop(0, count // EDGE, step, carry, unroll=unroll)


def eight(row):
    return jnp.broadcast_to(row, (8, row.shape[-1]))


def halves(block):
    return block.reshape(block.shape[0] // 8, 8, block.shape[1])


def flat(block):
    return block.reshape(block.shape[0] * 8, block.shape[2])


def row_sum(block):
    return jnp.sum(block, axis=0, keepdims=True)


class Place:
    def __init__(self, nd, nq):
        self.nd, self.nq = nd, nq
        self.s, self.d, self.q = (lax.axis_index(a) for a in ("section", "dp", "seq"))
        self.mirror = nq - 1 - self.q
        self.next = lax.rem(self.q + 1, nq)
        self.prev = lax.rem(self.q + nq - 1, nq)
        self.partner = (1 - self.s, self.d, self.q)

    def plane(self):
        return [(self.s, lax.rem(self.d + i, self.nd), self.q) for i in range(1, self.nd)]

    def line(self):
        return [(self.s, self.d, lax.rem(self.q + i, self.nq)) for i in range(1, self.nq)]

    def greet(self, devices):
        barrier = pltpu.get_barrier_semaphore()
        for device in devices:
            pl.semaphore_signal(barrier, inc=1, device_id=device, device_id_type=MESH)
        pl.semaphore_wait(barrier, len(devices))


def remote(src, dst, send_sem, recv_sem, device):
    return pltpu.make_async_remote_copy(
        src_ref=src,
        dst_ref=dst,
        send_sem=send_sem,
        recv_sem=recv_sem,
        device_id=device,
        device_id_type=MESH,
    )


class Exchange:
    def __init__(self, place, number, plane_buf, line_buf, send_sem, recv_sem):
        self.place, self.number = place, number
        self.plane_buf, self.line_buf = plane_buf.at[number], line_buf.at[number]
        self.send_sem, self.recv_sem = send_sem.at[number], recv_sem.at[number]

    def _start(self, buf, slot, rows, devices, base):
        for at, row in enumerate(rows):
            buf[slot, at : at + 1, 0 : row.shape[1]] = row
        self.copies = [
            remote(
                buf.at[slot],
                buf.at[slot],
                self.send_sem.at[base + i],
                self.recv_sem.at[base + i],
                device,
            )
            for i, device in enumerate(devices)
        ]
        for copy in self.copies:
            copy.start()

    def _finish(self, buf, count, n_rows, width):
        for copy in self.copies:
            copy.wait()
        return [[buf[j, at : at + 1, 0:width] for at in range(n_rows)] for j in range(count)]

    def start(self, rows):
        self.n_rows, self.width = len(rows), rows[0].shape[1]
        self._start(self.plane_buf, self.place.d, rows, self.place.plane(), 0)

    def relay(self, join):
        parts = self._finish(self.plane_buf, self.place.nd, self.n_rows, self.width)
        self._start(
            self.line_buf, self.place.q, join(parts), self.place.line(), self.place.nd - 1
        )

    def finish(self, join):
        return join(self._finish(self.line_buf, self.place.nq, self.n_rows, self.width))


def join_sums(parts):
    totals = parts[0]
    for part in parts[1:]:
        totals = [total + row for total, row in zip(totals, part)]
    return totals


def join_moments(count):
    def join(parts):
        n = len(parts[0]) // 2
        totals = join_sums(parts)
        means = [total * (1.0 / len(parts)) for total in totals[:n]]
        squares = totals[n:]
        for part in parts:
            squares = [
                square + count * (row - mean) * (row - mean)
                for square, row, mean in zip(squares, part[:n], means)
            ]
        return means + squares

    return join


class Norm:
    def __init__(self, mean, inv, gain, bias):
        self.mean, self.inv, self.gain, self.bias = eight(mean), eight(inv), eight(gain), eight(bias)

    def normed(self, block):
        return (block - self.mean[None]) * self.inv[None]

    def pre(self, normed):
        return normed * self.gain[None] + self.bias[None]


def first_kernel(
    dims,
    inputs,
    out_grad,
    shifts,
    flips,
    gain1,
    bias1,
    weight1,
    gain2,
    bias2,
    weight2,
    gain3,
    bias3,
    weight3,
    taps_out,
    placed_out,
    grad_out,
    halo_out,
    stats_out,
    sums_out,
    result_out,
    conv2_out,
    conv3_out,
    window,
    placed,
    act,
    taps,
    w1,
    w2,
    w3,
    even,
    odd,
    share,
    pooled,
    edges,
    edges_in,
    second,
    narrow,
    own_grad,
    far_grad,
    third_in,
    third,
    narrow_grad,
    narrow_taps,
    second_grad,
    conv2_grad,
    conv3_grad,
    wide_grad,
    halo,
    ours,
    near,
    far,
    stats,
    sums,
    plane_buf,
    line_buf,
    local_sem,
    exchange_send,
    exchange_recv,
    halo_send,
    halo_recv,
    far_send,
    far_recv,
    result_send,
    result_recv,
):
    C, H, L, B, nd, nq = dims
    half = L // 2
    rows = B * half
    place = Place(nd, nq)
    s, q = place.s, place.q
    cross = (1 - s, place.d, place.mirror)
    place.greet(place.plane() + place.line() + [place.partner, cross])

    flip = [flips[s * B + b] for b in range(B)]
    shift = [shifts[s * B + b] for b in range(B)]
    block_at = [flip[b] * (nq - 1 - q) + (1 - flip[b]) * q for b in range(B)]
    mine = pl.ds(s * B, B)

    def exchange(number):
        return Exchange(place, number, plane_buf, line_buf, exchange_send, exchange_recv)

    def pair(number, to_next, to_prev, from_prev, from_next):
        return [
            remote(
                to_next,
                from_prev,
                halo_send.at[number, 0],
                halo_recv.at[number, 0],
                (s, place.d, place.next),
            ),
            remote(
                to_prev,
                from_next,
                halo_send.at[number, 1],
                halo_recv.at[number, 1],
                (s, place.d, place.prev),
            ),
        ]

    load = [
        pltpu.make_async_copy(inputs.at[mine], window.at[:, EDGE : EDGE + L], local_sem.at[0]),
        pltpu.make_async_copy(weight1, w1, local_sem.at[1]),
        pltpu.make_async_copy(weight2, w2, local_sem.at[2]),
        pltpu.make_async_copy(weight3, w3, local_sem.at[3]),
        pltpu.make_async_copy(out_grad.at[mine], own_grad, local_sem.at[4]),
    ]
    for copy in load:
        copy.start()
    ring = pair(
        0,
        inputs.at[mine, L - EDGE : L],
        inputs.at[mine, 0:EDGE],
        window.at[:, 0:EDGE],
        window.at[:, EDGE + L : 2 * EDGE + L],
    )
    for copy in ring:
        copy.start()

    load[0].wait()
    zero = jnp.zeros((8, C), F32)

    def moments(read, count, width):
        none = jnp.zeros((8, width), F32)
        means, squares = [], []
        for b in range(B):
            total = chunks(count, lambda r, t: t + jnp.sum(halves(read(b, r)), axis=0), none, 2)
            mean = row_sum(total) * (1.0 / count)
            mean8 = eight(mean)

            def deviations(r, t):
                away = halves(read(b, r)) - mean8[None]
                return t + jnp.sum(away * away, axis=0)

            means.append(mean)
            squares.append(row_sum(chunks(count, deviations, none, 2)))
        return means + squares

    def norms(exchange, count, gain, bias):
        exchange.relay(join_moments(float(count)))
        joined = exchange.finish(join_moments(float(count * nd)))
        scale = 1.0 / (count * nd * nq)
        inverse = [lax.rsqrt(square * scale + EPSILON) for square in joined[B:]]
        return [Norm(joined[b], inverse[b], gain[...], bias[...]) for b in range(B)]

    step = exchange(0)
    step.start(
        moments(lambda b, r: window[b, pl.ds(EDGE + r, EDGE)].astype(F32), L, C)
    )

    for copy in ring:
        copy.wait()
    tall = half + EDGE
    for b in range(B):
        for parity in range(2):
            shape = (tall, L + 2 * EDGE)
            at = 2 * (lax.broadcasted_iota(jnp.int32, shape, 0) - 8) + parity
            source = flip[b] * (L - 1) + (1 - 2 * flip[b]) * at - shift[b] + EDGE
            pick = jnp.where(lax.broadcasted_iota(jnp.int32, shape, 1) == source, 1.0, 0.0)
            placed[b, parity] = jnp.dot(
                pick.astype(BF16), window[b], preferred_element_type=F32
            ).astype(BF16)
    first_norm = norms(step, L, gain1, bias1)
    mirrored = remote(
        out_grad.at[mine],
        far_grad,
        far_send.at[0],
        far_recv.at[0],
        (s, place.d, place.mirror),
    )
    mirrored.start()
    save = [pltpu.make_async_copy(placed, placed_out, local_sem.at[5])]
    save[0].start()

    for b in range(B):
        stats[b : b + 1, :] = first_norm[b].mean[0:1]
        stats[B + b : B + b + 1, :] = first_norm[b].inv[0:1]
        for parity in range(2):

            def activate(r, c):
                norm = first_norm[b]
                value = gelu(norm.pre(norm.normed(halves(placed[b, parity, pl.ds(r, EDGE)].astype(F32)))))
                value = flat(value)
                at = lax.broadcasted_iota(jnp.int32, value.shape, 0) + (r - 8)
                at = 2 * at + (parity + block_at[b] * L)
                act[pl.ds(r, EDGE)] = jnp.where((at >= 0) & (at < nq * L), value, 0.0)
                return c

            chunks(tall, activate)

            def spread(r, c):
                values = act[pl.ds(r, 2 * EDGE)]
                for off in range(3):
                    at = (2 * off + parity) * C
                    taps[pl.ds(b * half + r, EDGE), at : at + C] = values[
                        7 + off : 7 + off + EDGE
                    ].astype(BF16)
                return c

            chunks(half, spread)
    save.append(pltpu.make_async_copy(taps, taps_out, local_sem.at[6]))
    save[1].start()

    load[1].wait()
    wide = even.shape[1]
    for j in range(C // wide):
        cols = slice(j * wide, (j + 1) * wide)
        even[...] = jnp.dot(taps[:, 0 : 5 * C], w1[:, cols], preferred_element_type=F32)
        odd[...] = jnp.dot(taps[:, C : 6 * C], w1[:, cols], preferred_element_type=F32)
        for b in range(B):

            def pool(r, c):
                at = pl.ds(b * half + r, EDGE)
                left, right = even[at, :], odd[at, :]
                away = left - right
                small = jnp.exp(-jnp.abs(away))
                pooled[b, pl.ds(EDGE + r, EDGE), cols] = (
                    jnp.maximum(left, right) + jnp.log(1.0 + small)
                ).astype(BF16)
                part = 1.0 / (1.0 + small)
                share[at, cols] = jnp.where(away >= 0, part, small * part)
                return c

            chunks(half, pool)

    def send_edges(number, first, last, width):
        for b in range(B):
            for at, (head, tail) in enumerate(zip(first(b), last(b))):
                head, tail = head.astype(F32), tail.astype(F32)
                turned = flip[b] == 1
                place_at = at * B + b
                edges[number, 0, place_at, :, 0:width] = jnp.where(turned, head, tail).astype(BF16)
                edges[number, 1, place_at, :, 0:width] = jnp.where(turned, tail, head).astype(BF16)
        copies = pair(
            number + 1,
            edges.at[number, 0],
            edges.at[number, 1],
            edges_in.at[number, 0],
            edges_in.at[number, 1],
        )
        for copy in copies:
            copy.start()
        return copies

    def take_edges(number, at, b, width):
        from_prev = edges_in[number, 0, at * B + b, :, 0:width].astype(F32)
        from_next = edges_in[number, 1, at * B + b, :, 0:width].astype(F32)
        turned = flip[b] == 1
        before = jnp.where(turned, from_next, from_prev)
        after = jnp.where(turned, from_prev, from_next)
        before = jnp.where(block_at[b] > 0, before, 0.0)
        after = jnp.where(block_at[b] < nq - 1, after, 0.0)
        return before, after

    step = exchange(1)
    step.start(moments(lambda b, r: pooled[b, pl.ds(EDGE + r, EDGE)].astype(F32), half, C))
    ring = send_edges(
        0,
        lambda b: [pooled[b, EDGE : 2 * EDGE]],
        lambda b: [pooled[b, half : half + EDGE]],
        C,
    )
    second_norm = norms(step, half, gain2, bias2)
    for copy in ring:
        copy.wait()
    for b in range(B):
        before, after = take_edges(0, 0, b, C)
        pooled[b, 0:EDGE] = before.astype(BF16)
        pooled[b, EDGE + half : 2 * EDGE + half] = after.astype(BF16)
        norm = second_norm[b]

        def activate(r, c):
            value = flat(gelu(norm.pre(norm.normed(halves(pooled[b, pl.ds(r, EDGE)].astype(F32))))))
            at = lax.broadcasted_iota(jnp.int32, value.shape, 0) + (r - EDGE + block_at[b] * half)
            act[pl.ds(r, EDGE)] = jnp.where((at >= 0) & (at < nq * half), value, 0.0)
            return c

        chunks(half + 2 * EDGE, activate)

        def spread(r, c):
            values = act[pl.ds(r, 3 * EDGE)]
            for k in range(3):
                at = EDGE + (k - 1) * DILATION_SIZE
                second[pl.ds(b * half + r, EDGE), k * C : (k + 1) * C] = values[
                    at : at + EDGE
                ].astype(BF16)
            return c

        chunks(half, spread)

    load[2].wait()
    narrow[...] = jnp.dot(second[...], w2[...], preferred_element_type=F32)
    step = exchange(2)
    step.start(moments(lambda b, r: narrow[pl.ds(b * half + r, EDGE)], half, H))
    load[3].wait()
    load[4].wait()
    mirrored.wait()
    for b in range(B):

        def choose(r, c):
            at = pl.ds(r, EDGE)
            own_grad[b, at] = jnp.where(
                flip[b] == 1, far_grad[b, at].astype(F32), own_grad[b, at].astype(F32)
            ).astype(BF16)
            return c

        chunks(half, choose)
        third_in[b * half : (b + 1) * half] = lax.dot_general(
            own_grad[b], w3[...], NT, preferred_element_type=F32
        )
    third_norm = norms(step, half, gain3, bias3)

    none = jnp.zeros((8, H), F32)
    totals = []
    for b in range(B):
        norm = third_norm[b]

        def activate(r, carry):
            at = pl.ds(b * half + r, EDGE)
            normed = norm.normed(halves(narrow[at]))
            pre = norm.pre(normed)
            third[at] = flat(gelu(pre)).astype(BF16)
            grad = halves(third_in[at]) * gelu_slope(pre)
            third_in[at] = flat(grad)
            return carry[0] + jnp.sum(grad, axis=0), carry[1] + jnp.sum(grad * normed, axis=0)

        totals.append(chunks(half, activate, (none, none)))
    step = exchange(3)
    step.start([row_sum(t[0]) for t in totals] + [row_sum(t[1]) for t in totals])

    for b in range(B):
        at = slice(b * half, (b + 1) * half)
        for side in range(2):
            cols = slice(side * (C // 2), (side + 1) * (C // 2))
            ours[side, b] = (
                pooled[b, EDGE : EDGE + half, cols].astype(F32)
                + jnp.dot(third[at], w3[:, cols], preferred_element_type=F32)
            ).astype(BF16)
    step.relay(join_sums)
    away = [
        remote(
            ours.at[side],
            far.at[mine],
            result_send.at[i],
            result_recv.at[i],
            (side, place.d, place.mirror),
        )
        for i, side in enumerate((s, 1 - s))
    ]
    across = remote(
        ours.at[1 - s], near.at[mine], result_send.at[2], result_recv.at[2], place.partner
    )
    conv3_grad[...] = sum(
        lax.dot_general(
            third[b * half : (b + 1) * half], own_grad[b], TN, preferred_element_type=F32
        )
        for b in range(B)
    ).astype(BF16)
    back = step.finish(join_sums)
    for copy in away + [across]:
        copy.start()
    save.append(pltpu.make_async_copy(conv3_grad, conv3_out, local_sem.at[7]))
    save[2].start()
    sums[4:5, 0:H] = sum(back[B:])
    sums[5:6, 0:H] = sum(back[:B])
    scale = 1.0 / (half * nd * nq)
    for b in range(B):
        norm = third_norm[b]
        mean_bias, mean_gain = eight(back[b] * scale), eight(back[B + b] * scale)
        factor = norm.gain * norm.inv

        def input_grad(r, c):
            at = pl.ds(b * half + r, EDGE)
            normed = norm.normed(halves(narrow[at]))
            value = factor[None] * (halves(third_in[at]) - mean_bias[None] - normed * mean_gain[None])
            narrow_grad[b, pl.ds(EDGE + r, EDGE)] = flat(value).astype(BF16)
            return c

        chunks(half, input_grad)
    ring = send_edges(
        1,
        lambda b: [narrow_grad[b, EDGE : 2 * EDGE]],
        lambda b: [narrow_grad[b, half : half + EDGE]],
        H,
    )
    for k in range(3):
        conv2_grad[k * C : (k + 1) * C] = sum(
            lax.dot_general(
                second[b * half : (b + 1) * half, k * C : (k + 1) * C],
                narrow_grad[b, EDGE : EDGE + half],
                TN,
                preferred_element_type=F32,
            )
            for b in range(B)
        ).astype(BF16)
    save.append(pltpu.make_async_copy(conv2_grad, conv2_out, local_sem.at[8]))
    save[3].start()
    for copy in ring:
        copy.wait()
    for b in range(B):
        before, after = take_edges(1, 0, b, H)
        narrow_grad[b, 0:EDGE] = before.astype(BF16)
        narrow_grad[b, EDGE + half : 2 * EDGE + half] = after.astype(BF16)

        def spread(r, c):
            values = narrow_grad[b, pl.ds(r, 3 * EDGE)].astype(F32)
            for k in range(3):
                at = EDGE - (k - 1) * DILATION_SIZE
                narrow_taps[pl.ds(b * half + r, EDGE), k * H : (k + 1) * H] = values[
                    at : at + EDGE
                ].astype(BF16)
            return c

        chunks(half, spread)
    second_grad[...] = sum(
        lax.dot_general(
            narrow_taps[:, k * H : (k + 1) * H],
            w2[k * C : (k + 1) * C],
            NT,
            preferred_element_type=F32,
        )
        for k in range(3)
    )
    totals = []
    for b in range(B):
        norm = second_norm[b]

        def slope(r, carry):
            at = pl.ds(b * half + r, EDGE)
            normed = norm.normed(halves(pooled[b, pl.ds(EDGE + r, EDGE)].astype(F32)))
            grad = halves(second_grad[at]) * gelu_slope(norm.pre(normed))
            second_grad[at] = flat(grad)
            return carry[0] + jnp.sum(grad, axis=0), carry[1] + jnp.sum(grad * normed, axis=0)

        totals.append(chunks(half, slope, (zero, zero)))
    step = exchange(4)
    step.start([row_sum(t[0]) for t in totals] + [row_sum(t[1]) for t in totals])
    step.relay(join_sums)
    back = step.finish(join_sums)
    sums[2:3, :] = sum(back[B:])
    sums[3:4, :] = sum(back[:B])
    for b in range(B):
        norm = second_norm[b]
        mean_bias, mean_gain = eight(back[b] * scale), eight(back[B + b] * scale)
        factor = norm.gain * norm.inv

        def unpool(r, c):
            at = pl.ds(b * half + r, EDGE)
            normed = norm.normed(halves(pooled[b, pl.ds(EDGE + r, EDGE)].astype(F32)))
            value = factor[None] * (
                halves(second_grad[at]) - mean_bias[None] - normed * mean_gain[None]
            )
            value = flat(value) + own_grad[b, pl.ds(r, EDGE)].astype(F32)
            value = value.astype(BF16).astype(F32)
            part = share[at]
            wide_grad[0, at] = (value * part).astype(BF16)
            wide_grad[1, at] = (value * (1.0 - part)).astype(BF16)
            return c

        chunks(half, unpool)
    ring = send_edges(
        2,
        lambda b: [wide_grad[p, b * half : b * half + EDGE] for p in range(2)],
        lambda b: [wide_grad[p, (b + 1) * half - EDGE : (b + 1) * half] for p in range(2)],
        C,
    )
    save.append(pltpu.make_async_copy(wide_grad, grad_out, local_sem.at[9]))
    save[4].start()
    for copy in away + [across]:
        copy.wait()
    for b in range(B):
        near[s * B + b] = ours[s, b]
    for b in range(2 * B):
        turned = flips[b]

        def deliver(r, c):
            at = pl.ds(r, EDGE)
            near[b, at] = jnp.where(
                turned == 1, far[b, at].astype(F32), near[b, at].astype(F32)
            ).astype(BF16)
            return c

        chunks(half, deliver)
    save.append(pltpu.make_async_copy(near, result_out, local_sem.at[10]))
    save[5].start()
    for copy in ring:
        copy.wait()
    for b in range(B):
        for parity in range(2):
            before, after = take_edges(2, parity, b, C)
            halo[0, parity, b] = before.astype(BF16)
            halo[1, parity, b] = after.astype(BF16)
    save += [
        pltpu.make_async_copy(halo, halo_out, local_sem.at[11]),
        pltpu.make_async_copy(stats, stats_out, local_sem.at[12]),
        pltpu.make_async_copy(sums, sums_out, local_sem.at[13]),
    ]
    for copy in save[6:]:
        copy.start()
    for copy in save:
        copy.wait()


def weight_kernel(even, odd, even_grad, odd_grad, out):
    out[...] = (
        lax.dot_general(even[...], even_grad[0], TN, preferred_element_type=F32)
        + lax.dot_general(odd[...], odd_grad[0], TN, preferred_element_type=F32)
    ).astype(BF16)


def last_kernel(
    dims,
    placed_in,
    grad_in,
    halo_in,
    stats,
    sums_in,
    shifts,
    flips,
    gain1,
    bias1,
    weight1,
    out,
    sums_out,
    placed,
    grads,
    halo,
    w1,
    taps,
    act_grad,
    edges,
    edges_in,
    window,
    ours,
    final,
    sums,
    plane_buf,
    line_buf,
    local_sem,
    exchange_send,
    exchange_recv,
    halo_send,
    halo_recv,
    core_send,
    core_recv,
):
    C, H, L, B, nd, nq = dims
    half = L // 2
    place = Place(nd, nq)
    s, q = place.s, place.q
    place.greet(place.plane() + place.line() + [place.partner])
    flip = [flips[s * B + b] for b in range(B)]
    shift = [shifts[s * B + b] for b in range(B)]
    load = [
        pltpu.make_async_copy(grad_in, grads, local_sem.at[0]),
        pltpu.make_async_copy(halo_in, halo, local_sem.at[1]),
        pltpu.make_async_copy(weight1, w1, local_sem.at[2]),
        pltpu.make_async_copy(placed_in, placed, local_sem.at[3]),
    ]
    for copy in load:
        copy.start()
    load[0].wait()
    load[1].wait()
    for b in range(B):
        for parity in range(2):
            base = (1 - parity) * C

            def put(r, values):
                for at in range(3):
                    lanes = base + 2 * at * C
                    taps[pl.ds(b * half + r, EDGE), lanes : lanes + C] = values[
                        EDGE + 1 - at : 2 * EDGE + 1 - at
                    ].astype(BF16)

            def spread(r, c):
                put(r, grads[parity, pl.ds(b * half + r - EDGE, 3 * EDGE)].astype(F32))
                return c

            lax.fori_loop(
                1, half // EDGE - 1, lambda i, c: spread(pl.multiple_of(i * EDGE, EDGE), c), 0
            )
            low, high = b * half, (b + 1) * half
            put(
                0,
                jnp.concatenate(
                    [halo[0, parity, b], grads[parity, low : low + 2 * EDGE]], axis=0
                ).astype(F32),
            )
            put(
                half - EDGE,
                jnp.concatenate(
                    [grads[parity, high - 2 * EDGE : high], halo[1, parity, b]], axis=0
                ).astype(F32),
            )
    load[2].wait()
    load[3].wait()
    for parity in range(2):

        def convolve(j, c):
            cols = pl.multiple_of(j * 256, 256)
            total = None
            for k in range(5):
                lanes = (k + 1 - parity) * C
                part = lax.dot_general(
                    taps[:, lanes : lanes + C],
                    w1[k, pl.ds(cols, 256), :],
                    NT,
                    preferred_element_type=F32,
                )
                total = part if total is None else total + part
            act_grad[parity, :, pl.ds(cols, 256)] = total
            return c

        lax.fori_loop(0, C // 256, convolve, 0)
    norms = [
        Norm(stats[b : b + 1, :], stats[B + b : B + b + 1, :], gain1[...], bias1[...])
        for b in range(B)
    ]
    zero = jnp.zeros((8, C), F32)
    totals = []
    for b in range(B):
        norm = norms[b]
        carry = (zero, zero)
        for parity in range(2):

            def slope(r, carry):
                at = pl.ds(b * half + r, EDGE)
                values = placed[b, parity, pl.ds(r, 2 * EDGE)].astype(F32)[8 : 8 + EDGE]
                normed = norm.normed(halves(values))
                grad = halves(act_grad[parity, at]) * gelu_slope(norm.pre(normed))
                act_grad[parity, at] = flat(grad)
                return carry[0] + jnp.sum(grad, axis=0), carry[1] + jnp.sum(grad * normed, axis=0)

            carry = chunks(half, slope, carry)
        totals.append(carry)
    step = Exchange(place, 0, plane_buf, line_buf, exchange_send, exchange_recv)
    step.start([row_sum(t[0]) for t in totals] + [row_sum(t[1]) for t in totals])
    step.relay(join_sums)
    back = step.finish(join_sums)
    sums[0] = sums_in[...]
    sums[0, 0:1, :] = sum(back[B:])
    sums[0, 1:2, :] = sum(back[:B])
    swap = remote(sums.at[0], sums.at[1], core_send.at[0], core_recv.at[0], place.partner)
    swap.start()
    scale = 1.0 / (L * nd * nq)
    for b in range(B):
        norm = norms[b]
        mean_bias, mean_gain = eight(back[b] * scale), eight(back[B + b] * scale)
        factor = norm.gain * norm.inv
        for parity in range(2):

            def input_grad(r, c):
                values = placed[b, parity, pl.ds(r, 2 * EDGE)].astype(F32)[8 : 8 + EDGE]
                normed = norm.normed(halves(values))
                value = factor[None] * (
                    halves(act_grad[parity, pl.ds(b * half + r, EDGE)])
                    - mean_bias[None]
                    - normed * mean_gain[None]
                )
                window[b, pl.ds(parity * (half + 2 * EDGE) + EDGE + r, EDGE)] = flat(value).astype(
                    BF16
                )
                return c

            chunks(half, input_grad)
    for b in range(B):
        turned = flip[b] == 1
        for parity in range(2):
            low = parity * (half + 2 * EDGE)
            head = window[b, low + EDGE : low + 2 * EDGE].astype(F32)
            tail = window[b, low + half : low + half + EDGE].astype(F32)
            edges[0, parity, b] = jnp.where(turned, head, tail).astype(BF16)
            edges[1, parity, b] = jnp.where(turned, tail, head).astype(BF16)
    ring = [
        remote(
            edges.at[i],
            edges_in.at[i],
            halo_send.at[i],
            halo_recv.at[i],
            (s, place.d, at),
        )
        for i, at in enumerate((place.next, place.prev))
    ]
    for copy in ring:
        copy.start()
    for copy in ring:
        copy.wait()
    for b in range(B):
        turned = flip[b] == 1
        for parity in range(2):
            low = parity * (half + 2 * EDGE)
            from_prev = edges_in[0, parity, b].astype(F32)
            from_next = edges_in[1, parity, b].astype(F32)
            window[b, low : low + EDGE] = jnp.where(turned, from_next, from_prev).astype(BF16)
            window[b, low + EDGE + half : low + 2 * EDGE + half] = jnp.where(
                turned, from_prev, from_next
            ).astype(BF16)
        shape = (L, 2 * (half + 2 * EDGE))
        at = lax.broadcasted_iota(jnp.int32, shape, 0) + shift[b]
        at = flip[b] * (L - 1) + (1 - 2 * flip[b]) * at
        source = (at & 1) * (half + 2 * EDGE) + (at >> 1) + EDGE
        pick = jnp.where(lax.broadcasted_iota(jnp.int32, shape, 1) == source, 1.0, 0.0).astype(BF16)
        for side in range(2):
            cols = slice(side * (C // 2), (side + 1) * (C // 2))
            ours[side, b] = jnp.dot(pick, window[b, :, cols], preferred_element_type=F32).astype(
                BF16
            )
    across = remote(
        ours.at[1 - s],
        final.at[pl.ds(s * B, B)],
        core_send.at[1],
        core_recv.at[1],
        place.partner,
    )
    across.start()
    keep = pltpu.make_async_copy(ours.at[s], out.at[pl.ds(s * B, B)], local_sem.at[4])
    keep.start()
    swap.wait()
    sums_out[...] = sums[0] + sums[1]
    across.wait()
    other = pl.ds((1 - s) * B, B)
    give = pltpu.make_async_copy(final.at[other], out.at[other], local_sem.at[5])
    give.start()
    keep.wait()
    give.wait()


def on_device(
    nd,
    nq,
    inputs,
    shifts,
    flips,
    gain1,
    bias1,
    weight1,
    gain2,
    bias2,
    weight2,
    gain3,
    bias3,
    weight3,
    out_grad,
):
    sequences, L, C = inputs.shape
    H = weight3.shape[0]
    B, half = sequences // 2, L // 2
    rows = B * half
    dims = (C, H, L, B, nd, nq)
    anywhere = pl.BlockSpec(memory_space=pl.ANY)
    vmem = pl.BlockSpec(memory_space=pltpu.VMEM)
    smem = pl.BlockSpec(memory_space=pltpu.SMEM)
    peers = nd - 1 + nq - 1
    shape = jax.ShapeDtypeStruct
    dma = pltpu.SemaphoreType.DMA
    gain1, bias1, gain2, bias2, gain3, bias3 = (
        v.reshape(1, -1) for v in (gain1, bias1, gain2, bias2, gain3, bias3)
    )
    taps, placed, grads, halo, stats, sums, result, conv2, conv3 = pl.pallas_call(
        functools.partial(first_kernel, dims),
        name="forward_and_back",
        out_shape=(
            shape((rows, 6 * C), BF16),
            shape((B, 2, half + EDGE, C), BF16),
            shape((2, rows, C), BF16),
            shape((2, 2, B, EDGE, C), BF16),
            shape((8, C), F32),
            shape((8, C), F32),
            shape((2 * B, half, C // 2), BF16),
            shape((3 * C, H), BF16),
            shape((H, C), BF16),
        ),
        in_specs=[
            anywhere,
            anywhere,
            smem,
            smem,
            vmem,
            vmem,
            anywhere,
            vmem,
            vmem,
            anywhere,
            vmem,
            vmem,
            anywhere,
        ],
        out_specs=[anywhere] * 9,
        scratch_shapes=[
            pltpu.VMEM((B, L + 2 * EDGE, C), BF16),
            pltpu.VMEM((B, 2, half + EDGE, C), BF16),
            pltpu.VMEM((half + 2 * EDGE, C), F32),
            pltpu.VMEM((rows, 6 * C), BF16),
            pltpu.VMEM((5 * C, C), BF16),
            pltpu.VMEM((3 * C, H), BF16),
            pltpu.VMEM((H, C), BF16),
            pltpu.VMEM((rows, C // 3), F32),
            pltpu.VMEM((rows, C // 3), F32),
            pltpu.VMEM((rows, C), F32),
            pltpu.VMEM((B, half + 2 * EDGE, C), BF16),
            pltpu.VMEM((3, 2, 2 * B, EDGE, C), BF16),
            pltpu.VMEM((3, 2, 2 * B, EDGE, C), BF16),
            pltpu.VMEM((rows, 3 * C), BF16),
            pltpu.VMEM((rows, H), F32),
            pltpu.VMEM((B, half, C), BF16),
            pltpu.VMEM((B, half, C), BF16),
            pltpu.VMEM((rows, H), F32),
            pltpu.VMEM((rows, H), BF16),
            pltpu.VMEM((B, half + 2 * EDGE, H), BF16),
            pltpu.VMEM((rows, 3 * H), BF16),
            pltpu.VMEM((rows, C), F32),
            pltpu.VMEM((3 * C, H), BF16),
            pltpu.VMEM((H, C), BF16),
            pltpu.VMEM((2, rows, C), BF16),
            pltpu.VMEM((2, 2, B, EDGE, C), BF16),
            pltpu.VMEM((2, B, half, C // 2), BF16),
            pltpu.VMEM((2 * B, half, C // 2), BF16),
            pltpu.VMEM((2 * B, half, C // 2), BF16),
            pltpu.VMEM((8, C), F32),
            pltpu.VMEM((8, C), F32),
            pltpu.VMEM((5, nd, 8, C), F32),
            pltpu.VMEM((5, nq, 8, C), F32),
            dma((14,)),
            dma((5, peers)),
            dma((5, peers)),
            dma((4, 2)),
            dma((4, 2)),
            dma((1,)),
            dma((1,)),
            dma((3,)),
            dma((3,)),
        ],
        compiler_params=pltpu.CompilerParams(
            collective_id=0, has_side_effects=True, vmem_limit_bytes=58 * 2**20
        ),
    )(
        inputs,
        out_grad,
        shifts,
        flips,
        gain1,
        bias1,
        weight1.reshape(5 * C, C),
        gain2,
        bias2,
        weight2.reshape(3 * C, H),
        gain3,
        bias3,
        weight3,
    )
    axes = ("section", "dp", "seq")
    conv2, conv3 = lax.psum((conv2, conv3), axes)
    conv1 = pl.pallas_call(
        weight_kernel,
        name="first_weight_gradient",
        grid=(5,),
        out_shape=shape((5 * C, C), BF16),
        in_specs=[
            pl.BlockSpec((rows, C), lambda k: (0, k)),
            pl.BlockSpec((rows, C), lambda k: (0, k + 1)),
            pl.BlockSpec((1, rows, C), lambda k: (0, 0, 0)),
            pl.BlockSpec((1, rows, C), lambda k: (1, 0, 0)),
        ],
        out_specs=pl.BlockSpec((C, C), lambda k: (k, 0)),
        compiler_params=pltpu.CompilerParams(vmem_limit_bytes=32 * 2**20),
        cost_estimate=pl.CostEstimate(
            flops=20 * rows * C * C, bytes_accessed=30 * C * C, transcendentals=0
        ),
    )(taps, taps, grads, grads)
    conv1 = lax.psum(conv1, axes)
    back, sums = pl.pallas_call(
        functools.partial(last_kernel, dims),
        name="first_input_gradient",
        out_shape=(shape((2 * B, L, C // 2), BF16), shape((8, C), F32)),
        in_specs=[
            anywhere,
            anywhere,
            anywhere,
            vmem,
            vmem,
            smem,
            smem,
            vmem,
            vmem,
            anywhere,
        ],
        out_specs=[anywhere, vmem],
        scratch_shapes=[
            pltpu.VMEM((B, 2, half + EDGE, C), BF16),
            pltpu.VMEM((2, rows, C), BF16),
            pltpu.VMEM((2, 2, B, EDGE, C), BF16),
            pltpu.VMEM((5, C, C), BF16),
            pltpu.VMEM((rows, 6 * C), BF16),
            pltpu.VMEM((2, rows, C), F32),
            pltpu.VMEM((2, 2, B, EDGE, C), BF16),
            pltpu.VMEM((2, 2, B, EDGE, C), BF16),
            pltpu.VMEM((B, 2 * (half + 2 * EDGE), C), BF16),
            pltpu.VMEM((2, B, L, C // 2), BF16),
            pltpu.VMEM((2 * B, L, C // 2), BF16),
            pltpu.VMEM((2, 8, C), F32),
            pltpu.VMEM((1, nd, 8, C), F32),
            pltpu.VMEM((1, nq, 8, C), F32),
            dma((6,)),
            dma((1, peers)),
            dma((1, peers)),
            dma((2,)),
            dma((2,)),
            dma((2,)),
            dma((2,)),
        ],
        compiler_params=pltpu.CompilerParams(
            collective_id=1, has_side_effects=True, vmem_limit_bytes=48 * 2**20
        ),
        cost_estimate=pl.CostEstimate(
            flops=20 * rows * C * C, bytes_accessed=30 * C * C, transcendentals=0
        ),
    )(placed, grads, halo, stats, sums, shifts, flips, gain1, bias1, weight1)
    return (
        result,
        back,
        conv1.reshape(5, C, C).astype(F32),
        sums[0],
        sums[1],
        conv2.reshape(3, C, H).astype(F32),
        sums[2],
        sums[3],
        conv3.astype(F32),
        sums[4, :H],
        sums[5, :H],
    )


def solution(mesh):
    whole = P()
    split = P("dp", "seq", None)
    return jax.shard_map(
        functools.partial(on_device, mesh.shape["dp"], mesh.shape["seq"]),
        mesh=mesh,
        in_specs=(split, P("dp"), P("dp")) + (whole,) * 9 + (split,),
        out_specs=(P("dp", "seq", "section"),) * 2 + (whole,) * 9,
        check_vma=False,
    )
```

```python
import functools

import jax
import jax.numpy as jnp
from jax import lax
from jax.experimental import pallas as pl
from jax.experimental.pallas import tpu as pltpu
from jax.sharding import PartitionSpec as P

DILATION_SIZE = 11
EPSILON = 0.001
EDGE = 16
MESH = pl.DeviceIdType.MESH
F32 = jnp.float32
BF16 = jnp.bfloat16
SCALE = 0.7978845608028654
CUBIC = 0.044715
TN = (((0,), (0,)), ((), ()))
NT = (((1,), (1,)), ((), ()))


def gelu(u):
    return 0.5 * u * (1.0 + jnp.tanh(SCALE * u * (1.0 + CUBIC * (u * u))))


def gelu_slope(u):
    square = u * u
    t = jnp.tanh(SCALE * u * (1.0 + CUBIC * square))
    return 0.5 * (1.0 + t) + (0.5 * SCALE) * u * (1.0 - t * t) * (1.0 + (3.0 * CUBIC) * square)


def chunks(count, body, carry=0, unroll=1):
    def step(i, carry):
        return body(pl.multiple_of(i * EDGE, EDGE), carry)

    return lax.fori_loop(0, count // EDGE, step, carry, unroll=unroll)


def eight(row):
    return jnp.broadcast_to(row, (8, row.shape[-1]))


def halves(block):
    return block.reshape(block.shape[0] // 8, 8, block.shape[1])


def flat(block):
    return block.reshape(block.shape[0] * 8, block.shape[2])


def row_sum(block):
    return jnp.sum(block, axis=0, keepdims=True)


class Place:
    def __init__(self, nd, nq):
        self.nd, self.nq = nd, nq
        self.s, self.d, self.q = (lax.axis_index(a) for a in ("section", "dp", "seq"))
        self.mirror = nq - 1 - self.q
        self.next = lax.rem(self.q + 1, nq)
        self.prev = lax.rem(self.q + nq - 1, nq)
        self.partner = (1 - self.s, self.d, self.q)

    def plane(self):
        return [(self.s, lax.rem(self.d + i, self.nd), self.q) for i in range(1, self.nd)]

    def line(self):
        return [(self.s, self.d, lax.rem(self.q + i, self.nq)) for i in range(1, self.nq)]

    def greet(self, devices):
        barrier = pltpu.get_barrier_semaphore()
        for device in devices:
            pl.semaphore_signal(barrier, inc=1, device_id=device, device_id_type=MESH)
        pl.semaphore_wait(barrier, len(devices))


def remote(src, dst, send_sem, recv_sem, device):
    return pltpu.make_async_remote_copy(
        src_ref=src,
        dst_ref=dst,
        send_sem=send_sem,
        recv_sem=recv_sem,
        device_id=device,
        device_id_type=MESH,
    )


class Exchange:
    def __init__(self, place, number, plane_buf, line_buf, send_sem, recv_sem):
        self.place, self.number = place, number
        self.plane_buf, self.line_buf = plane_buf.at[number], line_buf.at[number]
        self.send_sem, self.recv_sem = send_sem.at[number], recv_sem.at[number]

    def _start(self, buf, slot, rows, devices, base):
        for at, row in enumerate(rows):
            buf[slot, at : at + 1, 0 : row.shape[1]] = row
        self.copies = [
            remote(
                buf.at[slot],
                buf.at[slot],
                self.send_sem.at[base + i],
                self.recv_sem.at[base + i],
                device,
            )
            for i, device in enumerate(devices)
        ]
        for copy in self.copies:
            copy.start()

    def _finish(self, buf, count, n_rows, width):
        for copy in self.copies:
            copy.wait()
        return [[buf[j, at : at + 1, 0:width] for at in range(n_rows)] for j in range(count)]

    def start(self, rows):
        self.n_rows, self.width = len(rows), rows[0].shape[1]
        self._start(self.plane_buf, self.place.d, rows, self.place.plane(), 0)

    def relay(self, join):
        parts = self._finish(self.plane_buf, self.place.nd, self.n_rows, self.width)
        self._start(
            self.line_buf, self.place.q, join(parts), self.place.line(), self.place.nd - 1
        )

    def finish(self, join):
        return join(self._finish(self.line_buf, self.place.nq, self.n_rows, self.width))


def join_sums(parts):
    totals = parts[0]
    for part in parts[1:]:
        totals = [total + row for total, row in zip(totals, part)]
    return totals


def join_moments(count):
    def join(parts):
        n = len(parts[0]) // 2
        totals = join_sums(parts)
        means = [total * (1.0 / len(parts)) for total in totals[:n]]
        squares = totals[n:]
        for part in parts:
            squares = [
                square + count * (row - mean) * (row - mean)
                for square, row, mean in zip(squares, part[:n], means)
            ]
        return means + squares

    return join


class Norm:
    def __init__(self, mean, inv, gain, bias):
        self.mean, self.inv, self.gain, self.bias = eight(mean), eight(inv), eight(gain), eight(bias)

    def normed(self, block):
        return (block - self.mean[None]) * self.inv[None]

    def pre(self, normed):
        return normed * self.gain[None] + self.bias[None]


def first_kernel(
    dims,
    inputs,
    out_grad,
    shifts,
    flips,
    gain1,
    bias1,
    weight1,
    gain2,
    bias2,
    weight2,
    gain3,
    bias3,
    weight3,
    taps_out,
    placed_out,
    grad_out,
    halo_out,
    stats_out,
    sums_out,
    result_out,
    own_out,
    other_out,
    window,
    placed,
    act,
    taps,
    w1,
    w2,
    w3,
    even,
    odd,
    share,
    pooled,
    edges,
    edges_in,
    second,
    narrow,
    own_grad,
    far_grad,
    third_in,
    third,
    narrow_grad,
    narrow_taps,
    second_grad,
    block_grad,
    block_send,
    wide_grad,
    halo,
    ours,
    stats,
    sums,
    plane_buf,
    line_buf,
    local_sem,
    exchange_send,
    exchange_recv,
    halo_send,
    halo_recv,
    far_send,
    far_recv,
):
    C, H, L, B, nd, nq = dims
    half = L // 2
    place = Place(nd, nq)
    s, q = place.s, place.q
    place.greet(place.plane() + place.line())

    flip = [flips[s * B + b] for b in range(B)]
    shift = [shifts[s * B + b] for b in range(B)]
    block_at = [flip[b] * (nq - 1 - q) + (1 - flip[b]) * q for b in range(B)]
    mine = pl.ds(s * B, B)

    def exchange(number):
        return Exchange(place, number, plane_buf, line_buf, exchange_send, exchange_recv)

    def pair(number, to_next, to_prev, from_prev, from_next):
        return [
            remote(
                to_next,
                from_prev,
                halo_send.at[number, 0],
                halo_recv.at[number, 0],
                (s, place.d, place.next),
            ),
            remote(
                to_prev,
                from_next,
                halo_send.at[number, 1],
                halo_recv.at[number, 1],
                (s, place.d, place.prev),
            ),
        ]

    load = [
        pltpu.make_async_copy(inputs.at[mine], window.at[:, EDGE : EDGE + L], local_sem.at[0]),
        pltpu.make_async_copy(weight1, w1, local_sem.at[1]),
        pltpu.make_async_copy(weight2, w2, local_sem.at[2]),
        pltpu.make_async_copy(weight3, w3, local_sem.at[3]),
        pltpu.make_async_copy(out_grad.at[mine], own_grad, local_sem.at[4]),
    ]
    for copy in load:
        copy.start()
    ring = pair(
        0,
        inputs.at[mine, L - EDGE : L],
        inputs.at[mine, 0:EDGE],
        window.at[:, 0:EDGE],
        window.at[:, EDGE + L : 2 * EDGE + L],
    )
    for copy in ring:
        copy.start()

    load[0].wait()
    zero = jnp.zeros((8, C), F32)

    def moments(read, count, width):
        none = jnp.zeros((8, width), F32)
        means, squares = [], []
        for b in range(B):
            total = chunks(count, lambda r, t: t + jnp.sum(halves(read(b, r)), axis=0), none, 2)
            mean = row_sum(total) * (1.0 / count)
            mean8 = eight(mean)

            def deviations(r, t):
                away = halves(read(b, r)) - mean8[None]
                return t + jnp.sum(away * away, axis=0)

            means.append(mean)
            squares.append(row_sum(chunks(count, deviations, none, 2)))
        return means + squares

    def norms(exchange, count, gain, bias):
        exchange.relay(join_moments(float(count)))
        joined = exchange.finish(join_moments(float(count * nd)))
        scale = 1.0 / (count * nd * nq)
        inverse = [lax.rsqrt(square * scale + EPSILON) for square in joined[B:]]
        return [Norm(joined[b], inverse[b], gain[...], bias[...]) for b in range(B)]

    step = exchange(0)
    step.start(
        moments(lambda b, r: window[b, pl.ds(EDGE + r, EDGE)].astype(F32), L, C)
    )

    for copy in ring:
        copy.wait()
    tall = half + EDGE
    for b in range(B):
        for parity in range(2):
            shape = (tall, L + 2 * EDGE)
            at = 2 * (lax.broadcasted_iota(jnp.int32, shape, 0) - 8) + parity
            source = flip[b] * (L - 1) + (1 - 2 * flip[b]) * at - shift[b] + EDGE
            pick = jnp.where(lax.broadcasted_iota(jnp.int32, shape, 1) == source, 1.0, 0.0)
            placed[b, parity] = jnp.dot(
                pick.astype(BF16), window[b], preferred_element_type=F32
            ).astype(BF16)
    first_norm = norms(step, L, gain1, bias1)
    mirrored = remote(
        out_grad.at[mine],
        far_grad,
        far_send.at[0],
        far_recv.at[0],
        (s, place.d, place.mirror),
    )
    mirrored.start()
    save = [pltpu.make_async_copy(placed, placed_out, local_sem.at[5])]
    save[0].start()

    for b in range(B):
        stats[b : b + 1, :] = first_norm[b].mean[0:1]
        stats[B + b : B + b + 1, :] = first_norm[b].inv[0:1]
        for parity in range(2):

            def activate(r, c):
                norm = first_norm[b]
                value = gelu(norm.pre(norm.normed(halves(placed[b, parity, pl.ds(r, EDGE)].astype(F32)))))
                value = flat(value)
                at = lax.broadcasted_iota(jnp.int32, value.shape, 0) + (r - 8)
                at = 2 * at + (parity + block_at[b] * L)
                act[pl.ds(r, EDGE)] = jnp.where((at >= 0) & (at < nq * L), value, 0.0)
                return c

            chunks(tall, activate)

            def spread(r, c):
                values = act[pl.ds(r, 2 * EDGE)]
                for off in range(3):
                    at = (2 * off + parity) * C
                    taps[pl.ds(b * half + r, EDGE), at : at + C] = values[
                        7 + off : 7 + off + EDGE
                    ].astype(BF16)
                return c

            chunks(half, spread)
    save.append(pltpu.make_async_copy(taps, taps_out, local_sem.at[6]))
    save[1].start()

    load[1].wait()
    wide = even.shape[1]
    for j in range(C // wide):
        cols = slice(j * wide, (j + 1) * wide)
        even[...] = jnp.dot(taps[:, 0 : 5 * C], w1[:, cols], preferred_element_type=F32)
        odd[...] = jnp.dot(taps[:, C : 6 * C], w1[:, cols], preferred_element_type=F32)
        for b in range(B):

            def pool(r, c):
                at = pl.ds(b * half + r, EDGE)
                left, right = even[at, :], odd[at, :]
                away = left - right
                small = jnp.exp(-jnp.abs(away))
                pooled[b, pl.ds(EDGE + r, EDGE), cols] = (
                    jnp.maximum(left, right) + jnp.log(1.0 + small)
                ).astype(BF16)
                part = 1.0 / (1.0 + small)
                share[at, cols] = jnp.where(away >= 0, part, small * part)
                return c

            chunks(half, pool)

    def send_edges(number, first, last, width):
        for b in range(B):
            for at, (head, tail) in enumerate(zip(first(b), last(b))):
                head, tail = head.astype(F32), tail.astype(F32)
                turned = flip[b] == 1
                place_at = at * B + b
                edges[number, 0, place_at, :, 0:width] = jnp.where(turned, head, tail).astype(BF16)
                edges[number, 1, place_at, :, 0:width] = jnp.where(turned, tail, head).astype(BF16)
        copies = pair(
            number + 1,
            edges.at[number, 0],
            edges.at[number, 1],
            edges_in.at[number, 0],
            edges_in.at[number, 1],
        )
        for copy in copies:
            copy.start()
        return copies

    def take_edges(number, at, b, width):
        from_prev = edges_in[number, 0, at * B + b, :, 0:width].astype(F32)
        from_next = edges_in[number, 1, at * B + b, :, 0:width].astype(F32)
        turned = flip[b] == 1
        before = jnp.where(turned, from_next, from_prev)
        after = jnp.where(turned, from_prev, from_next)
        before = jnp.where(block_at[b] > 0, before, 0.0)
        after = jnp.where(block_at[b] < nq - 1, after, 0.0)
        return before, after

    step = exchange(1)
    step.start(moments(lambda b, r: pooled[b, pl.ds(EDGE + r, EDGE)].astype(F32), half, C))
    ring = send_edges(
        0,
        lambda b: [pooled[b, EDGE : 2 * EDGE]],
        lambda b: [pooled[b, half : half + EDGE]],
        C,
    )
    second_norm = norms(step, half, gain2, bias2)
    for copy in ring:
        copy.wait()
    for b in range(B):
        before, after = take_edges(0, 0, b, C)
        pooled[b, 0:EDGE] = before.astype(BF16)
        pooled[b, EDGE + half : 2 * EDGE + half] = after.astype(BF16)
        norm = second_norm[b]

        def activate(r, c):
            value = flat(gelu(norm.pre(norm.normed(halves(pooled[b, pl.ds(r, EDGE)].astype(F32))))))
            at = lax.broadcasted_iota(jnp.int32, value.shape, 0) + (r - EDGE + block_at[b] * half)
            act[pl.ds(r, EDGE)] = jnp.where((at >= 0) & (at < nq * half), value, 0.0)
            return c

        chunks(half + 2 * EDGE, activate)

        def spread(r, c):
            values = act[pl.ds(r, 3 * EDGE)]
            for k in range(3):
                at = EDGE + (k - 1) * DILATION_SIZE
                second[pl.ds(b * half + r, EDGE), k * C : (k + 1) * C] = values[
                    at : at + EDGE
                ].astype(BF16)
            return c

        chunks(half, spread)

    load[2].wait()
    narrow[...] = jnp.dot(second[...], w2[...], preferred_element_type=F32)
    step = exchange(2)
    step.start(moments(lambda b, r: narrow[pl.ds(b * half + r, EDGE)], half, H))
    load[3].wait()
    load[4].wait()
    mirrored.wait()
    for b in range(B):

        def choose(r, c):
            at = pl.ds(r, EDGE)
            own_grad[b, at] = jnp.where(
                flip[b] == 1, far_grad[b, at].astype(F32), own_grad[b, at].astype(F32)
            ).astype(BF16)
            return c

        chunks(half, choose)
        third_in[b * half : (b + 1) * half] = lax.dot_general(
            own_grad[b], w3[...], NT, preferred_element_type=F32
        )
    third_norm = norms(step, half, gain3, bias3)

    none = jnp.zeros((8, H), F32)
    totals = []
    for b in range(B):
        norm = third_norm[b]

        def activate(r, carry):
            at = pl.ds(b * half + r, EDGE)
            normed = norm.normed(halves(narrow[at]))
            pre = norm.pre(normed)
            third[at] = flat(gelu(pre)).astype(BF16)
            grad = halves(third_in[at]) * gelu_slope(pre)
            third_in[at] = flat(grad)
            return carry[0] + jnp.sum(grad, axis=0), carry[1] + jnp.sum(grad * normed, axis=0)

        totals.append(chunks(half, activate, (none, none)))
    step = exchange(3)
    step.start([row_sum(t[0]) for t in totals] + [row_sum(t[1]) for t in totals])

    for b in range(B):
        at = slice(b * half, (b + 1) * half)
        for side in range(2):
            cols = slice(side * (C // 2), (side + 1) * (C // 2))
            ours[side, b] = (
                pooled[b, EDGE : EDGE + half, cols].astype(F32)
                + jnp.dot(third[at], w3[:, cols], preferred_element_type=F32)
            ).astype(BF16)
    save.append(pltpu.make_async_copy(ours, result_out, local_sem.at[7]))
    save[2].start()
    step.relay(join_sums)
    width = C // 2

    def keep(first, value):
        block_grad[first : first + value.shape[0]] = value
        block_send[first : first + value.shape[0]] = value.astype(BF16)

    value = sum(
        lax.dot_general(
            third[b * half : (b + 1) * half], own_grad[b], TN, preferred_element_type=F32
        )
        for b in range(B)
    )
    keep(3 * C, value[:, 0:width])
    keep(3 * C + H, value[:, width:])
    back = step.finish(join_sums)
    sums[4:5, 0:H] = sum(back[B:])
    sums[5:6, 0:H] = sum(back[:B])
    scale = 1.0 / (half * nd * nq)
    for b in range(B):
        norm = third_norm[b]
        mean_bias, mean_gain = eight(back[b] * scale), eight(back[B + b] * scale)
        factor = norm.gain * norm.inv

        def input_grad(r, c):
            at = pl.ds(b * half + r, EDGE)
            normed = norm.normed(halves(narrow[at]))
            value = factor[None] * (halves(third_in[at]) - mean_bias[None] - normed * mean_gain[None])
            narrow_grad[b, pl.ds(EDGE + r, EDGE)] = flat(value).astype(BF16)
            return c

        chunks(half, input_grad)
    ring = send_edges(
        1,
        lambda b: [narrow_grad[b, EDGE : 2 * EDGE]],
        lambda b: [narrow_grad[b, half : half + EDGE]],
        H,
    )
    for k in range(3):
        keep(
            k * C,
            sum(
                lax.dot_general(
                    second[b * half : (b + 1) * half, k * C : (k + 1) * C],
                    narrow_grad[b, EDGE : EDGE + half],
                    TN,
                    preferred_element_type=F32,
                )
                for b in range(B)
            ),
        )
    side = block_grad.shape[0] // 2
    save += [
        pltpu.make_async_copy(block_grad.at[pl.ds(s * side, side)], own_out, local_sem.at[8]),
        pltpu.make_async_copy(
            block_send.at[pl.ds((1 - s) * side, side)], other_out, local_sem.at[10]
        ),
    ]
    save[3].start()
    save[4].start()
    for copy in ring:
        copy.wait()
    for b in range(B):
        before, after = take_edges(1, 0, b, H)
        narrow_grad[b, 0:EDGE] = before.astype(BF16)
        narrow_grad[b, EDGE + half : 2 * EDGE + half] = after.astype(BF16)

        def spread(r, c):
            values = narrow_grad[b, pl.ds(r, 3 * EDGE)].astype(F32)
            for k in range(3):
                at = EDGE - (k - 1) * DILATION_SIZE
                narrow_taps[pl.ds(b * half + r, EDGE), k * H : (k + 1) * H] = values[
                    at : at + EDGE
                ].astype(BF16)
            return c

        chunks(half, spread)
    second_grad[...] = sum(
        lax.dot_general(
            narrow_taps[:, k * H : (k + 1) * H],
            w2[k * C : (k + 1) * C],
            NT,
            preferred_element_type=F32,
        )
        for k in range(3)
    )
    totals = []
    for b in range(B):
        norm = second_norm[b]

        def slope(r, carry):
            at = pl.ds(b * half + r, EDGE)
            normed = norm.normed(halves(pooled[b, pl.ds(EDGE + r, EDGE)].astype(F32)))
            grad = halves(second_grad[at]) * gelu_slope(norm.pre(normed))
            second_grad[at] = flat(grad)
            return carry[0] + jnp.sum(grad, axis=0), carry[1] + jnp.sum(grad * normed, axis=0)

        totals.append(chunks(half, slope, (zero, zero)))
    step = exchange(4)
    step.start([row_sum(t[0]) for t in totals] + [row_sum(t[1]) for t in totals])
    step.relay(join_sums)
    back = step.finish(join_sums)
    sums[2:3, :] = sum(back[B:])
    sums[3:4, :] = sum(back[:B])
    for b in range(B):
        norm = second_norm[b]
        mean_bias, mean_gain = eight(back[b] * scale), eight(back[B + b] * scale)
        factor = norm.gain * norm.inv

        def unpool(r, c):
            at = pl.ds(b * half + r, EDGE)
            normed = norm.normed(halves(pooled[b, pl.ds(EDGE + r, EDGE)].astype(F32)))
            value = factor[None] * (
                halves(second_grad[at]) - mean_bias[None] - normed * mean_gain[None]
            )
            value = flat(value) + own_grad[b, pl.ds(r, EDGE)].astype(F32)
            value = value.astype(BF16).astype(F32)
            part = share[at]
            wide_grad[0, at] = (value * part).astype(BF16)
            wide_grad[1, at] = (value * (1.0 - part)).astype(BF16)
            return c

        chunks(half, unpool)
    ring = send_edges(
        2,
        lambda b: [wide_grad[p, b * half : b * half + EDGE] for p in range(2)],
        lambda b: [wide_grad[p, (b + 1) * half - EDGE : (b + 1) * half] for p in range(2)],
        C,
    )
    save.append(pltpu.make_async_copy(wide_grad, grad_out, local_sem.at[9]))
    save[5].start()
    for copy in ring:
        copy.wait()
    for b in range(B):
        for parity in range(2):
            before, after = take_edges(2, parity, b, C)
            halo[0, parity, b] = before.astype(BF16)
            halo[1, parity, b] = after.astype(BF16)
    save += [
        pltpu.make_async_copy(halo, halo_out, local_sem.at[11]),
        pltpu.make_async_copy(stats, stats_out, local_sem.at[12]),
        pltpu.make_async_copy(sums, sums_out, local_sem.at[13]),
    ]
    for copy in save[6:]:
        copy.start()
    for copy in save:
        copy.wait()


class Cube:
    def __init__(self, place, blocks, width, refs):
        self.place, self.blocks, self.width = place, blocks, width
        self.total, self.inbox, self.relayed, self.summed, self.out = refs[:5]
        (
            self.core_send,
            self.core_recv,
            self.down_send,
            self.down_recv,
            self.up_send,
            self.up_recv,
            self.share_send,
            self.share_recv,
            self.out_sem,
        ) = refs[5:]
        self.sources = [None] * blocks
        self.axes = cube_axes(place)
        self.flight = [None] * blocks
        self.state = [None] * blocks

    def order(self, block):
        return [self.axes[i] for i in cube_order(block, len(self.axes))]

    def events(self):
        depth = len(self.axes)
        return ["core"] + ["down"] * depth + ["up"] * halvings(depth) + ["share", "out"]

    def _add(self, block, incoming, first, count, send):
        total, inbox, width = self.total, self.inbox, self.width

        def add(r, c):
            at = pl.ds(pl.multiple_of(first + r, EDGE), EDGE)
            value = total[block, at] + incoming(r).astype(F32)
            total[block, at] = value
            if send:
                inbox[block, at] = value.astype(BF16)
            return c

        chunks(count, add)

    def run(self, block, stage):
        place, depth = self.place, len(self.axes)
        s = place.s
        last = depth + halvings(depth)
        if self.flight[block] is not None:
            self.flight[block].wait()
        if stage == 0:
            copy = remote(
                self.sources[block],
                self.inbox.at[block],
                self.core_send.at[block],
                self.core_recv.at[block],
                place.partner,
            )
        elif stage <= depth:
            k = stage - 1
            partner, side = self.order(block)[k]
            size, first, past = sizes(k), [0], None
            if k > 0:
                first, past = self.state[block]
            offset = first[-1]
            if k == 0:
                incoming = lambda base: lambda r: self.inbox[
                    block, pl.ds(pl.multiple_of(base + r, EDGE), EDGE)
                ]
                base_of = lambda at: at
            else:
                incoming = lambda base: lambda r: self.relayed[
                    block, pl.ds(pl.multiple_of(base + r, EDGE), EDGE)
                ]
                base_of = lambda at: at - offset + region(k - 1)
            if size >= 2 * EDGE:
                small = size // 2
                give, hold = offset + (1 - side) * small, offset + side * small
                self._add(block, incoming(base_of(give)), give, small, True)
            else:
                small, give, hold = size, offset, offset
                self._add(block, incoming(base_of(give)), give, small, True)
                at = pl.ds(pl.multiple_of(give, EDGE), small)
                self.total[block, at] = self.inbox[block, at].astype(F32)
            copy = remote(
                self.inbox.at[block, pl.ds(pl.multiple_of(give, EDGE), small)],
                self.relayed.at[block, region(k) : region(k) + small],
                self.down_send.at[block, k],
                self.down_recv.at[block, k],
                partner,
            )
            self.state[block] = (first + [hold], past)
        elif stage <= last:
            k = last - stage
            first, _ = self.state[block]
            partner, _ = self.order(block)[k]
            hold, small = first[k + 1], sizes(k + 1)
            at = pl.ds(pl.multiple_of(hold, EDGE), small)
            if stage == depth + 1:
                end = pl.ds(pl.multiple_of(first[-1], EDGE), sizes(depth))
                begin = region(depth - 1)
                self.summed[s, block, end] = (
                    self.total[block, end]
                    + self.relayed[block, begin : begin + sizes(depth)].astype(F32)
                ).astype(BF16)
            copy = remote(
                self.summed.at[s, block, at],
                self.summed.at[s, block, at],
                self.up_send.at[block, k],
                self.up_recv.at[block, k],
                partner,
            )
        elif stage == last + 1:
            copy = remote(
                self.summed.at[s, block],
                self.summed.at[s, block],
                self.share_send.at[block],
                self.share_recv.at[block],
                place.partner,
            )
        else:
            copy = pltpu.make_async_copy(
                self.summed.at[:, block], self.out.at[:, block], self.out_sem.at[block]
            )
        if stage > 0 and stage <= depth:
            copy.start()
            if size >= 2 * EDGE:
                self._add(block, incoming(base_of(hold)), hold, small, False)
        else:
            copy.start()
        self.flight[block] = copy

    def end(self):
        for copy in self.flight:
            copy.wait()


BLOCK = 256


def sizes(k):
    return max(BLOCK >> k, EDGE)


def region(k):
    return sum(sizes(i + 1) for i in range(k))


def halvings(depth):
    return sum(sizes(k) >= 2 * EDGE for k in range(depth))


def cube_axes(place):
    axes = []
    bit = 1
    while bit < place.nd:
        side = lax.rem(place.d // bit, 2)
        axes.append(((place.s, place.d + bit * (1 - 2 * side), place.q), side))
        bit *= 2
    span = 2
    while span <= place.nq:
        low = lax.rem(place.q, span)
        side = lax.rem(place.q // (span // 2) + place.q // span, 2)
        axes.append(((place.s, place.d, place.q - low + span - 1 - low), side))
        span *= 2
    return axes


def cube_order(block, depth):
    others = [(block + i) % (depth - 1) for i in range(depth - 1)]
    at = 1 if (block // (depth - 1)) % 2 else depth - 1
    return others[:at] + [depth - 1] + others[at:]


def plan(depth, blocks, pieces, events):
    rate, wait, cost = 95e3, 1.6, 0.2
    free = [0.0] * (depth + 1)
    ready = {}
    due = [(0, 0.0)] * 0
    now, order = 0.0, []
    pieces = list(pieces)
    while pieces or ready:
        able = sorted((t, b) for b, (t, _) in ready.items() if t <= now)
        if able:
            _, block = able[0]
            _, stage = ready.pop(block)
            order.append((block, stage))
            kind = events[stage]
            now += cost if kind == "down" else 0.05
            if stage + 1 < len(events):
                if kind in ("core", "share"):
                    axis, size, speed = depth, 256, 4 * rate
                elif kind == "down":
                    k = stage - 1
                    axis, size, speed = cube_order(block, depth)[k], sizes(k + 1), rate
                elif kind == "up":
                    k = depth + halvings(depth) - stage
                    axis, size, speed = cube_order(block, depth)[k], sizes(k + 1), rate
                begin = max(now, free[axis])
                free[axis] = begin + 2 * size * 768 / speed
                ready[block] = (free[axis] + wait, stage + 1)
        elif pieces:
            name, time, made, sends = pieces.pop(0)
            order.append(name)
            now += time
            for block in made:
                ready[block] = (now, 0)
            for axis, size in sends:
                free[axis] = max(now, free[axis]) + size / rate
        else:
            now = min(t for t, _ in ready.values())
    return order


def tail_kernel(
    dims,
    taps_in,
    placed_in,
    grad_in,
    halo_in,
    own_in,
    other_in,
    result_in,
    stats,
    sums_in,
    shifts,
    flips,
    gain1,
    bias1,
    weight1,
    summed_out,
    near_out,
    far_out,
    back_out,
    sums_out,
    total,
    inbox,
    sending,
    relayed,
    summed,
    product,
    placed,
    grads,
    halo,
    w1,
    taps,
    act_grad,
    edges,
    edges_in,
    window,
    ours,
    final,
    sums,
    plane_buf,
    line_buf,
    local_sem,
    exchange_send,
    exchange_recv,
    halo_send,
    halo_recv,
    core_send,
    core_recv,
    result_send,
    result_recv,
    *cube_sems,
):
    C, H, L, B, nd, nq = dims
    half = L // 2
    width = C // 2
    place = Place(nd, nq)
    s, q = place.s, place.q
    cross = (1 - s, place.d, place.mirror)
    mine = pl.ds(s * B, B)
    first_blocks = own_in.shape[0] // BLOCK
    per_tap = C // BLOCK
    blocks = first_blocks + 5 * per_tap
    cube = Cube(place, blocks, width, (total, inbox, relayed, summed, summed_out) + cube_sems)
    depth = len(cube.axes)
    greeted = place.plane() + place.line() + [place.partner, cross]
    bit = 1
    place.greet(greeted)
    flip = [flips[s * B + b] for b in range(B)]
    shift = [shifts[s * B + b] for b in range(B)]
    load = [
        pltpu.make_async_copy(
            own_in.at[i * BLOCK : (i + 1) * BLOCK], total.at[i], local_sem.at[6 + i]
        )
        for i in range(first_blocks)
    ]
    load_taps = pltpu.make_async_copy(taps_in, taps, local_sem.at[0])
    load_grads = pltpu.make_async_copy(grad_in, grads, local_sem.at[1])
    load_rest = [
        pltpu.make_async_copy(halo_in, halo, local_sem.at[2]),
        pltpu.make_async_copy(weight1, w1, local_sem.at[3]),
        pltpu.make_async_copy(placed_in, placed, local_sem.at[4]),
    ]
    for copy in [load_taps, load_grads] + load + load_rest:
        copy.start()
    for i in range(first_blocks):
        cube.sources[i] = other_in.at[i * BLOCK : (i + 1) * BLOCK]
    for i in range(5 * per_tap):
        cube.sources[first_blocks + i] = sending.at[i]
    todo, pieces = {}, []

    def piece(name, time, made=(), sends=()):
        def keep(body):
            todo[name] = body
            pieces.append((name, time, made, sends))
            return body

        return keep

    @piece("block gradients", 0.3, range(first_blocks))
    def _():
        for copy in load:
            copy.wait()

    across = remote(
        result_in.at[1 - s], near_out.at[mine], result_send.at[0], result_recv.at[0], place.partner
    )
    keep_near = pltpu.make_async_copy(result_in.at[s], near_out.at[mine], local_sem.at[5])
    away = [
        remote(
            result_in.at[side, b],
            far_out.at[s * B + b],
            result_send.at[1 + 2 * b + i],
            result_recv.at[1 + 2 * b + i],
            (side, place.d, place.mirror),
        )
        for b in range(B)
        for i, side in enumerate((s, 1 - s))
    ]
    across.start()
    keep_near.start()

    def result_piece(i):
        @piece(("result", i), 0.05, (), [(depth - 1, 2 * half * width * 2)])
        def _():
            away[i].start()

    def weight_piece(k):
        made = range(first_blocks + k * per_tap, first_blocks + (k + 1) * per_tap)

        @piece(("weight", k), 1.9, made)
        def _():
            if k == 0:
                load_taps.wait()
                load_grads.wait()

            def tile(m, c):
                lanes = pl.multiple_of(k * C + m * BLOCK, BLOCK)
                product[...] = lax.dot_general(
                    taps[:, pl.ds(lanes, BLOCK)], grads[0], TN, preferred_element_type=F32
                ) + lax.dot_general(
                    taps[:, pl.ds(lanes + C, BLOCK)], grads[1], TN, preferred_element_type=F32
                )

                def split(r, c):
                    at = pl.ds(r, EDGE)
                    low = pl.ds(pl.multiple_of(s * width, width), width)
                    high = pl.ds(pl.multiple_of((1 - s) * width, width), width)
                    total[first_blocks + k * per_tap + m, at] = product[at, low]
                    sending[k * per_tap + m, at] = product[at, high].astype(BF16)
                    return c

                chunks(BLOCK, split)
                return c

            lax.fori_loop(0, per_tap, tile, 0)

    for k in range(5):
        if k < 2 * B:
            result_piece(k)
        weight_piece(k)

    def put(b, parity, r, values):
        base = (1 - parity) * C
        for at in range(3):
            lanes = base + 2 * at * C
            taps[pl.ds(b * half + r, EDGE), lanes : lanes + C] = values[
                EDGE + 1 - at : 2 * EDGE + 1 - at
            ].astype(BF16)

    def spread_piece(b, parity):
        @piece(("spread", b, parity), 0.6)
        def _():
            if b == 0 and parity == 0:
                load_rest[0].wait()

            def spread(i, c):
                r = pl.multiple_of(i * EDGE, EDGE)
                values = grads[parity, pl.ds(b * half + r - EDGE, 3 * EDGE)].astype(F32)
                put(b, parity, r, values)
                return c

            lax.fori_loop(1, half // EDGE - 1, spread, 0)
            low, high = b * half, (b + 1) * half
            put(
                b,
                parity,
                0,
                jnp.concatenate(
                    [halo[0, parity, b], grads[parity, low : low + 2 * EDGE]], axis=0
                ).astype(F32),
            )
            put(
                b,
                parity,
                half - EDGE,
                jnp.concatenate(
                    [grads[parity, high - 2 * EDGE : high], halo[1, parity, b]], axis=0
                ).astype(F32),
            )

    for b in range(B):
        for parity in range(2):
            spread_piece(b, parity)

    def convolve_piece(parity, j):
        @piece(("convolve", parity, j), 1.4)
        def _():
            if parity == 0 and j == 0:
                load_rest[1].wait()
                load_rest[2].wait()
            part = None
            for k in range(5):
                lanes = (k + 1 - parity) * C
                more = lax.dot_general(
                    taps[:, lanes : lanes + C],
                    w1[k, j * 256 : (j + 1) * 256, :],
                    NT,
                    preferred_element_type=F32,
                )
                part = more if part is None else part + more
            act_grad[parity, :, j * 256 : (j + 1) * 256] = part

    for parity in range(2):
        for j in range(C // 256):
            convolve_piece(parity, j)
    norms = [
        Norm(stats[b : b + 1, :], stats[B + b : B + b + 1, :], gain1[...], bias1[...])
        for b in range(B)
    ]
    zero = jnp.zeros((8, C), F32)
    carries = [(zero, zero) for _ in range(B)]

    def slope_piece(b, parity):
        @piece(("slope", b, parity), 1.2)
        def _():
            norm = norms[b]

            def slope(r, carry):
                at = pl.ds(b * half + r, EDGE)
                values = placed[b, parity, pl.ds(r, 2 * EDGE)].astype(F32)[8 : 8 + EDGE]
                normed = norm.normed(halves(values))
                grad = halves(act_grad[parity, at]) * gelu_slope(norm.pre(normed))
                act_grad[parity, at] = flat(grad)
                return carry[0] + jnp.sum(grad, axis=0), carry[1] + jnp.sum(grad * normed, axis=0)

            carries[b] = chunks(half, slope, carries[b])

    for b in range(B):
        for parity in range(2):
            slope_piece(b, parity)
    step = Exchange(place, 0, plane_buf, line_buf, exchange_send, exchange_recv)
    back = []
    swap = remote(sums.at[0], sums.at[1], core_send.at[0], core_recv.at[0], place.partner)

    @piece("exchange", 4.0)
    def _():
        step.start([row_sum(t[0]) for t in carries] + [row_sum(t[1]) for t in carries])

    @piece("relay", 4.0)
    def _():
        step.relay(join_sums)

    @piece("finish", 0.1)
    def _():
        back.extend(step.finish(join_sums))
        sums[0] = sums_in[...]
        sums[0, 0:1, :] = sum(back[B:])
        sums[0, 1:2, :] = sum(back[:B])
        swap.start()

    scale = 1.0 / (L * nd * nq)
    tall = half + 2 * EDGE

    def gradient_piece(b, parity):
        @piece(("gradient", b, parity), 0.8)
        def _():
            norm = norms[b]
            mean_bias, mean_gain = eight(back[b] * scale), eight(back[B + b] * scale)
            factor = norm.gain * norm.inv

            def input_grad(r, c):
                values = placed[b, parity, pl.ds(r, 2 * EDGE)].astype(F32)[8 : 8 + EDGE]
                normed = norm.normed(halves(values))
                value = factor[None] * (
                    halves(act_grad[parity, pl.ds(b * half + r, EDGE)])
                    - mean_bias[None]
                    - normed * mean_gain[None]
                )
                window[b, pl.ds(parity * tall + EDGE + r, EDGE)] = flat(value).astype(BF16)
                return c

            chunks(half, input_grad)

    for b in range(B):
        for parity in range(2):
            gradient_piece(b, parity)
    ring = [
        remote(
            edges.at[i],
            edges_in.at[i],
            halo_send.at[i],
            halo_recv.at[i],
            (s, place.d, at),
        )
        for i, at in enumerate((place.next, place.prev))
    ]

    @piece("edges", 4.0)
    def _():
        for b in range(B):
            turned = flip[b] == 1
            for parity in range(2):
                low = parity * tall
                head = window[b, low + EDGE : low + 2 * EDGE].astype(F32)
                end = window[b, low + half : low + half + EDGE].astype(F32)
                edges[0, parity, b] = jnp.where(turned, head, end).astype(BF16)
                edges[1, parity, b] = jnp.where(turned, end, head).astype(BF16)
        for copy in ring:
            copy.start()

    @piece("halo", 0.1)
    def _():
        for copy in ring:
            copy.wait()

    def place_piece(b, side):
        @piece(("place", b, side), 1.0)
        def _():
            turned = flip[b] == 1
            for parity in range(2):
                low = parity * tall
                from_prev = edges_in[0, parity, b].astype(F32)
                from_next = edges_in[1, parity, b].astype(F32)
                window[b, low : low + EDGE] = jnp.where(turned, from_next, from_prev).astype(BF16)
                window[b, low + EDGE + half : low + tall] = jnp.where(
                    turned, from_prev, from_next
                ).astype(BF16)
            shape = (L, 2 * tall)
            at = lax.broadcasted_iota(jnp.int32, shape, 0) + shift[b]
            at = flip[b] * (L - 1) + (1 - 2 * flip[b]) * at
            source = (at & 1) * tall + (at >> 1) + EDGE
            pick = jnp.where(lax.broadcasted_iota(jnp.int32, shape, 1) == source, 1.0, 0.0)
            cols = slice(side * width, (side + 1) * width)
            ours[side, b] = jnp.dot(
                pick.astype(BF16), window[b, :, cols], preferred_element_type=F32
            ).astype(BF16)

    for b in range(B):
        for side in range(2):
            place_piece(b, side)
    cross_back = remote(
        ours.at[1 - s], final, core_send.at[1], core_recv.at[1], place.partner
    )
    keep_back = pltpu.make_async_copy(ours.at[s], back_out.at[mine], local_sem.at[0])
    give_back = pltpu.make_async_copy(
        final, back_out.at[pl.ds((1 - s) * B, B)], local_sem.at[1]
    )

    @piece("swap", 2.0)
    def _():
        cross_back.start()
        keep_back.start()
        swap.wait()
        sums_out[...] = sums[0] + sums[1]

    @piece("give", 0.1)
    def _():
        cross_back.wait()
        give_back.start()

    for item in plan(depth, blocks, pieces, cube.events()):
        if item in todo:
            todo[item]()
        else:
            cube.run(*item)
    cube.end()
    across.wait()
    for copy in away:
        copy.wait()
    keep_near.wait()
    keep_back.wait()
    give_back.wait()


def finish_kernel(
    dims,
    first_blocks,
    summed,
    near,
    far,
    back,
    flips,
    conv1,
    conv2,
    conv3,
    result,
    back_out,
    held,
    wide,
    near_buf,
    far_buf,
    back_buf,
    in_sem,
    out_sem,
    side_sem,
):
    C, H, L, B, nd, nq = dims
    blocks = summed.shape[1]
    width = C // 2
    tasks = [(block, side) for block in range(blocks) for side in range(2)]
    slots = wide.shape[0]
    loads = [
        pltpu.make_async_copy(summed.at[side, block], held.at[i], in_sem.at[i])
        for i, (block, side) in enumerate(tasks)
    ]
    sides = [
        pltpu.make_async_copy(near, near_buf, side_sem.at[0]),
        pltpu.make_async_copy(far, far_buf, side_sem.at[1]),
        pltpu.make_async_copy(back, back_buf, side_sem.at[2]),
    ]
    for copy in loads[:8] + sides + loads[8:]:
        copy.start()
    bottom = 3 * C

    def targets(block, side, slot):
        if block >= first_blocks:
            row = (block - first_blocks) * BLOCK
            cols = slice(side * width, (side + 1) * width)
            return [(wide.at[slot], conv1.at[row : row + BLOCK, cols])]
        row = side * first_blocks * BLOCK + block * BLOCK
        if row < bottom:
            return [(wide.at[slot], conv2.at[row : row + BLOCK])]
        parts, at = [], 0
        while at < BLOCK:
            place = row - bottom + at
            which, first = place // H, place % H
            count = min(BLOCK - at, H - first)
            cols = slice(which * width, (which + 1) * width)
            parts.append((wide.at[slot, at : at + count], conv3.at[first : first + count, cols]))
            at += count
        return parts

    going = [[] for _ in range(slots)]
    for i, (block, side) in enumerate(tasks):
        slot = i % slots
        for copy in going[slot]:
            copy.wait()
        loads[i].wait()

        def widen(r, c):
            at = pl.ds(r, EDGE)
            wide[slot, at] = held[i, at].astype(F32)
            return c

        chunks(BLOCK, widen, 0, 2)
        going[slot] = [
            pltpu.make_async_copy(src, dst, out_sem.at[slot, j])
            for j, (src, dst) in enumerate(targets(block, side, slot))
        ]
        for copy in going[slot]:
            copy.start()
    for copy in sides:
        copy.wait()
    give = pltpu.make_async_copy(back_buf, back_out, side_sem.at[2])
    give.start()
    for b in range(near.shape[0]):
        turned = flips[b]

        def deliver(r, c):
            at = pl.ds(r, EDGE)
            near_buf[b, at] = jnp.where(
                turned == 1, far_buf[b, at].astype(F32), near_buf[b, at].astype(F32)
            ).astype(BF16)
            return c

        chunks(L // 2, deliver)
    hand = pltpu.make_async_copy(near_buf, result, side_sem.at[0])
    hand.start()
    for copies in going:
        for copy in copies:
            copy.wait()
    give.wait()
    hand.wait()


def on_device(
    nd,
    nq,
    inputs,
    shifts,
    flips,
    gain1,
    bias1,
    weight1,
    gain2,
    bias2,
    weight2,
    gain3,
    bias3,
    weight3,
    out_grad,
):
    sequences, L, C = inputs.shape
    H = weight3.shape[0]
    B, half = sequences // 2, L // 2
    rows = B * half
    dims = (C, H, L, B, nd, nq)
    anywhere = pl.BlockSpec(memory_space=pl.ANY)
    vmem = pl.BlockSpec(memory_space=pltpu.VMEM)
    smem = pl.BlockSpec(memory_space=pltpu.SMEM)
    peers = nd - 1 + nq - 1
    shape = jax.ShapeDtypeStruct
    dma = pltpu.SemaphoreType.DMA
    gain1, bias1, gain2, bias2, gain3, bias3 = (
        v.reshape(1, -1) for v in (gain1, bias1, gain2, bias2, gain3, bias3)
    )
    width = C // 2
    side = (3 * C * H + H * C) // width // 2
    taps, placed, grads, halo, stats, sums, result, own, other = pl.pallas_call(
        functools.partial(first_kernel, dims),
        name="forward_and_back",
        out_shape=(
            shape((rows, 6 * C), BF16),
            shape((B, 2, half + EDGE, C), BF16),
            shape((2, rows, C), BF16),
            shape((2, 2, B, EDGE, C), BF16),
            shape((8, C), F32),
            shape((8, C), F32),
            shape((2, B, half, width), BF16),
            shape((side, width), F32),
            shape((side, width), BF16),
        ),
        in_specs=[
            anywhere,
            anywhere,
            smem,
            smem,
            vmem,
            vmem,
            anywhere,
            vmem,
            vmem,
            anywhere,
            vmem,
            vmem,
            anywhere,
        ],
        out_specs=[anywhere] * 9,
        scratch_shapes=[
            pltpu.VMEM((B, L + 2 * EDGE, C), BF16),
            pltpu.VMEM((B, 2, half + EDGE, C), BF16),
            pltpu.VMEM((half + 2 * EDGE, C), F32),
            pltpu.VMEM((rows, 6 * C), BF16),
            pltpu.VMEM((5 * C, C), BF16),
            pltpu.VMEM((3 * C, H), BF16),
            pltpu.VMEM((H, C), BF16),
            pltpu.VMEM((rows, C // 3), F32),
            pltpu.VMEM((rows, C // 3), F32),
            pltpu.VMEM((rows, C), F32),
            pltpu.VMEM((B, half + 2 * EDGE, C), BF16),
            pltpu.VMEM((3, 2, 2 * B, EDGE, C), BF16),
            pltpu.VMEM((3, 2, 2 * B, EDGE, C), BF16),
            pltpu.VMEM((rows, 3 * C), BF16),
            pltpu.VMEM((rows, H), F32),
            pltpu.VMEM((B, half, C), BF16),
            pltpu.VMEM((B, half, C), BF16),
            pltpu.VMEM((rows, H), F32),
            pltpu.VMEM((rows, H), BF16),
            pltpu.VMEM((B, half + 2 * EDGE, H), BF16),
            pltpu.VMEM((rows, 3 * H), BF16),
            pltpu.VMEM((rows, C), F32),
            pltpu.VMEM((2 * side, width), F32),
            pltpu.VMEM((2 * side, width), BF16),
            pltpu.VMEM((2, rows, C), BF16),
            pltpu.VMEM((2, 2, B, EDGE, C), BF16),
            pltpu.VMEM((2, B, half, width), BF16),
            pltpu.VMEM((8, C), F32),
            pltpu.VMEM((8, C), F32),
            pltpu.VMEM((5, nd, 8, C), F32),
            pltpu.VMEM((5, nq, 8, C), F32),
            dma((14,)),
            dma((5, peers)),
            dma((5, peers)),
            dma((4, 2)),
            dma((4, 2)),
            dma((1,)),
            dma((1,)),
        ],
        compiler_params=pltpu.CompilerParams(
            collective_id=0, has_side_effects=True, vmem_limit_bytes=58 * 2**20
        ),
    )(
        inputs,
        out_grad,
        shifts,
        flips,
        gain1,
        bias1,
        weight1.reshape(5 * C, C),
        gain2,
        bias2,
        weight2.reshape(3 * C, H),
        gain3,
        bias3,
        weight3,
    )
    first_blocks = side // BLOCK
    blocks = first_blocks + 5 * C // BLOCK
    depth = (nd.bit_length() - 1) + (nq.bit_length() - 1)
    summed, near, far, back, sums = pl.pallas_call(
        functools.partial(tail_kernel, dims),
        name="sum_and_back",
        out_shape=(
            shape((2, blocks, BLOCK, width), BF16),
            shape((2 * B, half, width), BF16),
            shape((2 * B, half, width), BF16),
            shape((2 * B, L, width), BF16),
            shape((8, C), F32),
        ),
        in_specs=[
            anywhere,
            anywhere,
            anywhere,
            anywhere,
            anywhere,
            anywhere,
            anywhere,
            vmem,
            vmem,
            smem,
            smem,
            vmem,
            vmem,
            anywhere,
        ],
        out_specs=[anywhere] * 4 + [vmem],
        scratch_shapes=[
            pltpu.VMEM((blocks, BLOCK, width), F32),
            pltpu.VMEM((blocks, BLOCK, width), BF16),
            pltpu.VMEM((blocks - first_blocks, BLOCK, width), BF16),
            pltpu.VMEM((blocks, region(depth), width), BF16),
            pltpu.VMEM((2, blocks, BLOCK, width), BF16),
            pltpu.VMEM((BLOCK, C), F32),
            pltpu.VMEM((B, 2, half + EDGE, C), BF16),
            pltpu.VMEM((2, rows, C), BF16),
            pltpu.VMEM((2, 2, B, EDGE, C), BF16),
            pltpu.VMEM((5, C, C), BF16),
            pltpu.VMEM((rows, 6 * C), BF16),
            pltpu.VMEM((2, rows, C), F32),
            pltpu.VMEM((2, 2, B, EDGE, C), BF16),
            pltpu.VMEM((2, 2, B, EDGE, C), BF16),
            pltpu.VMEM((B, 2 * (half + 2 * EDGE), C), BF16),
            pltpu.VMEM((2, B, L, width), BF16),
            pltpu.VMEM((B, L, width), BF16),
            pltpu.VMEM((2, 8, C), F32),
            pltpu.VMEM((1, nd, 8, C), F32),
            pltpu.VMEM((1, nq, 8, C), F32),
            dma((6 + first_blocks,)),
            dma((1, peers)),
            dma((1, peers)),
            dma((2,)),
            dma((2,)),
            dma((2,)),
            dma((2,)),
            dma((1 + 2 * B,)),
            dma((1 + 2 * B,)),
            dma((blocks,)),
            dma((blocks,)),
            dma((blocks, depth)),
            dma((blocks, depth)),
            dma((blocks, depth)),
            dma((blocks, depth)),
            dma((blocks,)),
            dma((blocks,)),
            dma((blocks,)),
        ],
        compiler_params=pltpu.CompilerParams(
            collective_id=1, has_side_effects=True, vmem_limit_bytes=60 * 2**20
        ),
    )(
        taps,
        placed,
        grads,
        halo,
        own,
        other,
        result,
        stats,
        sums,
        shifts,
        flips,
        gain1,
        bias1,
        weight1,
    )
    slots = 6
    conv1, conv2, conv3, result, back = pl.pallas_call(
        functools.partial(finish_kernel, dims, first_blocks),
        name="widen",
        out_shape=(
            shape((5 * C, C), F32),
            shape((3 * C, H), F32),
            shape((H, C), F32),
            shape((2 * B, half, width), BF16),
            shape((2 * B, L, width), BF16),
        ),
        in_specs=[anywhere] * 4 + [smem],
        out_specs=[anywhere] * 5,
        scratch_shapes=[
            pltpu.VMEM((2 * blocks, BLOCK, width), BF16),
            pltpu.VMEM((slots, BLOCK, width), F32),
            pltpu.VMEM((2 * B, half, width), BF16),
            pltpu.VMEM((2 * B, half, width), BF16),
            pltpu.VMEM((2 * B, L, width), BF16),
            dma((2 * blocks,)),
            dma((slots, 2)),
            dma((3,)),
        ],
        compiler_params=pltpu.CompilerParams(vmem_limit_bytes=32 * 2**20),
    )(summed, near, far, back, flips)
    return (
        result,
        back,
        conv1.reshape(5, C, C),
        sums[0],
        sums[1],
        conv2.reshape(3, C, H),
        sums[2],
        sums[3],
        conv3,
        sums[4, :H],
        sums[5, :H],
    )


def solution(mesh):
    whole = P()
    split = P("dp", "seq", None)
    return jax.shard_map(
        functools.partial(on_device, mesh.shape["dp"], mesh.shape["seq"]),
        mesh=mesh,
        in_specs=(split, P("dp"), P("dp")) + (whole,) * 9 + (split,),
        out_specs=(P("dp", "seq", "section"),) * 2 + (whole,) * 9,
        check_vma=False,
    )
```

```python
import functools

import jax
import jax.numpy as jnp
from jax import lax
from jax.experimental import pallas as pl
from jax.experimental.pallas import tpu as pltpu
from jax.sharding import PartitionSpec as P

DILATION_SIZE = 11
EPSILON = 0.001
EDGE = 16
MESH = pl.DeviceIdType.MESH
F32 = jnp.float32
BF16 = jnp.bfloat16
SCALE = 0.7978845608028654
CUBIC = 0.044715
TN = (((0,), (0,)), ((), ()))
NT = (((1,), (1,)), ((), ()))


def gelu(u):
    return 0.5 * u * (1.0 + jnp.tanh(SCALE * u * (1.0 + CUBIC * (u * u))))


def gelu_slope(u):
    square = u * u
    t = jnp.tanh(SCALE * u * (1.0 + CUBIC * square))
    return 0.5 * (1.0 + t) + (0.5 * SCALE) * u * (1.0 - t * t) * (1.0 + (3.0 * CUBIC) * square)


def chunks(count, body, carry=0, unroll=1):
    def step(i, carry):
        return body(pl.multiple_of(i * EDGE, EDGE), carry)

    return lax.fori_loop(0, count // EDGE, step, carry, unroll=unroll)


def eight(row):
    return jnp.broadcast_to(row, (8, row.shape[-1]))


def halves(block):
    return block.reshape(block.shape[0] // 8, 8, block.shape[1])


def flat(block):
    return block.reshape(block.shape[0] * 8, block.shape[2])


def row_sum(block):
    return jnp.sum(block, axis=0, keepdims=True)


class Place:
    def __init__(self, nd, nq):
        self.nd, self.nq = nd, nq
        self.s, self.d, self.q = (lax.axis_index(a) for a in ("section", "dp", "seq"))
        self.mirror = nq - 1 - self.q
        self.next = lax.rem(self.q + 1, nq)
        self.prev = lax.rem(self.q + nq - 1, nq)
        self.partner = (1 - self.s, self.d, self.q)

    def plane(self):
        return [(self.s, lax.rem(self.d + i, self.nd), self.q) for i in range(1, self.nd)]

    def line(self):
        return [(self.s, self.d, lax.rem(self.q + i, self.nq)) for i in range(1, self.nq)]

    def greet(self, devices):
        barrier = pltpu.get_barrier_semaphore()
        for device in devices:
            pl.semaphore_signal(barrier, inc=1, device_id=device, device_id_type=MESH)
        pl.semaphore_wait(barrier, len(devices))


def remote(src, dst, send_sem, recv_sem, device):
    return pltpu.make_async_remote_copy(
        src_ref=src,
        dst_ref=dst,
        send_sem=send_sem,
        recv_sem=recv_sem,
        device_id=device,
        device_id_type=MESH,
    )


class Exchange:
    def __init__(self, place, number, plane_buf, line_buf, send_sem, recv_sem):
        self.place, self.number = place, number
        self.plane_buf, self.line_buf = plane_buf.at[number], line_buf.at[number]
        self.send_sem, self.recv_sem = send_sem.at[number], recv_sem.at[number]

    def _start(self, buf, slot, rows, devices, base):
        for at, row in enumerate(rows):
            buf[slot, at : at + 1, 0 : row.shape[1]] = row
        self.copies = [
            remote(
                buf.at[slot],
                buf.at[slot],
                self.send_sem.at[base + i],
                self.recv_sem.at[base + i],
                device,
            )
            for i, device in enumerate(devices)
        ]
        for copy in self.copies:
            copy.start()

    def _finish(self, buf, count, n_rows, width):
        for copy in self.copies:
            copy.wait()
        return [[buf[j, at : at + 1, 0:width] for at in range(n_rows)] for j in range(count)]

    def start(self, rows):
        self.n_rows, self.width = len(rows), rows[0].shape[1]
        self._start(self.plane_buf, self.place.d, rows, self.place.plane(), 0)

    def relay(self, join):
        parts = self._finish(self.plane_buf, self.place.nd, self.n_rows, self.width)
        self._start(
            self.line_buf, self.place.q, join(parts), self.place.line(), self.place.nd - 1
        )

    def finish(self, join):
        return join(self._finish(self.line_buf, self.place.nq, self.n_rows, self.width))


def join_sums(parts):
    totals = parts[0]
    for part in parts[1:]:
        totals = [total + row for total, row in zip(totals, part)]
    return totals


def join_moments(count):
    def join(parts):
        n = len(parts[0]) // 2
        totals = join_sums(parts)
        means = [total * (1.0 / len(parts)) for total in totals[:n]]
        squares = totals[n:]
        for part in parts:
            squares = [
                square + count * (row - mean) * (row - mean)
                for square, row, mean in zip(squares, part[:n], means)
            ]
        return means + squares

    return join


class Norm:
    def __init__(self, mean, inv, gain, bias):
        self.mean, self.inv = eight(mean), eight(inv)
        self.gain, self.bias = (
            eight(vector[...].reshape(1, vector.shape[0])) for vector in (gain, bias)
        )

    def normed(self, block):
        return (block - self.mean[None]) * self.inv[None]

    def pre(self, normed):
        return normed * self.gain[None] + self.bias[None]


def first_kernel(
    dims,
    inputs,
    out_grad,
    shifts,
    flips,
    gain1,
    bias1,
    weight1,
    gain2,
    bias2,
    weight2,
    gain3,
    bias3,
    weight3,
    taps_out,
    placed_out,
    grad_out,
    halo_out,
    stats_out,
    sums_out,
    result_out,
    own_out,
    other_out,
    window,
    placed,
    act,
    taps,
    w1,
    w2,
    w3,
    even,
    odd,
    share,
    pooled,
    edges,
    edges_in,
    second,
    narrow,
    own_grad,
    far_grad,
    third_in,
    third,
    narrow_grad,
    narrow_taps,
    second_grad,
    block_grad,
    block_send,
    wide_grad,
    halo,
    ours,
    stats,
    sums,
    plane_buf,
    line_buf,
    local_sem,
    exchange_send,
    exchange_recv,
    halo_send,
    halo_recv,
    far_send,
    far_recv,
):
    C, H, L, B, nd, nq = dims
    half = L // 2
    place = Place(nd, nq)
    s, q = place.s, place.q
    place.greet(place.plane() + place.line())

    flip = [flips[s * B + b] for b in range(B)]
    shift = [shifts[s * B + b] for b in range(B)]
    block_at = [flip[b] * (nq - 1 - q) + (1 - flip[b]) * q for b in range(B)]
    mine = pl.ds(s * B, B)

    def exchange(number):
        return Exchange(place, number, plane_buf, line_buf, exchange_send, exchange_recv)

    def pair(number, to_next, to_prev, from_prev, from_next):
        return [
            remote(
                to_next,
                from_prev,
                halo_send.at[number, 0],
                halo_recv.at[number, 0],
                (s, place.d, place.next),
            ),
            remote(
                to_prev,
                from_next,
                halo_send.at[number, 1],
                halo_recv.at[number, 1],
                (s, place.d, place.prev),
            ),
        ]

    load = [
        pltpu.make_async_copy(inputs.at[mine], window.at[:, EDGE : EDGE + L], local_sem.at[0]),
        pltpu.make_async_copy(weight1, w1, local_sem.at[1]),
        pltpu.make_async_copy(weight2, w2, local_sem.at[2]),
        pltpu.make_async_copy(weight3, w3, local_sem.at[3]),
        pltpu.make_async_copy(out_grad.at[mine], own_grad, local_sem.at[4]),
    ]
    for copy in load:
        copy.start()
    ring = pair(
        0,
        inputs.at[mine, L - EDGE : L],
        inputs.at[mine, 0:EDGE],
        window.at[:, 0:EDGE],
        window.at[:, EDGE + L : 2 * EDGE + L],
    )
    for copy in ring:
        copy.start()

    load[0].wait()
    zero = jnp.zeros((8, C), F32)

    def moments(read, count, width):
        none = jnp.zeros((8, width), F32)
        means, squares = [], []
        for b in range(B):
            total = chunks(count, lambda r, t: t + jnp.sum(halves(read(b, r)), axis=0), none, 2)
            mean = row_sum(total) * (1.0 / count)
            mean8 = eight(mean)

            def deviations(r, t):
                away = halves(read(b, r)) - mean8[None]
                return t + jnp.sum(away * away, axis=0)

            means.append(mean)
            squares.append(row_sum(chunks(count, deviations, none, 2)))
        return means + squares

    def norms(exchange, count, gain, bias):
        exchange.relay(join_moments(float(count)))
        joined = exchange.finish(join_moments(float(count * nd)))
        scale = 1.0 / (count * nd * nq)
        inverse = [lax.rsqrt(square * scale + EPSILON) for square in joined[B:]]
        return [Norm(joined[b], inverse[b], gain, bias) for b in range(B)]

    step = exchange(0)
    step.start(
        moments(lambda b, r: window[b, pl.ds(EDGE + r, EDGE)].astype(F32), L, C)
    )

    for copy in ring:
        copy.wait()
    tall = half + EDGE
    for b in range(B):
        for parity in range(2):
            shape = (tall, L + 2 * EDGE)
            at = 2 * (lax.broadcasted_iota(jnp.int32, shape, 0) - 8) + parity
            source = flip[b] * (L - 1) + (1 - 2 * flip[b]) * at - shift[b] + EDGE
            pick = jnp.where(lax.broadcasted_iota(jnp.int32, shape, 1) == source, 1.0, 0.0)
            placed[b, parity] = jnp.dot(
                pick.astype(BF16), window[b], preferred_element_type=F32
            ).astype(BF16)
    first_norm = norms(step, L, gain1, bias1)
    mirrored = remote(
        out_grad.at[mine],
        far_grad,
        far_send.at[0],
        far_recv.at[0],
        (s, place.d, place.mirror),
    )
    mirrored.start()
    save = [pltpu.make_async_copy(placed, placed_out, local_sem.at[5])]
    save[0].start()

    for b in range(B):
        stats[b : b + 1, :] = first_norm[b].mean[0:1]
        stats[B + b : B + b + 1, :] = first_norm[b].inv[0:1]
        for parity in range(2):

            def activate(r, c):
                norm = first_norm[b]
                value = gelu(norm.pre(norm.normed(halves(placed[b, parity, pl.ds(r, EDGE)].astype(F32)))))
                value = flat(value)
                at = lax.broadcasted_iota(jnp.int32, value.shape, 0) + (r - 8)
                at = 2 * at + (parity + block_at[b] * L)
                act[pl.ds(r, EDGE)] = jnp.where((at >= 0) & (at < nq * L), value, 0.0)
                return c

            chunks(tall, activate)

            def spread(r, c):
                values = act[pl.ds(r, 2 * EDGE)]
                for off in range(3):
                    at = (2 * off + parity) * C
                    taps[pl.ds(b * half + r, EDGE), at : at + C] = values[
                        7 + off : 7 + off + EDGE
                    ].astype(BF16)
                return c

            chunks(half, spread)
    save.append(pltpu.make_async_copy(taps, taps_out, local_sem.at[6]))
    save[1].start()

    load[1].wait()
    wide = even.shape[1]
    for j in range(C // wide):
        cols = slice(j * wide, (j + 1) * wide)
        even[...] = jnp.dot(taps[:, 0 : 5 * C], w1[:, cols], preferred_element_type=F32)
        odd[...] = jnp.dot(taps[:, C : 6 * C], w1[:, cols], preferred_element_type=F32)
        for b in range(B):

            def pool(r, c):
                at = pl.ds(b * half + r, EDGE)
                left, right = even[at, :], odd[at, :]
                away = left - right
                small = jnp.exp(-jnp.abs(away))
                pooled[b, pl.ds(EDGE + r, EDGE), cols] = (
                    jnp.maximum(left, right) + jnp.log(1.0 + small)
                ).astype(BF16)
                part = 1.0 / (1.0 + small)
                share[at, cols] = jnp.where(away >= 0, part, small * part)
                return c

            chunks(half, pool)

    def send_edges(number, first, last, width):
        for b in range(B):
            for at, (head, tail) in enumerate(zip(first(b), last(b))):
                head, tail = head.astype(F32), tail.astype(F32)
                turned = flip[b] == 1
                place_at = at * B + b
                edges[number, 0, place_at, :, 0:width] = jnp.where(turned, head, tail).astype(BF16)
                edges[number, 1, place_at, :, 0:width] = jnp.where(turned, tail, head).astype(BF16)
        copies = pair(
            number + 1,
            edges.at[number, 0],
            edges.at[number, 1],
            edges_in.at[number, 0],
            edges_in.at[number, 1],
        )
        for copy in copies:
            copy.start()
        return copies

    def take_edges(number, at, b, width):
        from_prev = edges_in[number, 0, at * B + b, :, 0:width].astype(F32)
        from_next = edges_in[number, 1, at * B + b, :, 0:width].astype(F32)
        turned = flip[b] == 1
        before = jnp.where(turned, from_next, from_prev)
        after = jnp.where(turned, from_prev, from_next)
        before = jnp.where(block_at[b] > 0, before, 0.0)
        after = jnp.where(block_at[b] < nq - 1, after, 0.0)
        return before, after

    step = exchange(1)
    step.start(moments(lambda b, r: pooled[b, pl.ds(EDGE + r, EDGE)].astype(F32), half, C))
    ring = send_edges(
        0,
        lambda b: [pooled[b, EDGE : 2 * EDGE]],
        lambda b: [pooled[b, half : half + EDGE]],
        C,
    )
    second_norm = norms(step, half, gain2, bias2)
    for copy in ring:
        copy.wait()
    for b in range(B):
        before, after = take_edges(0, 0, b, C)
        pooled[b, 0:EDGE] = before.astype(BF16)
        pooled[b, EDGE + half : 2 * EDGE + half] = after.astype(BF16)
        norm = second_norm[b]

        def activate(r, c):
            value = flat(gelu(norm.pre(norm.normed(halves(pooled[b, pl.ds(r, EDGE)].astype(F32))))))
            at = lax.broadcasted_iota(jnp.int32, value.shape, 0) + (r - EDGE + block_at[b] * half)
            act[pl.ds(r, EDGE)] = jnp.where((at >= 0) & (at < nq * half), value, 0.0)
            return c

        chunks(half + 2 * EDGE, activate)

        def spread(r, c):
            values = act[pl.ds(r, 3 * EDGE)]
            for k in range(3):
                at = EDGE + (k - 1) * DILATION_SIZE
                second[pl.ds(b * half + r, EDGE), k * C : (k + 1) * C] = values[
                    at : at + EDGE
                ].astype(BF16)
            return c

        chunks(half, spread)

    load[2].wait()
    narrow[...] = jnp.dot(second[...], w2[...], preferred_element_type=F32)
    step = exchange(2)
    step.start(moments(lambda b, r: narrow[pl.ds(b * half + r, EDGE)], half, H))
    load[3].wait()
    load[4].wait()
    mirrored.wait()
    for b in range(B):

        def choose(r, c):
            at = pl.ds(r, EDGE)
            own_grad[b, at] = jnp.where(
                flip[b] == 1, far_grad[b, at].astype(F32), own_grad[b, at].astype(F32)
            ).astype(BF16)
            return c

        chunks(half, choose)
        third_in[b * half : (b + 1) * half] = lax.dot_general(
            own_grad[b], w3[...], NT, preferred_element_type=F32
        )
    third_norm = norms(step, half, gain3, bias3)

    none = jnp.zeros((8, H), F32)
    totals = []
    for b in range(B):
        norm = third_norm[b]

        def activate(r, carry):
            at = pl.ds(b * half + r, EDGE)
            normed = norm.normed(halves(narrow[at]))
            pre = norm.pre(normed)
            third[at] = flat(gelu(pre)).astype(BF16)
            grad = halves(third_in[at]) * gelu_slope(pre)
            third_in[at] = flat(grad)
            return carry[0] + jnp.sum(grad, axis=0), carry[1] + jnp.sum(grad * normed, axis=0)

        totals.append(chunks(half, activate, (none, none)))
    step = exchange(3)
    step.start([row_sum(t[0]) for t in totals] + [row_sum(t[1]) for t in totals])

    for b in range(B):
        at = slice(b * half, (b + 1) * half)
        for side in range(2):
            cols = slice(side * (C // 2), (side + 1) * (C // 2))
            ours[side, b] = (
                pooled[b, EDGE : EDGE + half, cols].astype(F32)
                + jnp.dot(third[at], w3[:, cols], preferred_element_type=F32)
            ).astype(BF16)
    save.append(pltpu.make_async_copy(ours, result_out, local_sem.at[7]))
    save[2].start()
    step.relay(join_sums)
    width = C // 2

    def keep(first, value):
        block_grad[first : first + value.shape[0]] = value
        block_send[first : first + value.shape[0]] = value.astype(BF16)

    value = sum(
        lax.dot_general(
            third[b * half : (b + 1) * half], own_grad[b], TN, preferred_element_type=F32
        )
        for b in range(B)
    )
    keep(3 * C, value[:, 0:width])
    keep(3 * C + H, value[:, width:])
    back = step.finish(join_sums)
    sums[4:5, 0:H] = sum(back[B:])
    sums[5:6, 0:H] = sum(back[:B])
    scale = 1.0 / (half * nd * nq)
    for b in range(B):
        norm = third_norm[b]
        mean_bias, mean_gain = eight(back[b] * scale), eight(back[B + b] * scale)
        factor = norm.gain * norm.inv

        def input_grad(r, c):
            at = pl.ds(b * half + r, EDGE)
            normed = norm.normed(halves(narrow[at]))
            value = factor[None] * (halves(third_in[at]) - mean_bias[None] - normed * mean_gain[None])
            narrow_grad[b, pl.ds(EDGE + r, EDGE)] = flat(value).astype(BF16)
            return c

        chunks(half, input_grad)
    ring = send_edges(
        1,
        lambda b: [narrow_grad[b, EDGE : 2 * EDGE]],
        lambda b: [narrow_grad[b, half : half + EDGE]],
        H,
    )
    for k in range(3):
        keep(
            k * C,
            sum(
                lax.dot_general(
                    second[b * half : (b + 1) * half, k * C : (k + 1) * C],
                    narrow_grad[b, EDGE : EDGE + half],
                    TN,
                    preferred_element_type=F32,
                )
                for b in range(B)
            ),
        )
    side = block_grad.shape[0] // 2
    save += [
        pltpu.make_async_copy(block_grad.at[pl.ds(s * side, side)], own_out, local_sem.at[8]),
        pltpu.make_async_copy(
            block_send.at[pl.ds((1 - s) * side, side)], other_out, local_sem.at[10]
        ),
    ]
    save[3].start()
    save[4].start()
    for copy in ring:
        copy.wait()
    for b in range(B):
        before, after = take_edges(1, 0, b, H)
        narrow_grad[b, 0:EDGE] = before.astype(BF16)
        narrow_grad[b, EDGE + half : 2 * EDGE + half] = after.astype(BF16)

        def spread(r, c):
            values = narrow_grad[b, pl.ds(r, 3 * EDGE)].astype(F32)
            for k in range(3):
                at = EDGE - (k - 1) * DILATION_SIZE
                narrow_taps[pl.ds(b * half + r, EDGE), k * H : (k + 1) * H] = values[
                    at : at + EDGE
                ].astype(BF16)
            return c

        chunks(half, spread)
    second_grad[...] = sum(
        lax.dot_general(
            narrow_taps[:, k * H : (k + 1) * H],
            w2[k * C : (k + 1) * C],
            NT,
            preferred_element_type=F32,
        )
        for k in range(3)
    )
    totals = []
    for b in range(B):
        norm = second_norm[b]

        def slope(r, carry):
            at = pl.ds(b * half + r, EDGE)
            normed = norm.normed(halves(pooled[b, pl.ds(EDGE + r, EDGE)].astype(F32)))
            grad = halves(second_grad[at]) * gelu_slope(norm.pre(normed))
            second_grad[at] = flat(grad)
            return carry[0] + jnp.sum(grad, axis=0), carry[1] + jnp.sum(grad * normed, axis=0)

        totals.append(chunks(half, slope, (zero, zero)))
    step = exchange(4)
    step.start([row_sum(t[0]) for t in totals] + [row_sum(t[1]) for t in totals])
    step.relay(join_sums)
    back = step.finish(join_sums)
    sums[2:3, :] = sum(back[B:])
    sums[3:4, :] = sum(back[:B])
    for b in range(B):
        norm = second_norm[b]
        mean_bias, mean_gain = eight(back[b] * scale), eight(back[B + b] * scale)
        factor = norm.gain * norm.inv

        def unpool(r, c):
            at = pl.ds(b * half + r, EDGE)
            normed = norm.normed(halves(pooled[b, pl.ds(EDGE + r, EDGE)].astype(F32)))
            value = factor[None] * (
                halves(second_grad[at]) - mean_bias[None] - normed * mean_gain[None]
            )
            value = flat(value) + own_grad[b, pl.ds(r, EDGE)].astype(F32)
            value = value.astype(BF16).astype(F32)
            part = share[at]
            wide_grad[0, at] = (value * part).astype(BF16)
            wide_grad[1, at] = (value * (1.0 - part)).astype(BF16)
            return c

        chunks(half, unpool)
    ring = send_edges(
        2,
        lambda b: [wide_grad[p, b * half : b * half + EDGE] for p in range(2)],
        lambda b: [wide_grad[p, (b + 1) * half - EDGE : (b + 1) * half] for p in range(2)],
        C,
    )
    save.append(pltpu.make_async_copy(wide_grad, grad_out, local_sem.at[9]))
    save[5].start()
    for copy in ring:
        copy.wait()
    for b in range(B):
        for parity in range(2):
            before, after = take_edges(2, parity, b, C)
            halo[0, parity, b] = before.astype(BF16)
            halo[1, parity, b] = after.astype(BF16)
    save += [
        pltpu.make_async_copy(halo, halo_out, local_sem.at[11]),
        pltpu.make_async_copy(stats, stats_out, local_sem.at[12]),
        pltpu.make_async_copy(sums, sums_out, local_sem.at[13]),
    ]
    for copy in save[6:]:
        copy.start()
    for copy in save:
        copy.wait()


class Cube:
    def __init__(self, place, blocks, width, refs):
        self.place, self.blocks, self.width = place, blocks, width
        self.total, self.inbox, self.relayed, self.summed, self.out = refs[:5]
        self.send_sem, self.core_recv, self.down_recv, self.up_recv, self.share_recv = refs[5:]
        self.sources = [None] * blocks
        self.axes = cube_axes(place)
        self.planar = place.nd.bit_length() - 1
        self.flight = [None] * blocks
        self.state = [None] * blocks

    def order(self, block):
        return [self.axes[i] for i in cube_order(block, self.planar, len(self.axes))]

    def events(self):
        depth = len(self.axes)
        return ["core"] + ["down"] * depth + ["up"] * halvings(depth) + ["share", "out"]

    def _add(self, block, incoming, first, count, send):
        total, inbox = self.total, self.inbox

        step = min(count, 4 * EDGE)
        for r in range(0, count, step):
            at = pl.ds(pl.multiple_of(first + r, EDGE), step)
            value = total[block, at] + incoming(r, step).astype(F32)
            total[block, at] = value
            if send:
                inbox[block, at] = value.astype(BF16)

    def run(self, block, stage):
        place, depth = self.place, len(self.axes)
        s = place.s
        last = depth + halvings(depth)
        if self.flight[block] is not None:
            self.flight[block].wait()
        if stage == 0:
            copy = remote(
                self.sources[block],
                self.inbox.at[block],
                self.send_sem.at[block],
                self.core_recv.at[block],
                place.partner,
            )
        elif stage <= depth:
            k = stage - 1
            partner, side = self.order(block)[k]
            size, first, past = sizes(k), [0], None
            if k > 0:
                first, past = self.state[block]
            offset = first[-1]
            if k == 0:
                incoming = lambda base: lambda r, n: self.inbox[
                    block, pl.ds(pl.multiple_of(base + r, EDGE), n)
                ]
                base_of = lambda at: at
            else:
                incoming = lambda base: lambda r, n: self.relayed[
                    block, pl.ds(pl.multiple_of(base + r, EDGE), n)
                ]
                base_of = lambda at: at - offset + region(k - 1)
            if size >= 2 * EDGE:
                small = size // 2
                give, hold = offset + (1 - side) * small, offset + side * small
                self._add(block, incoming(base_of(give)), give, small, True)
            else:
                small, give, hold = size, offset, offset
                self._add(block, incoming(base_of(give)), give, small, True)
                at = pl.ds(pl.multiple_of(give, EDGE), small)
                self.total[block, at] = self.inbox[block, at].astype(F32)
            copy = remote(
                self.inbox.at[block, pl.ds(pl.multiple_of(give, EDGE), small)],
                self.relayed.at[block, region(k) : region(k) + small],
                self.send_sem.at[block],
                self.down_recv.at[block, k],
                partner,
            )
            self.state[block] = (first + [hold], past)
        elif stage <= last:
            k = last - stage
            first, _ = self.state[block]
            partner, _ = self.order(block)[k]
            hold, small = first[k + 1], sizes(k + 1)
            at = pl.ds(pl.multiple_of(hold, EDGE), small)
            if stage == depth + 1:
                end = pl.ds(pl.multiple_of(first[-1], EDGE), sizes(depth))
                begin = region(depth - 1)
                self.summed[s, block, end] = (
                    self.total[block, end]
                    + self.relayed[block, begin : begin + sizes(depth)].astype(F32)
                ).astype(BF16)
            copy = remote(
                self.summed.at[s, block, at],
                self.summed.at[s, block, at],
                self.send_sem.at[block],
                self.up_recv.at[block, k],
                partner,
            )
        elif stage == last + 1:
            copy = remote(
                self.summed.at[s, block],
                self.summed.at[s, block],
                self.send_sem.at[block],
                self.share_recv.at[block],
                place.partner,
            )
        else:
            copy = pltpu.make_async_copy(
                self.summed.at[:, block], self.out.at[:, block], self.send_sem.at[block]
            )
        if stage > 0 and stage <= depth:
            copy.start()
            if size >= 2 * EDGE:
                self._add(block, incoming(base_of(hold)), hold, small, False)
        else:
            copy.start()
        self.flight[block] = copy

    def end(self):
        for copy in self.flight:
            copy.wait()


BLOCK = 256
HOP = 14.0


def sizes(k):
    return max(BLOCK >> k, EDGE)


def region(k):
    return sum(sizes(i + 1) for i in range(k))


def halvings(depth):
    return sum(sizes(k) >= 2 * EDGE for k in range(depth))


def cube_axes(place):
    axes = []
    bit = 1
    while bit < place.nd:
        side = lax.rem(place.d // bit, 2)
        axes.append(((place.s, place.d + bit * (1 - 2 * side), place.q), side))
        bit *= 2
    bit = 1
    while bit < place.nq:
        side = lax.rem(place.q // bit, 2)
        axes.append(((place.s, place.d, place.q + bit * (1 - 2 * side)), side))
        bit *= 2
    return axes


def cube_order(block, planar, depth):
    order = [(block + i) % planar for i in range(planar)] + list(range(planar, depth))
    if block % 6 == 5:
        order.remove(planar)
        order = [planar] + order
    return order


def plan(planar, depth, blocks, pieces, events):
    rate, cost = 95e3, 0.2
    free = [0.0] * (depth + 1)
    ready = {}
    now, order, done = 0.0, [], 0.0
    pieces = list(pieces)

    def send(axis, size):
        if axis == depth:
            loads, speed, wait = [(depth, 1)], 6 * rate, 1.1
        elif axis > planar:
            loads, speed, wait = [(planar, 1), (axis, 2)], rate, 2.8
        else:
            loads, speed, wait = [(axis, 1)], rate, 2.2
        begin = max([now] + [free[i] for i, _ in loads])
        for i, times in loads:
            free[i] = begin + times * size / speed
        return max(free[i] for i, _ in loads) + wait

    while pieces or ready:
        able = sorted((t, b) for b, (t, _) in ready.items() if t <= now)
        if able:
            _, block = able[0]
            _, stage = ready.pop(block)
            order.append((block, stage))
            kind = events[stage]
            now += cost if kind == "down" else 0.05
            if stage + 1 < len(events):
                axes = cube_order(block, planar, depth)
                if kind in ("core", "share"):
                    axis, size = depth, BLOCK
                elif kind == "down":
                    axis, size = axes[stage - 1], sizes(stage)
                elif kind == "up":
                    k = depth + halvings(depth) - stage
                    axis, size = axes[k], sizes(k + 1)
                else:
                    axis, size = depth, 0
                ready[block] = (send(axis, 2 * size * 768), stage + 1)
        elif pieces and done + pieces[0][4] <= now:
            name, time, made, sends, _ = pieces.pop(0)
            order.append(name)
            now += time
            done = now
            for block in made:
                ready[block] = (now, 0)
            for axis, size in sends:
                send(axis, size)
        else:
            now = min([t for t, _ in ready.values()] + [done + p[4] for p in pieces[:1]])
    return order


def tail_kernel(
    dims,
    taps_in,
    placed_in,
    grad_in,
    halo_in,
    own_in,
    other_in,
    result_in,
    stats,
    sums_in,
    shifts,
    flips,
    gain1,
    bias1,
    weight1,
    summed_out,
    near_out,
    far_out,
    back_out,
    gain1_out,
    bias1_out,
    gain2_out,
    bias2_out,
    gain3_out,
    bias3_out,
    total,
    inbox,
    sending,
    relayed,
    summed,
    product,
    placed,
    grads,
    halo,
    w1,
    taps,
    act_grad,
    edges,
    edges_in,
    window,
    ours,
    final,
    sums,
    plane_buf,
    line_buf,
    local_sem,
    exchange_send,
    exchange_recv,
    halo_send,
    halo_recv,
    core_send,
    core_recv,
    result_send,
    result_recv,
    *cube_sems,
):
    C, H, L, B, nd, nq = dims
    half = L // 2
    width = C // 2
    place = Place(nd, nq)
    s, q = place.s, place.q
    cross = (1 - s, place.d, place.mirror)
    mine = pl.ds(s * B, B)
    first_blocks = own_in.shape[0] // BLOCK
    per_tap = C // BLOCK
    blocks = first_blocks + 5 * per_tap
    cube = Cube(place, blocks, width, (total, inbox, relayed, summed, summed_out) + cube_sems)
    depth = len(cube.axes)
    place.greet(place.plane() + place.line() + [place.partner, cross])
    flip = [flips[s * B + b] for b in range(B)]
    shift = [shifts[s * B + b] for b in range(B)]
    load = [
        pltpu.make_async_copy(
            own_in.at[i * BLOCK : (i + 1) * BLOCK], total.at[i], local_sem.at[6 + i]
        )
        for i in range(first_blocks)
    ]
    load_taps = pltpu.make_async_copy(taps_in, taps, local_sem.at[0])
    load_grads = pltpu.make_async_copy(grad_in, grads, local_sem.at[1])
    load_rest = [
        pltpu.make_async_copy(halo_in, halo, local_sem.at[2]),
        pltpu.make_async_copy(weight1, w1, local_sem.at[3]),
        pltpu.make_async_copy(placed_in, placed, local_sem.at[4]),
    ]
    for copy in [load_taps, load_grads] + load + load_rest:
        copy.start()
    for i in range(first_blocks):
        cube.sources[i] = other_in.at[i * BLOCK : (i + 1) * BLOCK]
    for i in range(5 * per_tap):
        cube.sources[first_blocks + i] = sending.at[i]
    todo, pieces = {}, []

    def piece(name, time, made=(), sends=(), after=0.0):
        def keep(body):
            todo[name] = body
            pieces.append((name, time, made, sends, after))
            return body

        return keep

    @piece("block gradients", 0.3, range(first_blocks))
    def _():
        for copy in load:
            copy.wait()

    across = remote(
        result_in.at[1 - s], near_out, result_send.at[0], result_recv.at[0], place.partner
    )
    away = [
        remote(
            result_in.at[side, b],
            far_out.at[s * B + b],
            result_send.at[1 + 2 * b + i],
            result_recv.at[1 + 2 * b + i],
            (side, place.d, place.mirror),
        )
        for b in range(B)
        for i, side in enumerate((s, 1 - s))
    ]
    across.start()

    def result_piece(i):
        @piece(("result", i), 0.05, (), [(depth - 1, 4 * half * width)])
        def _():
            away[i].start()

    def weight_piece(k):
        made = range(first_blocks + k * per_tap, first_blocks + (k + 1) * per_tap)

        @piece(("weight", k), 1.9, made)
        def _():
            if k == 0:
                load_taps.wait()
                load_grads.wait()

            def tile(m, c):
                lanes = pl.multiple_of(k * C + m * BLOCK, BLOCK)
                product[...] = lax.dot_general(
                    taps[:, pl.ds(lanes, BLOCK)], grads[0], TN, preferred_element_type=F32
                ) + lax.dot_general(
                    taps[:, pl.ds(lanes + C, BLOCK)], grads[1], TN, preferred_element_type=F32
                )

                def split(r, c):
                    at = pl.ds(r, EDGE)
                    low = pl.ds(pl.multiple_of(s * width, width), width)
                    high = pl.ds(pl.multiple_of((1 - s) * width, width), width)
                    total[first_blocks + k * per_tap + m, at] = product[at, low]
                    sending[k * per_tap + m, at] = product[at, high].astype(BF16)
                    return c

                chunks(BLOCK, split)
                return c

            lax.fori_loop(0, per_tap, tile, 0)

    for k in range(5):
        if k < 2 * B:
            result_piece(k)
        weight_piece(k)

    def put(b, parity, r, values):
        base = (1 - parity) * C
        for at in range(3):
            lanes = base + 2 * at * C
            taps[pl.ds(b * half + r, EDGE), lanes : lanes + C] = values[
                EDGE + 1 - at : 2 * EDGE + 1 - at
            ].astype(BF16)

    def spread_piece(b, parity):
        @piece(("spread", b, parity), 0.6)
        def _():
            if b == 0 and parity == 0:
                load_rest[0].wait()

            def spread(i, c):
                r = pl.multiple_of(i * EDGE, EDGE)
                values = grads[parity, pl.ds(b * half + r - EDGE, 3 * EDGE)].astype(F32)
                put(b, parity, r, values)
                return c

            lax.fori_loop(1, half // EDGE - 1, spread, 0)
            low, high = b * half, (b + 1) * half
            put(
                b,
                parity,
                0,
                jnp.concatenate(
                    [halo[0, parity, b], grads[parity, low : low + 2 * EDGE]], axis=0
                ).astype(F32),
            )
            put(
                b,
                parity,
                half - EDGE,
                jnp.concatenate(
                    [grads[parity, high - 2 * EDGE : high], halo[1, parity, b]], axis=0
                ).astype(F32),
            )

    for b in range(B):
        for parity in range(2):
            spread_piece(b, parity)

    def convolve_piece(parity, j):
        @piece(("convolve", parity, j), 1.4)
        def _():
            if parity == 0 and j == 0:
                load_rest[1].wait()
                load_rest[2].wait()
            part = None
            for k in range(5):
                lanes = (k + 1 - parity) * C
                more = lax.dot_general(
                    taps[:, lanes : lanes + C],
                    w1[k, j * 256 : (j + 1) * 256, :],
                    NT,
                    preferred_element_type=F32,
                )
                part = more if part is None else part + more
            act_grad[parity, :, j * 256 : (j + 1) * 256] = part

    for parity in range(2):
        for j in range(C // 256):
            convolve_piece(parity, j)
    norms = [
        Norm(stats[b : b + 1, :], stats[B + b : B + b + 1, :], gain1, bias1)
        for b in range(B)
    ]
    zero = jnp.zeros((8, C), F32)
    carries = [(zero, zero) for _ in range(B)]

    def slope_piece(b, parity):
        @piece(("slope", b, parity), 1.2)
        def _():
            norm = norms[b]

            def slope(r, carry):
                at = pl.ds(b * half + r, EDGE)
                values = placed[b, parity, pl.ds(r, 2 * EDGE)].astype(F32)[8 : 8 + EDGE]
                normed = norm.normed(halves(values))
                grad = halves(act_grad[parity, at]) * gelu_slope(norm.pre(normed))
                act_grad[parity, at] = flat(grad)
                return carry[0] + jnp.sum(grad, axis=0), carry[1] + jnp.sum(grad * normed, axis=0)

            carries[b] = chunks(half, slope, carries[b])

    for b in range(B):
        for parity in range(2):
            slope_piece(b, parity)
    step = Exchange(place, 0, plane_buf, line_buf, exchange_send, exchange_recv)
    back = []
    swap = remote(sums.at[0], sums.at[1], core_send.at[0], core_recv.at[0], place.partner)

    @piece("exchange", 0.3)
    def _():
        step.start([row_sum(t[0]) for t in carries] + [row_sum(t[1]) for t in carries])

    @piece("relay", 0.3, after=HOP)
    def _():
        step.relay(join_sums)

    @piece("finish", 0.1, after=HOP)
    def _():
        back.extend(step.finish(join_sums))
        sums[0] = sums_in[...]
        sums[0, 0:1, :] = sum(back[B:])
        sums[0, 1:2, :] = sum(back[:B])
        swap.start()

    scale = 1.0 / (L * nd * nq)
    tall = half + 2 * EDGE

    def gradient_piece(b, parity):
        @piece(("gradient", b, parity), 0.8)
        def _():
            norm = norms[b]
            mean_bias, mean_gain = eight(back[b] * scale), eight(back[B + b] * scale)
            factor = norm.gain * norm.inv

            def input_grad(r, c):
                values = placed[b, parity, pl.ds(r, 2 * EDGE)].astype(F32)[8 : 8 + EDGE]
                normed = norm.normed(halves(values))
                value = factor[None] * (
                    halves(act_grad[parity, pl.ds(b * half + r, EDGE)])
                    - mean_bias[None]
                    - normed * mean_gain[None]
                )
                window[b, pl.ds(parity * tall + EDGE + r, EDGE)] = flat(value).astype(BF16)
                return c

            chunks(half, input_grad)

    for b in range(B):
        for parity in range(2):
            gradient_piece(b, parity)
    ring = [
        remote(
            edges.at[i],
            edges_in.at[i],
            halo_send.at[i],
            halo_recv.at[i],
            (s, place.d, at),
        )
        for i, at in enumerate((place.next, place.prev))
    ]

    @piece("edges", 0.3)
    def _():
        for b in range(B):
            turned = flip[b] == 1
            for parity in range(2):
                low = parity * tall
                head = window[b, low + EDGE : low + 2 * EDGE].astype(F32)
                end = window[b, low + half : low + half + EDGE].astype(F32)
                edges[0, parity, b] = jnp.where(turned, head, end).astype(BF16)
                edges[1, parity, b] = jnp.where(turned, end, head).astype(BF16)
        for copy in ring:
            copy.start()

    @piece("halo", 0.1, after=HOP)
    def _():
        for copy in ring:
            copy.wait()

    def place_piece(b, side):
        @piece(("place", b, side), 1.0)
        def _():
            turned = flip[b] == 1
            for parity in range(2):
                low = parity * tall
                from_prev = edges_in[0, parity, b].astype(F32)
                from_next = edges_in[1, parity, b].astype(F32)
                window[b, low : low + EDGE] = jnp.where(turned, from_next, from_prev).astype(BF16)
                window[b, low + EDGE + half : low + tall] = jnp.where(
                    turned, from_prev, from_next
                ).astype(BF16)
            shape = (L, 2 * tall)
            at = lax.broadcasted_iota(jnp.int32, shape, 0) + shift[b]
            at = flip[b] * (L - 1) + (1 - 2 * flip[b]) * at
            source = (at & 1) * tall + (at >> 1) + EDGE
            pick = jnp.where(lax.broadcasted_iota(jnp.int32, shape, 1) == source, 1.0, 0.0)
            cols = slice(side * width, (side + 1) * width)
            ours[side, b] = jnp.dot(
                pick.astype(BF16), window[b, :, cols], preferred_element_type=F32
            ).astype(BF16)

    for b in range(B):
        for side in range(2):
            place_piece(b, side)
    cross_back = remote(
        ours.at[1 - s], final, core_send.at[1], core_recv.at[1], place.partner
    )
    keep_back = pltpu.make_async_copy(ours.at[s], back_out.at[mine], local_sem.at[0])
    give_back = pltpu.make_async_copy(
        final, back_out.at[pl.ds((1 - s) * B, B)], local_sem.at[1]
    )

    @piece("swap", 0.1)
    def _():
        cross_back.start()
        keep_back.start()
        swap.wait()
        outs = (gain1_out, bias1_out, gain2_out, bias2_out, gain3_out, bias3_out)
        for i, to in enumerate(outs):
            count = to.shape[0]
            row = sums[0, i : i + 1, 0:count] + sums[1, i : i + 1, 0:count]
            to[...] = row.reshape(count)

    @piece("give", 0.1, after=4.0)
    def _():
        cross_back.wait()
        give_back.start()

    for item in plan(cube.planar, depth, blocks, pieces, cube.events()):
        if item in todo:
            todo[item]()
        else:
            cube.run(*item)
    cube.end()
    across.wait()
    for copy in away:
        copy.wait()
    keep_back.wait()
    give_back.wait()


def finish_kernel(
    dims,
    first_blocks,
    summed,
    mine,
    near,
    far,
    back,
    flips,
    conv1,
    conv2,
    conv3,
    result,
    back_out,
    held,
    wide,
    narrow,
    near_buf,
    far_buf,
    back_buf,
    in_sem,
    wide_sem,
    narrow_sem,
    side_sem,
):
    C, H, L, B, nd, nq = dims
    s = lax.axis_index("section")
    blocks = summed.shape[1]
    width = C // 2
    slots = wide.shape[0]
    order = list(range(first_blocks, blocks)) + list(range(first_blocks))
    loads = {
        block: pltpu.make_async_copy(summed.at[:, block], held.at[block], in_sem.at[block])
        for block in order
    }
    sides = [
        pltpu.make_async_copy(mine.at[s], near_buf.at[pl.ds(s * B, B)], side_sem.at[0]),
        pltpu.make_async_copy(near, near_buf.at[pl.ds((1 - s) * B, B)], side_sem.at[1]),
        pltpu.make_async_copy(far, far_buf, side_sem.at[2]),
        pltpu.make_async_copy(back, back_buf, side_sem.at[3]),
    ]
    for block in order[:4]:
        loads[block].start()
    for copy in sides:
        copy.start()
    for block in order[4:]:
        loads[block].start()
    bottom = 3 * C

    def targets(block, side):
        row = side * first_blocks * BLOCK + block * BLOCK
        if row < bottom:
            return [(0, BLOCK, conv2.at[row : row + BLOCK])]
        parts, at = [], 0
        while at < BLOCK:
            which, first = (row - bottom + at) // H, (row - bottom + at) % H
            count = min(BLOCK - at, H - first)
            cols = slice(which * width, (which + 1) * width)
            parts.append((at, count, conv3.at[first : first + count, cols]))
            at += count
        return parts

    going = [[] for _ in range(slots)]
    for i, block in enumerate(order):
        slot = i % slots
        for copy in going[slot]:
            copy.wait()
        loads[block].wait()
        for side in range(2):

            def widen(r, c):
                at = pl.ds(pl.multiple_of(r * 64, 64), 64)
                value = held[block, side, at].astype(F32)
                if block >= first_blocks:
                    wide[slot, at, side * width : (side + 1) * width] = value
                else:
                    narrow[slot, side, at] = value
                return c

            lax.fori_loop(0, BLOCK // 64, widen, 0)
        if block >= first_blocks:
            row = (block - first_blocks) * BLOCK
            going[slot] = [
                pltpu.make_async_copy(
                    wide.at[slot], conv1.at[row : row + BLOCK], wide_sem.at[slot]
                )
            ]
        else:
            parts = [(side, *part) for side in range(2) for part in targets(block, side)]
            going[slot] = [
                pltpu.make_async_copy(
                    narrow.at[slot, side, at : at + count], to, narrow_sem.at[slot, j]
                )
                for j, (side, at, count, to) in enumerate(parts)
            ]
        for copy in going[slot]:
            copy.start()
        if i == 2:
            sides[3].wait()
            give = pltpu.make_async_copy(back_buf, back_out, side_sem.at[3])
            give.start()
        if i == 4:
            for copy in sides[:3]:
                copy.wait()
            for b in range(2 * B):
                turned = flips[b]

                def deliver(r, c):
                    at = pl.ds(pl.multiple_of(r * 64, 64), 64)
                    near_buf[b, at] = jnp.where(
                        turned == 1, far_buf[b, at].astype(F32), near_buf[b, at].astype(F32)
                    ).astype(BF16)
                    return c

                lax.fori_loop(0, L // 128, deliver, 0)
            hand = pltpu.make_async_copy(near_buf, result, side_sem.at[0])
            hand.start()
    for copies in going:
        for copy in copies:
            copy.wait()
    give.wait()
    hand.wait()


def on_device(
    nd,
    nq,
    inputs,
    shifts,
    flips,
    gain1,
    bias1,
    weight1,
    gain2,
    bias2,
    weight2,
    gain3,
    bias3,
    weight3,
    out_grad,
):
    sequences, L, C = inputs.shape
    H = weight3.shape[0]
    B, half = sequences // 2, L // 2
    rows = B * half
    dims = (C, H, L, B, nd, nq)
    anywhere = pl.BlockSpec(memory_space=pl.ANY)
    vmem = pl.BlockSpec(memory_space=pltpu.VMEM)
    smem = pl.BlockSpec(memory_space=pltpu.SMEM)
    peers = nd - 1 + nq - 1
    shape = jax.ShapeDtypeStruct
    dma = pltpu.SemaphoreType.DMA
    width = C // 2
    side = (3 * C * H + H * C) // width // 2
    taps, placed, grads, halo, stats, sums, result, own, other = pl.pallas_call(
        functools.partial(first_kernel, dims),
        name="forward_and_back",
        out_shape=(
            shape((rows, 6 * C), BF16),
            shape((B, 2, half + EDGE, C), BF16),
            shape((2, rows, C), BF16),
            shape((2, 2, B, EDGE, C), BF16),
            shape((8, C), F32),
            shape((8, C), F32),
            shape((2, B, half, width), BF16),
            shape((side, width), F32),
            shape((side, width), BF16),
        ),
        in_specs=[
            anywhere,
            anywhere,
            smem,
            smem,
            vmem,
            vmem,
            anywhere,
            vmem,
            vmem,
            anywhere,
            vmem,
            vmem,
            anywhere,
        ],
        out_specs=[anywhere] * 9,
        scratch_shapes=[
            pltpu.VMEM((B, L + 2 * EDGE, C), BF16),
            pltpu.VMEM((B, 2, half + EDGE, C), BF16),
            pltpu.VMEM((half + 2 * EDGE, C), F32),
            pltpu.VMEM((rows, 6 * C), BF16),
            pltpu.VMEM((5 * C, C), BF16),
            pltpu.VMEM((3 * C, H), BF16),
            pltpu.VMEM((H, C), BF16),
            pltpu.VMEM((rows, C // 3), F32),
            pltpu.VMEM((rows, C // 3), F32),
            pltpu.VMEM((rows, C), F32),
            pltpu.VMEM((B, half + 2 * EDGE, C), BF16),
            pltpu.VMEM((3, 2, 2 * B, EDGE, C), BF16),
            pltpu.VMEM((3, 2, 2 * B, EDGE, C), BF16),
            pltpu.VMEM((rows, 3 * C), BF16),
            pltpu.VMEM((rows, H), F32),
            pltpu.VMEM((B, half, C), BF16),
            pltpu.VMEM((B, half, C), BF16),
            pltpu.VMEM((rows, H), F32),
            pltpu.VMEM((rows, H), BF16),
            pltpu.VMEM((B, half + 2 * EDGE, H), BF16),
            pltpu.VMEM((rows, 3 * H), BF16),
            pltpu.VMEM((rows, C), F32),
            pltpu.VMEM((2 * side, width), F32),
            pltpu.VMEM((2 * side, width), BF16),
            pltpu.VMEM((2, rows, C), BF16),
            pltpu.VMEM((2, 2, B, EDGE, C), BF16),
            pltpu.VMEM((2, B, half, width), BF16),
            pltpu.VMEM((8, C), F32),
            pltpu.VMEM((8, C), F32),
            pltpu.VMEM((5, nd, 8, C), F32),
            pltpu.VMEM((5, nq, 8, C), F32),
            dma((14,)),
            dma((5, peers)),
            dma((5, peers)),
            dma((4, 2)),
            dma((4, 2)),
            dma((1,)),
            dma((1,)),
        ],
        compiler_params=pltpu.CompilerParams(
            collective_id=0, has_side_effects=True, vmem_limit_bytes=58 * 2**20
        ),
    )(
        inputs,
        out_grad,
        shifts,
        flips,
        gain1,
        bias1,
        weight1.reshape(5 * C, C),
        gain2,
        bias2,
        weight2.reshape(3 * C, H),
        gain3,
        bias3,
        weight3,
    )
    first_blocks = side // BLOCK
    blocks = first_blocks + 5 * C // BLOCK
    depth = (nd.bit_length() - 1) + (nq.bit_length() - 1)
    summed, near, far, back, *vectors = pl.pallas_call(
        functools.partial(tail_kernel, dims),
        name="sum_and_back",
        out_shape=(
            shape((2, blocks, BLOCK, width), BF16),
            shape((B, half, width), BF16),
            shape((2 * B, half, width), BF16),
            shape((2 * B, L, width), BF16),
        )
        + (shape((C,), F32),) * 4
        + (shape((H,), F32),) * 2,
        in_specs=[
            anywhere,
            anywhere,
            anywhere,
            anywhere,
            anywhere,
            anywhere,
            anywhere,
            vmem,
            vmem,
            smem,
            smem,
            vmem,
            vmem,
            anywhere,
        ],
        out_specs=[anywhere] * 4 + [vmem] * 6,
        scratch_shapes=[
            pltpu.VMEM((blocks, BLOCK, width), F32),
            pltpu.VMEM((blocks, BLOCK, width), BF16),
            pltpu.VMEM((blocks - first_blocks, BLOCK, width), BF16),
            pltpu.VMEM((blocks, region(depth), width), BF16),
            pltpu.VMEM((2, blocks, BLOCK, width), BF16),
            pltpu.VMEM((BLOCK, C), F32),
            pltpu.VMEM((B, 2, half + EDGE, C), BF16),
            pltpu.VMEM((2, rows, C), BF16),
            pltpu.VMEM((2, 2, B, EDGE, C), BF16),
            pltpu.VMEM((5, C, C), BF16),
            pltpu.VMEM((rows, 6 * C), BF16),
            pltpu.VMEM((2, rows, C), F32),
            pltpu.VMEM((2, 2, B, EDGE, C), BF16),
            pltpu.VMEM((2, 2, B, EDGE, C), BF16),
            pltpu.VMEM((B, 2 * (half + 2 * EDGE), C), BF16),
            pltpu.VMEM((2, B, L, width), BF16),
            pltpu.VMEM((B, L, width), BF16),
            pltpu.VMEM((2, 8, C), F32),
            pltpu.VMEM((1, nd, 8, C), F32),
            pltpu.VMEM((1, nq, 8, C), F32),
            dma((6 + first_blocks,)),
            dma((1, peers)),
            dma((1, peers)),
            dma((2,)),
            dma((2,)),
            dma((2,)),
            dma((2,)),
            dma((1 + 2 * B,)),
            dma((1 + 2 * B,)),
            dma((blocks,)),
            dma((blocks,)),
            dma((blocks, depth)),
            dma((blocks, halvings(depth))),
            dma((blocks,)),
        ],
        compiler_params=pltpu.CompilerParams(
            collective_id=1, has_side_effects=True, vmem_limit_bytes=60 * 2**20
        ),
    )(
        taps,
        placed,
        grads,
        halo,
        own,
        other,
        result,
        stats,
        sums,
        shifts,
        flips,
        gain1,
        bias1,
        weight1,
    )
    slots = 6
    conv1, conv2, conv3, result, back = pl.pallas_call(
        functools.partial(finish_kernel, dims, first_blocks),
        name="widen",
        out_shape=(
            shape((5 * C, C), F32),
            shape((3 * C, H), F32),
            shape((H, C), F32),
            shape((2 * B, half, width), BF16),
            shape((2 * B, L, width), BF16),
        ),
        in_specs=[anywhere] * 5 + [smem],
        out_specs=[anywhere] * 5,
        scratch_shapes=[
            pltpu.VMEM((blocks, 2, BLOCK, width), BF16),
            pltpu.VMEM((slots, BLOCK, C), F32),
            pltpu.VMEM((slots, 2, BLOCK, width), F32),
            pltpu.VMEM((2 * B, half, width), BF16),
            pltpu.VMEM((2 * B, half, width), BF16),
            pltpu.VMEM((2 * B, L, width), BF16),
            dma((blocks,)),
            dma((slots,)),
            dma((slots, 4)),
            dma((4,)),
        ],
        compiler_params=pltpu.CompilerParams(vmem_limit_bytes=32 * 2**20),
    )(summed, result, near, far, back, flips)
    return (
        result,
        back,
        conv1.reshape(5, C, C),
        vectors[0],
        vectors[1],
        conv2.reshape(3, C, H),
        vectors[2],
        vectors[3],
        conv3,
        vectors[4],
        vectors[5],
    )


def solution(mesh):
    whole = P()
    split = P("dp", "seq", None)
    return jax.shard_map(
        functools.partial(on_device, mesh.shape["dp"], mesh.shape["seq"]),
        mesh=mesh,
        in_specs=(split, P("dp"), P("dp")) + (whole,) * 9 + (split,),
        out_specs=(P("dp", "seq", "section"),) * 2 + (whole,) * 9,
        check_vma=False,
    )
```

```python
import functools

import jax
import jax.numpy as jnp
from jax import lax
from jax.experimental import pallas as pl
from jax.experimental.pallas import tpu as pltpu
from jax.sharding import PartitionSpec as P

DILATION_SIZE = 11
EPSILON = 0.001
EDGE = 16
MESH = pl.DeviceIdType.MESH
F32 = jnp.float32
BF16 = jnp.bfloat16
SCALE = 0.7978845608028654
CUBIC = 0.044715
TN = (((0,), (0,)), ((), ()))
NT = (((1,), (1,)), ((), ()))


def gelu(u):
    return 0.5 * u * (1.0 + jnp.tanh(SCALE * u * (1.0 + CUBIC * (u * u))))


def gelu_slope(u):
    square = u * u
    t = jnp.tanh(SCALE * u * (1.0 + CUBIC * square))
    return 0.5 * (1.0 + t) + (0.5 * SCALE) * u * (1.0 - t * t) * (1.0 + (3.0 * CUBIC) * square)


def chunks(count, body, carry=0, unroll=2):
    def step(i, carry):
        return body(pl.multiple_of(i * EDGE, EDGE), carry)

    return lax.fori_loop(0, count // EDGE, step, carry, unroll=unroll)


def eight(row):
    return jnp.broadcast_to(row, (8, row.shape[-1]))


def halves(block):
    return block.reshape(block.shape[0] // 8, 8, block.shape[1])


def flat(block):
    return block.reshape(block.shape[0] * 8, block.shape[2])


def row_sum(block):
    return jnp.sum(block, axis=0, keepdims=True)


class Place:
    def __init__(self, nd, nq):
        self.nd, self.nq = nd, nq
        self.s, self.d, self.q = (lax.axis_index(a) for a in ("section", "dp", "seq"))
        self.mirror = nq - 1 - self.q
        self.next = lax.rem(self.q + 1, nq)
        self.prev = lax.rem(self.q + nq - 1, nq)
        self.partner = (1 - self.s, self.d, self.q)

    def plane(self):
        return [(self.s, lax.rem(self.d + i, self.nd), self.q) for i in range(1, self.nd)]

    def line(self):
        return [(self.s, self.d, lax.rem(self.q + i, self.nq)) for i in range(1, self.nq)]

    def greet(self, devices):
        barrier = pltpu.get_barrier_semaphore()
        for device in devices:
            pl.semaphore_signal(barrier, inc=1, device_id=device, device_id_type=MESH)
        pl.semaphore_wait(barrier, len(devices))


def remote(src, dst, send_sem, recv_sem, device):
    return pltpu.make_async_remote_copy(
        src_ref=src,
        dst_ref=dst,
        send_sem=send_sem,
        recv_sem=recv_sem,
        device_id=device,
        device_id_type=MESH,
    )


class Exchange:
    def __init__(self, place, number, sems, plane_buf, line_buf, send_sem, recv_sem):
        self.place = place
        self.plane_buf, self.line_buf = plane_buf.at[number], line_buf.at[number]
        self.send_sem, self.recv_sem = send_sem.at[sems], recv_sem.at[sems]

    def _start(self, buf, slot, rows, devices, base):
        for at, row in enumerate(rows):
            buf[slot, at : at + 1, 0 : row.shape[1]] = row
        self.copies = [
            remote(
                buf.at[slot],
                buf.at[slot],
                self.send_sem.at[base + i],
                self.recv_sem.at[base + i],
                device,
            )
            for i, device in enumerate(devices)
        ]
        for copy in self.copies:
            copy.start()

    def _finish(self, buf, count, n_rows, width):
        for copy in self.copies:
            copy.wait()
        return [[buf[j, at : at + 1, 0:width] for at in range(n_rows)] for j in range(count)]

    def start(self, rows):
        self.n_rows, self.width = len(rows), rows[0].shape[1]
        self._start(self.plane_buf, self.place.d, rows, self.place.plane(), 0)

    def relay(self, join):
        parts = self._finish(self.plane_buf, self.place.nd, self.n_rows, self.width)
        self._start(
            self.line_buf, self.place.q, join(parts), self.place.line(), self.place.nd - 1
        )

    def finish(self, join):
        return join(self._finish(self.line_buf, self.place.nq, self.n_rows, self.width))


def join_sums(parts):
    totals = parts[0]
    for part in parts[1:]:
        totals = [total + row for total, row in zip(totals, part)]
    return totals


def join_moments(count):
    def join(parts):
        n = len(parts[0]) // 2
        totals = join_sums(parts)
        means = [total * (1.0 / len(parts)) for total in totals[:n]]
        squares = totals[n:]
        for part in parts:
            squares = [
                square + count * (row - mean) * (row - mean)
                for square, row, mean in zip(squares, part[:n], means)
            ]
        return means + squares

    return join


class Norm:
    def __init__(self, mean, inv, gain, bias):
        self.mean, self.inv = eight(mean), eight(inv)
        self.gain, self.bias = (
            eight(vector[...].reshape(1, vector.shape[0])) for vector in (gain, bias)
        )

    def normed(self, block):
        return (block - self.mean[None]) * self.inv[None]

    def pre(self, normed):
        return normed * self.gain[None] + self.bias[None]


def chain_kernel(
    dims,
    inputs,
    out_grad,
    shifts,
    flips,
    gain1,
    bias1,
    weight1,
    gain2,
    bias2,
    weight2,
    gain3,
    bias3,
    weight3,
    taps_out,
    grad_out,
    result_out,
    summed_out,
    back_out,
    gain1_out,
    bias1_out,
    gain2_out,
    bias2_out,
    gain3_out,
    bias3_out,
    window,
    placed,
    act,
    taps,
    w1,
    w2,
    w3,
    even,
    odd,
    share,
    pooled,
    edges,
    edges_in,
    second,
    narrow,
    own_grad,
    far_grad,
    third_in,
    third,
    narrow_grad,
    narrow_taps,
    second_grad,
    block_grad,
    block_send,
    inbox,
    relayed,
    summed,
    wide_grad,
    ours,
    act_grad,
    placed_back,
    final,
    sums,
    plane_buf,
    line_buf,
    local_sem,
    load_sem,
    exchange_send,
    exchange_recv,
    halo_send,
    halo_recv,
    far_send,
    far_recv,
    core_send,
    core_recv,
    *cube_sems,
):
    C, H, L, B, nd, nq = dims
    half = L // 2
    width = C // 2
    tall = half + EDGE
    long = half + 2 * EDGE
    place = Place(nd, nq)
    s, q = place.s, place.q
    blocks = inbox.shape[0]
    cube = Cube(place, blocks, s * blocks, (block_grad, inbox, relayed, summed, summed_out) + cube_sems)
    for i in range(blocks):
        cube.sources[i] = block_send.at[(1 - s) * blocks + i]
    place.greet(place.plane() + place.line() + [place.partner])
    flip = [flips[s * B + b] for b in range(B)]
    shift = [shifts[s * B + b] for b in range(B)]
    block_at = [flip[b] * (nq - 1 - q) + (1 - flip[b]) * q for b in range(B)]

    load = [
        pltpu.make_async_copy(
            inputs.at[s * B + b], window.at[b, EDGE : EDGE + L], load_sem.at[b]
        )
        for b in range(B)
    ]
    load_w1 = pltpu.make_async_copy(weight1, w1, local_sem.at[0])
    load_w2 = pltpu.make_async_copy(weight2, w2, local_sem.at[1])
    load_w3 = pltpu.make_async_copy(weight3, w3, local_sem.at[2])
    load_grad = pltpu.make_async_copy(out_grad.at[pl.ds(s * B, B)], own_grad, local_sem.at[3])

    def pair(number, b, to_next, to_prev, from_prev, from_next):
        return [
            remote(
                to_next,
                from_prev,
                halo_send.at[number, b, 0],
                halo_recv.at[number, b, 0],
                (s, place.d, place.next),
            ),
            remote(
                to_prev,
                from_next,
                halo_send.at[number, b, 1],
                halo_recv.at[number, b, 1],
                (s, place.d, place.prev),
            ),
        ]

    rings = [
        pair(
            4,
            b,
            inputs.at[s * B + b, L - EDGE : L],
            inputs.at[s * B + b, 0:EDGE],
            window.at[b, 0:EDGE],
            window.at[b, EDGE + L : 2 * EDGE + L],
        )
        for b in range(B)
    ]
    for b in range(B):
        load[b].start()
        for copy in rings[b]:
            copy.start()
    for copy in (load_w1, load_w2, load_w3, load_grad):
        copy.start()

    quarter = half // 4
    mirrored = [
        [
            remote(
                out_grad.at[s * B + b, i * quarter : (i + 1) * quarter],
                far_grad.at[b, i * quarter : (i + 1) * quarter],
                far_send.at[b, i],
                far_recv.at[b, i],
                (s, place.d, place.mirror),
            )
            for i in range(4)
        ]
        for b in range(B)
    ]
    letters = [copy for copies in mirrored for copy in copies]

    def post(count):
        for copy in letters[:count]:
            copy.start()
        del letters[:count]

    def send_edges(number, b, first, last, size, wrap=False):
        turned = flip[b] == 1
        for at, (head, tail) in enumerate(zip(first, last)):
            head, tail = head.astype(F32), tail.astype(F32)
            edges[number, 0, b, at, :, 0:size] = jnp.where(turned, head, tail).astype(BF16)
            edges[number, 1, b, at, :, 0:size] = jnp.where(turned, tail, head).astype(BF16)
        n = len(first)
        copies = pair(
            number,
            b,
            edges.at[number, 0, b, 0:n, :, 0:size],
            edges.at[number, 1, b, 0:n, :, 0:size],
            edges_in.at[number, 0, b, 0:n, :, 0:size],
            edges_in.at[number, 1, b, 0:n, :, 0:size],
        )
        for copy in copies:
            copy.start()
        return copies

    def take_edges(number, b, at, size, wrap=False):
        from_prev = edges_in[number, 0, b, at, :, 0:size].astype(F32)
        from_next = edges_in[number, 1, b, at, :, 0:size].astype(F32)
        turned = flip[b] == 1
        before = jnp.where(turned, from_next, from_prev)
        after = jnp.where(turned, from_prev, from_next)
        if not wrap:
            before = jnp.where(block_at[b] > 0, before, 0.0)
            after = jnp.where(block_at[b] < nq - 1, after, 0.0)
        return before.astype(BF16), after.astype(BF16)

    def moments(read, count, size):
        none = jnp.zeros((8, size), F32)
        total = chunks(count, lambda r, t: t + jnp.sum(halves(read(r)), axis=0), none, 2)
        mean = row_sum(total) * (1.0 / count)
        mean8 = eight(mean)

        def deviations(r, t):
            away = halves(read(r)) - mean8[None]
            return t + jnp.sum(away * away, axis=0)

        return [mean, row_sum(chunks(count, deviations, none, 2))]

    def norm_of(step, count, gain, bias):
        mean, square = step.finish(join_moments(float(count * nd)))
        return Norm(mean, lax.rsqrt(square * (1.0 / (count * nd * nq)) + EPSILON), gain, bias)

    def gradients(norm, back, count):
        scale = 1.0 / (count * nd * nq)
        bias_mean, gain_mean = eight(back[0] * scale), eight(back[1] * scale)
        factor = norm.gain * norm.inv

        def value(grad, normed):
            return factor[None] * (grad - bias_mean[None] - normed * gain_mean[None])

        return value

    def tally(row, b, back):
        for at, total in ((row, back[1]), (row + 1, back[0])):
            to = sums.at[0, at : at + 1, 0 : total.shape[1]]
            if b == 0:
                to[...] = total
            else:
                to[...] = to[...] + total

    def gather(b, first, value):
        at = slice(first // BLOCK, (first + value.shape[0]) // BLOCK)
        value = value.reshape(value.shape[0] // BLOCK, BLOCK, width)
        if b > 0:
            value = value + block_grad[at]
        block_grad[at] = value
        if b == B - 1:
            block_send[at] = value.astype(BF16)

    saved = []

    def save(src, dst, sem):
        copy = pltpu.make_async_copy(src, dst, sem)
        copy.start()
        saved.append(copy)
        return copy

    zero = jnp.zeros((8, C), F32)
    none = jnp.zeros((8, H), F32)
    tap_saves = [None] * B
    swap = remote(sums.at[0], sums.at[1], core_send.at[B], core_recv.at[B], place.partner)
    last = []

    def chain(b):
        low, high = b * half, (b + 1) * half
        turned = flip[b] == 1

        def exchange(number):
            return Exchange(
                place,
                b * 6 + number,
                b * 2 + number % 2,
                plane_buf,
                line_buf,
                exchange_send,
                exchange_recv,
            )

        load[b].wait()
        step = exchange(0)
        step.start(moments(lambda r: window[b, pl.ds(EDGE + r, EDGE)].astype(F32), L, C))
        yield
        for copy in rings[b]:
            copy.wait()
        for parity in range(2):
            shape = (tall, L + 2 * EDGE)
            at = 2 * (lax.broadcasted_iota(jnp.int32, shape, 0) - 8) + parity
            source = flip[b] * (L - 1) + (1 - 2 * flip[b]) * at - shift[b] + EDGE
            pick = jnp.where(lax.broadcasted_iota(jnp.int32, shape, 1) == source, 1.0, 0.0)
            placed[b, parity] = jnp.dot(
                pick.astype(BF16), window[b, 0 : L + 2 * EDGE], preferred_element_type=F32
            ).astype(BF16)
        step.relay(join_moments(float(L)))
        post(2)
        yield
        norm1 = norm_of(step, L, gain1, bias1)
        for parity in range(2):

            def activate(r, c):
                block = halves(placed[b, parity, pl.ds(r, EDGE)].astype(F32))
                value = flat(gelu(norm1.pre(norm1.normed(block))))
                at = lax.broadcasted_iota(jnp.int32, value.shape, 0) + (r - 8)
                at = 2 * at + (parity + block_at[b] * L)
                act[pl.ds(r, EDGE)] = jnp.where((at >= 0) & (at < nq * L), value, 0.0)
                return c

            chunks(tall, activate)

            def spread(r, c):
                values = act[pl.ds(r, 2 * EDGE)]
                for off in range(3):
                    at = (2 * off + parity) * C
                    taps[pl.ds(low + r, EDGE), at : at + C] = values[
                        7 + off : 7 + off + EDGE
                    ].astype(BF16)
                return c

            chunks(half, spread)
        tap_saves[b] = save(taps.at[low:high], taps_out.at[low:high], load_sem.at[B + b])
        yield
        if b == 0:
            load_w1.wait()
        tile = even.shape[1]

        def convolve(j, c):
            cols = pl.ds(pl.multiple_of(j * tile, tile), tile)
            even[...] = jnp.dot(
                taps[low:high, 0 : 5 * C], w1[:, cols], preferred_element_type=F32
            )
            odd[...] = jnp.dot(
                taps[low:high, C : 6 * C], w1[:, cols], preferred_element_type=F32
            )

            def pool(r, c):
                at = pl.ds(r, EDGE)
                left, right = even[at, :], odd[at, :]
                away = left - right
                small = jnp.exp(-jnp.abs(away))
                pooled[b, pl.ds(EDGE + r, EDGE), cols] = (
                    jnp.maximum(left, right) + jnp.log(1.0 + small)
                ).astype(BF16)
                part = 1.0 / (1.0 + small)
                share[pl.ds(low + r, EDGE), cols] = jnp.where(away >= 0, part, small * part)
                return c

            chunks(half, pool, 0, 2)
            return c

        lax.fori_loop(0, C // tile, convolve, 0)
        step = exchange(1)
        step.start(moments(lambda r: pooled[b, pl.ds(EDGE + r, EDGE)].astype(F32), half, C))
        ring = send_edges(
            0, b, [pooled[b, EDGE : 2 * EDGE]], [pooled[b, half : half + EDGE]], C
        )
        yield
        step.relay(join_moments(float(half)))
        post(2)
        yield
        norm2 = norm_of(step, half, gain2, bias2)
        for copy in ring:
            copy.wait()
        pooled[b, 0:EDGE], pooled[b, EDGE + half : long] = take_edges(0, b, 0, C)

        def activate(r, c):
            block = halves(pooled[b, pl.ds(r, EDGE)].astype(F32))
            value = flat(gelu(norm2.pre(norm2.normed(block))))
            at = lax.broadcasted_iota(jnp.int32, value.shape, 0) + (r - EDGE + block_at[b] * half)
            act[pl.ds(r, EDGE)] = jnp.where((at >= 0) & (at < nq * half), value, 0.0)
            return c

        chunks(long, activate)

        def spread(r, c):
            values = act[pl.ds(r, 3 * EDGE)]
            for k in range(3):
                at = EDGE + (k - 1) * DILATION_SIZE
                second[pl.ds(low + r, EDGE), k * C : (k + 1) * C] = values[
                    at : at + EDGE
                ].astype(BF16)
            return c

        chunks(half, spread)
        if b == 0:
            load_w2.wait()
        narrow[low:high] = jnp.dot(second[low:high], w2[...], preferred_element_type=F32)
        step = exchange(2)
        step.start(moments(lambda r: narrow[pl.ds(low + r, EDGE)], half, H))
        yield
        step.relay(join_moments(float(half)))
        if b == 0:
            load_w3.wait()
            load_grad.wait()
        for copy in mirrored[b]:
            copy.wait()

        def choose(r, c):
            at = pl.ds(r, EDGE)
            own_grad[b, at] = jnp.where(
                turned, far_grad[b, at].astype(F32), own_grad[b, at].astype(F32)
            ).astype(BF16)
            return c

        chunks(half, choose)
        third_in[low:high] = lax.dot_general(
            own_grad[b], w3[...], NT, preferred_element_type=F32
        )
        yield
        norm3 = norm_of(step, half, gain3, bias3)

        def activate(r, carry):
            at = pl.ds(low + r, EDGE)
            normed = norm3.normed(halves(narrow[at]))
            pre = norm3.pre(normed)
            third[at] = flat(gelu(pre)).astype(BF16)
            grad = halves(third_in[at]) * gelu_slope(pre)
            third_in[at] = flat(grad)
            return carry[0] + jnp.sum(grad, axis=0), carry[1] + jnp.sum(grad * normed, axis=0)

        step = exchange(3)
        step.start([row_sum(t) for t in chunks(half, activate, (none, none))])
        for side in range(2):
            cols = slice(side * width, (side + 1) * width)
            ours[side, b] = (
                pooled[b, EDGE : EDGE + half, cols].astype(F32)
                + jnp.dot(third[low:high], w3[:, cols], preferred_element_type=F32)
            ).astype(BF16)
        if b == B - 1:
            save(ours, result_out, local_sem.at[4])
        yield
        step.relay(join_sums)
        value = lax.dot_general(third[low:high], own_grad[b], TN, preferred_element_type=F32)
        gather(b, 3 * C, jnp.concatenate([value[:, 0:width], value[:, width:]], axis=0))
        yield
        back = step.finish(join_sums)
        tally(4, b, back)
        gradient = gradients(norm3, back, half)

        def input_grad(r, c):
            at = pl.ds(low + r, EDGE)
            value = gradient(halves(third_in[at]), norm3.normed(halves(narrow[at])))
            narrow_grad[b, pl.ds(EDGE + r, EDGE)] = flat(value).astype(BF16)
            return c

        chunks(half, input_grad)
        ring = send_edges(
            1, b, [narrow_grad[b, EDGE : 2 * EDGE]], [narrow_grad[b, half : half + EDGE]], H
        )
        for k in range(3):
            gather(
                b,
                k * C,
                lax.dot_general(
                    second[low:high, k * C : (k + 1) * C],
                    narrow_grad[b, EDGE : EDGE + half],
                    TN,
                    preferred_element_type=F32,
                ),
            )
        yield
        for copy in ring:
            copy.wait()
        narrow_grad[b, 0:EDGE], narrow_grad[b, EDGE + half : long] = take_edges(1, b, 0, H)

        def spread(r, c):
            values = narrow_grad[b, pl.ds(r, 3 * EDGE)].astype(F32)
            for k in range(3):
                at = EDGE - (k - 1) * DILATION_SIZE
                narrow_taps[pl.ds(low + r, EDGE), k * H : (k + 1) * H] = values[
                    at : at + EDGE
                ].astype(BF16)
            return c

        chunks(half, spread)
        second_grad[low:high] = sum(
            lax.dot_general(
                narrow_taps[low:high, k * H : (k + 1) * H],
                w2[k * C : (k + 1) * C],
                NT,
                preferred_element_type=F32,
            )
            for k in range(3)
        )

        def slope(r, carry):
            at = pl.ds(low + r, EDGE)
            normed = norm2.normed(halves(pooled[b, pl.ds(EDGE + r, EDGE)].astype(F32)))
            grad = halves(second_grad[at]) * gelu_slope(norm2.pre(normed))
            second_grad[at] = flat(grad)
            return carry[0] + jnp.sum(grad, axis=0), carry[1] + jnp.sum(grad * normed, axis=0)

        step = exchange(4)
        step.start([row_sum(t) for t in chunks(half, slope, (zero, zero))])
        yield
        step.relay(join_sums)
        yield
        back = step.finish(join_sums)
        tally(2, b, back)
        gradient = gradients(norm2, back, half)

        def unpool(r, c):
            at = pl.ds(low + r, EDGE)
            normed = norm2.normed(halves(pooled[b, pl.ds(EDGE + r, EDGE)].astype(F32)))
            value = flat(gradient(halves(second_grad[at]), normed))
            value = value + own_grad[b, pl.ds(r, EDGE)].astype(F32)
            value = value.astype(BF16).astype(F32)
            part = share[at]
            wide_grad[0, at] = (value * part).astype(BF16)
            wide_grad[1, at] = (value * (1.0 - part)).astype(BF16)
            return c

        chunks(half, unpool)
        ring = send_edges(
            2,
            b,
            [wide_grad[p, low : low + EDGE] for p in range(2)],
            [wide_grad[p, high - EDGE : high] for p in range(2)],
            C,
        )
        if b == B - 1:
            save(wide_grad, grad_out, local_sem.at[5])
        tap_saves[b].wait()
        saved.remove(tap_saves[b])

        def put(parity, r, values):
            for at in range(3):
                lanes = (1 - parity + 2 * at) * C
                taps[pl.ds(low + r, EDGE), lanes : lanes + C] = values[
                    EDGE + 1 - at : 2 * EDGE + 1 - at
                ].astype(BF16)

        for parity in range(2):

            def spread(i, c):
                r = pl.multiple_of(i * EDGE, EDGE)
                values = wide_grad[parity, pl.ds(low + r - EDGE, 3 * EDGE)].astype(F32)
                put(parity, r, values)
                return c

            lax.fori_loop(1, half // EDGE - 1, spread, 0)
        yield
        for copy in ring:
            copy.wait()
        for parity in range(2):
            before, after = take_edges(2, b, parity, C)
            put(
                parity,
                0,
                jnp.concatenate([before, wide_grad[parity, low : low + 2 * EDGE]], axis=0).astype(F32),
            )
            put(
                parity,
                half - EDGE,
                jnp.concatenate([wide_grad[parity, high - 2 * EDGE : high], after], axis=0).astype(F32),
            )
        carry = (zero, zero)
        for parity in range(2):
            if parity == 1:
                yield

            def convolve(j, c):
                at = pl.multiple_of(j * BLOCK, BLOCK)
                part = None
                for k in range(5):
                    lanes = (k + 1 - parity) * C
                    more = lax.dot_general(
                        taps[low:high, lanes : lanes + C],
                        w1[pl.ds(k * C + at, BLOCK), :],
                        NT,
                        preferred_element_type=F32,
                    )
                    part = more if part is None else part + more
                act_grad[parity, low:high, pl.ds(at, BLOCK)] = part
                return c

            lax.fori_loop(0, C // BLOCK, convolve, 0)

            def slope(r, carry):
                at = pl.ds(low + r, EDGE)
                values = placed[b, parity, pl.ds(r, 2 * EDGE)].astype(F32)[8 : 8 + EDGE]
                normed = norm1.normed(halves(values))
                grad = halves(act_grad[parity, at]) * gelu_slope(norm1.pre(normed))
                act_grad[parity, at] = flat(grad)
                return carry[0] + jnp.sum(grad, axis=0), carry[1] + jnp.sum(grad * normed, axis=0)

            carry = chunks(half, slope, carry)
        step = exchange(5)
        step.start([row_sum(t) for t in carry])
        yield
        step.relay(join_sums)
        yield
        back = step.finish(join_sums)
        tally(0, b, back)
        if b == B - 1:
            swap.start()
        gradient = gradients(norm1, back, L)
        for parity in range(2):

            def input_grad(r, c):
                values = placed[b, parity, pl.ds(r, 2 * EDGE)].astype(F32)[8 : 8 + EDGE]
                value = gradient(
                    halves(act_grad[parity, pl.ds(low + r, EDGE)]), norm1.normed(halves(values))
                )
                window[b, pl.ds(parity * long + EDGE + r, EDGE)] = flat(value).astype(BF16)
                return c

            chunks(half, input_grad)
        starts = [parity * long for parity in range(2)]
        ring = send_edges(
            3,
            b,
            [window[b, at + EDGE : at + 2 * EDGE] for at in starts],
            [window[b, at + half : at + half + EDGE] for at in starts],
            C,
        )
        yield
        for copy in ring:
            copy.wait()
        for parity, at in enumerate(starts):
            window[b, at : at + EDGE], window[b, at + EDGE + half : at + long] = take_edges(
                3, b, parity, C, True
            )
        shape = (L, 2 * long)
        at = lax.broadcasted_iota(jnp.int32, shape, 0) + shift[b]
        at = flip[b] * (L - 1) + (1 - 2 * flip[b]) * at
        source = (at & 1) * long + (at >> 1) + EDGE
        pick = jnp.where(lax.broadcasted_iota(jnp.int32, shape, 1) == source, 1.0, 0.0)
        pick = pick.astype(BF16)
        for side in range(2):
            cols = slice(side * width, (side + 1) * width)
            placed_back[side, b] = jnp.dot(
                pick, window[b, :, cols], preferred_element_type=F32
            ).astype(BF16)
        across = remote(
            placed_back.at[1 - s, b], final.at[b], core_send.at[b], core_recv.at[b], place.partner
        )
        across.start()
        save(placed_back.at[s, b], back_out.at[s * B + b], load_sem.at[2 * B + b])
        yield
        across.wait()
        save(final.at[b], back_out.at[(1 - s) * B + b], load_sem.at[3 * B + b])

    def adding():
        for stage in range(len(cube.events())):
            for block in range(blocks):
                cube.run(block, stage)
                if block % 3 == 2:
                    yield

    run_chains(chain, adding, B)
    cube.end()
    swap.wait()
    outs = (gain1_out, bias1_out, gain2_out, bias2_out, gain3_out, bias3_out)
    for i, to in enumerate(outs):
        count = to.shape[0]
        row = sums[0, i : i + 1, 0:count] + sums[1, i : i + 1, 0:count]
        to[...] = row.reshape(count)
    for copy in saved:
        copy.wait()


GRADS_STEP = 10


def run_chains(chain, adding, count):
    chains = [chain(b) for b in range(count)]
    taken = [0] * count
    extra = None

    def advance(b):
        taken[b] += 1
        return next(chains[b], "end") != "end"

    for b in range(count):
        advance(b)
    for b in range(count):
        advance(b)
    advance(0)
    live = list(range(count))
    while live:
        for b in list(live):
            if not advance(b):
                live.remove(b)
            if extra is None and taken[-1] >= GRADS_STEP:
                extra = adding()
            if extra is not None:
                next(extra, None)
    if extra is not None:
        for _ in extra:
            pass


class Cube:
    def __init__(self, place, blocks, base, refs):
        self.place, self.blocks, self.base = place, blocks, base
        self.total, self.inbox, self.relayed, self.summed, self.out = refs[:5]
        self.send_sem, self.core_recv, self.down_recv, self.up_recv, self.share_recv = refs[5:]
        self.sources = [None] * blocks
        self.axes = cube_axes(place)
        self.planar = place.nd.bit_length() - 1
        self.flight = [None] * blocks
        self.state = [None] * blocks

    def order(self, block):
        return [self.axes[i] for i in cube_order(block, self.planar, len(self.axes))]

    def events(self):
        depth = len(self.axes)
        return ["core"] + ["down"] * depth + ["up"] * halvings(depth) + ["share", "out"]

    def _add(self, block, incoming, first, count, send):
        total, inbox = self.total, self.inbox

        step = min(count, 4 * EDGE)
        for r in range(0, count, step):
            at = pl.ds(pl.multiple_of(first + r, EDGE), step)
            value = total[self.base + block, at] + incoming(r, step).astype(F32)
            total[self.base + block, at] = value
            if send:
                inbox[block, at] = value.astype(BF16)

    def run(self, block, stage):
        place, depth = self.place, len(self.axes)
        s = place.s
        last = depth + halvings(depth)
        if self.flight[block] is not None:
            self.flight[block].wait()
        if stage == 0:
            copy = remote(
                self.sources[block],
                self.inbox.at[block],
                self.send_sem.at[block],
                self.core_recv.at[block],
                place.partner,
            )
        elif stage <= depth:
            k = stage - 1
            partner, side = self.order(block)[k]
            size, first, past = sizes(k), [0], None
            if k > 0:
                first, past = self.state[block]
            offset = first[-1]
            if k == 0:
                incoming = lambda base: lambda r, n: self.inbox[
                    block, pl.ds(pl.multiple_of(base + r, EDGE), n)
                ]
                base_of = lambda at: at
            else:
                incoming = lambda base: lambda r, n: self.relayed[
                    block, pl.ds(pl.multiple_of(base + r, EDGE), n)
                ]
                base_of = lambda at: at - offset + region(k - 1)
            if size >= 2 * EDGE:
                small = size // 2
                give, hold = offset + (1 - side) * small, offset + side * small
                self._add(block, incoming(base_of(give)), give, small, True)
            else:
                small, give, hold = size, offset, offset
                self._add(block, incoming(base_of(give)), give, small, True)
                at = pl.ds(pl.multiple_of(give, EDGE), small)
                self.total[self.base + block, at] = self.inbox[block, at].astype(F32)
            copy = remote(
                self.inbox.at[block, pl.ds(pl.multiple_of(give, EDGE), small)],
                self.relayed.at[block, region(k) : region(k) + small],
                self.send_sem.at[block],
                self.down_recv.at[block, k],
                partner,
            )
            self.state[block] = (first + [hold], past)
        elif stage <= last:
            k = last - stage
            first, _ = self.state[block]
            partner, _ = self.order(block)[k]
            hold, small = first[k + 1], sizes(k + 1)
            at = pl.ds(pl.multiple_of(hold, EDGE), small)
            if stage == depth + 1:
                end = pl.ds(pl.multiple_of(first[-1], EDGE), sizes(depth))
                begin = region(depth - 1)
                self.summed[s, block, end] = (
                    self.total[self.base + block, end]
                    + self.relayed[block, begin : begin + sizes(depth)].astype(F32)
                ).astype(BF16)
            copy = remote(
                self.summed.at[s, block, at],
                self.summed.at[s, block, at],
                self.send_sem.at[block],
                self.up_recv.at[block, k],
                partner,
            )
        elif stage == last + 1:
            copy = remote(
                self.summed.at[s, block],
                self.summed.at[s, block],
                self.send_sem.at[block],
                self.share_recv.at[block],
                place.partner,
            )
        else:
            copy = pltpu.make_async_copy(
                self.summed.at[:, block], self.out.at[:, block], self.send_sem.at[block]
            )
        if stage > 0 and stage <= depth:
            copy.start()
            if size >= 2 * EDGE:
                self._add(block, incoming(base_of(hold)), hold, small, False)
        else:
            copy.start()
        self.flight[block] = copy

    def end(self):
        for copy in self.flight:
            copy.wait()


BLOCK = 256


def sizes(k):
    return max(BLOCK >> k, EDGE)


def region(k):
    return sum(sizes(i + 1) for i in range(k))


def halvings(depth):
    return sum(sizes(k) >= 2 * EDGE for k in range(depth))


def cube_axes(place):
    axes = []
    bit = 1
    while bit < place.nd:
        side = lax.rem(place.d // bit, 2)
        axes.append(((place.s, place.d + bit * (1 - 2 * side), place.q), side))
        bit *= 2
    bit = 1
    while bit < place.nq:
        side = lax.rem(place.q // bit, 2)
        axes.append(((place.s, place.d, place.q + bit * (1 - 2 * side)), side))
        bit *= 2
    return axes


def cube_order(block, planar, depth):
    order = [(block + i) % planar for i in range(planar)] + list(range(planar, depth))
    if block % 8 == 7:
        order.remove(planar)
        order = [planar] + order
    return order


def plan(planar, depth, blocks, pieces, events):
    rate, cost = 80e3, 0.1
    free = [0.0] * (depth + 1)
    ready = {}
    now, order, done = 0.0, [], 0.0
    pieces = list(pieces)

    def send(axis, size):
        if axis == depth:
            loads, speed, wait = [(depth, 1)], 6 * rate, 0.8
        elif axis > planar:
            loads, speed, wait = [(planar, 1), (axis, 2)], rate, 3.4
        else:
            loads, speed, wait = [(axis, 1)], rate, 2.8
        begin = max([now] + [free[i] for i, _ in loads])
        for i, times in loads:
            free[i] = begin + times * size / speed
        return max(free[i] for i, _ in loads) + wait

    while pieces or ready:
        able = sorted((t, b) for b, (t, _) in ready.items() if t <= now)
        if able:
            _, block = able[0]
            _, stage = ready.pop(block)
            order.append((block, stage))
            kind = events[stage]
            now += cost if kind == "down" else 0.05
            if stage + 1 < len(events):
                axes = cube_order(block, planar, depth)
                if kind in ("core", "share"):
                    axis, size = depth, BLOCK
                elif kind == "down":
                    axis, size = axes[stage - 1], sizes(stage)
                elif kind == "up":
                    k = depth + halvings(depth) - stage
                    axis, size = axes[k], sizes(k + 1)
                else:
                    axis, size = depth, 0
                ready[block] = (send(axis, 2 * size * 768), stage + 1)
        elif pieces and done + pieces[0][4] <= now:
            name, time, made, sends, _ = pieces.pop(0)
            order.append(name)
            now += time
            done = now
            for block in made:
                ready[block] = (now, 0)
            for axis, size in sends:
                send(axis, size)
        else:
            now = min([t for t, _ in ready.values()] + [done + p[4] for p in pieces[:1]])
    return order


def sum_kernel(
    dims,
    taps_in,
    grad_in,
    result_in,
    summed_out,
    near_out,
    far_out,
    total,
    inbox,
    sending,
    relayed,
    summed,
    product,
    taps,
    grads,
    load_sem,
    result_send,
    result_recv,
    *cube_sems,
):
    C, H, L, B, nd, nq = dims
    half = L // 2
    width = C // 2
    place = Place(nd, nq)
    s = place.s
    cross = (1 - s, place.d, place.mirror)
    mine = pl.ds(s * B, B)
    per_tap = C // BLOCK
    blocks = 5 * per_tap
    cube = Cube(place, blocks, 0, (total, inbox, relayed, summed, summed_out) + cube_sems)
    depth = len(cube.axes)
    load_grads = pltpu.make_async_copy(grad_in, grads, load_sem.at[6])
    load_taps = [
        pltpu.make_async_copy(
            taps_in.at[:, i * C : (i + 1) * C], taps.at[:, i * C : (i + 1) * C], load_sem.at[i]
        )
        for i in range(6)
    ]
    for copy in [load_grads] + load_taps:
        copy.start()
    place.greet(place.plane() + place.line() + [place.partner, cross])
    for i in range(blocks):
        cube.sources[i] = sending.at[i]
    todo, pieces = {}, []

    def piece(name, time, made=(), sends=(), after=0.0):
        def keep(body):
            todo[name] = body
            pieces.append((name, time, made, sends, after))
            return body

        return keep

    across = remote(
        result_in.at[1 - s], near_out, result_send.at[0], result_recv.at[0], place.partner
    )
    away = [
        remote(
            result_in.at[side, b],
            far_out.at[s * B + b],
            result_send.at[1 + 2 * b + i],
            result_recv.at[1 + 2 * b + i],
            (side, place.d, place.mirror),
        )
        for b in range(B)
        for i, side in enumerate((s, 1 - s))
    ]
    across.start()

    def result_piece(i, after):
        @piece(("result", i), 0.05, (), [(depth - 1, 4 * half * width)], after)
        def _():
            away[i].start()

    def weight_piece(k):
        @piece(("weight", k), WEIGHT_TIME, range(k * per_tap, (k + 1) * per_tap))
        def _():
            if k == 0:
                load_grads.wait()
                load_taps[0].wait()
            load_taps[k + 1].wait()

            def tile(m, c):
                lanes = pl.multiple_of(k * C + m * BLOCK, BLOCK)
                product[...] = lax.dot_general(
                    taps[:, pl.ds(lanes, BLOCK)], grads[0], TN, preferred_element_type=F32
                ) + lax.dot_general(
                    taps[:, pl.ds(lanes + C, BLOCK)], grads[1], TN, preferred_element_type=F32
                )

                def split(r, c):
                    at = pl.ds(r, EDGE)
                    low = pl.ds(pl.multiple_of(s * width, width), width)
                    high = pl.ds(pl.multiple_of((1 - s) * width, width), width)
                    total[k * per_tap + m, at] = product[at, low]
                    sending[k * per_tap + m, at] = product[at, high].astype(BF16)
                    return c

                chunks(BLOCK, split)
                return c

            lax.fori_loop(0, per_tap, tile, 0)

    early = len(away) // 2
    for k in range(5):
        weight_piece(k)
        if k < early:
            result_piece(k, 0.0)
    for i in range(early, len(away)):
        result_piece(i, LATE if i == early else 0.0)
    for item in plan(cube.planar, depth, blocks, pieces, cube.events()):
        if item in todo:
            todo[item]()
        else:
            cube.run(*item)
    cube.end()
    across.wait()
    for copy in away:
        copy.wait()


WEIGHT_TIME = 5.0
LATE = 45.0


def finish_kernel(
    dims,
    first,
    later,
    mine,
    near,
    far,
    back,
    flips,
    *refs,
):
    vectors, outs, rest = refs[:6], refs[6:17], refs[17:]
    for src, dst in zip(vectors, outs[5:]):
        dst[...] = src[...]
    finish(dims, first, later, mine, near, far, back, flips, *outs[:5], *rest)


def finish(
    dims,
    first,
    later,
    mine,
    near,
    far,
    back,
    flips,
    conv1,
    conv2,
    conv3,
    result,
    back_out,
    held,
    wide,
    narrow,
    near_buf,
    far_buf,
    back_buf,
    in_sem,
    wide_sem,
    narrow_sem,
    side_sem,
):
    C, H, L, B, nd, nq = dims
    s = lax.axis_index("section")
    first_blocks = first.shape[1]
    blocks = first_blocks + later.shape[1]
    width = C // 2
    slots = wide.shape[0]

    def summed(block):
        return first.at[:, block] if block < first_blocks else later.at[:, block - first_blocks]

    order = list(range(first_blocks, blocks)) + list(range(first_blocks))
    loads = {
        block: pltpu.make_async_copy(summed(block), held.at[block], in_sem.at[block])
        for block in order
    }
    sides = [
        pltpu.make_async_copy(mine.at[s], near_buf.at[pl.ds(s * B, B)], side_sem.at[0]),
        pltpu.make_async_copy(near, near_buf.at[pl.ds((1 - s) * B, B)], side_sem.at[1]),
        pltpu.make_async_copy(far, far_buf, side_sem.at[2]),
        pltpu.make_async_copy(back, back_buf, side_sem.at[3]),
    ]
    for block in order[:4]:
        loads[block].start()
    for copy in sides:
        copy.start()
    for block in order[4:]:
        loads[block].start()
    bottom = 3 * C

    def targets(block, side):
        row = side * first_blocks * BLOCK + block * BLOCK
        if row < bottom:
            return [(0, BLOCK, conv2.at[row : row + BLOCK])]
        parts, at = [], 0
        while at < BLOCK:
            which, begin = (row - bottom + at) // H, (row - bottom + at) % H
            count = min(BLOCK - at, H - begin)
            cols = slice(which * width, (which + 1) * width)
            parts.append((at, count, conv3.at[begin : begin + count, cols]))
            at += count
        return parts

    going = [[] for _ in range(slots)]
    for i, block in enumerate(order):
        slot = i % slots
        for copy in going[slot]:
            copy.wait()
        loads[block].wait()
        for side in range(2):

            def widen(r, c):
                at = pl.ds(pl.multiple_of(r * 64, 64), 64)
                value = held[block, side, at].astype(F32)
                if block >= first_blocks:
                    wide[slot, at, side * width : (side + 1) * width] = value
                else:
                    narrow[slot, side, at] = value
                return c

            lax.fori_loop(0, BLOCK // 64, widen, 0)
        if block >= first_blocks:
            row = (block - first_blocks) * BLOCK
            going[slot] = [
                pltpu.make_async_copy(
                    wide.at[slot], conv1.at[row : row + BLOCK], wide_sem.at[slot]
                )
            ]
        else:
            parts = [(side, *part) for side in range(2) for part in targets(block, side)]
            going[slot] = [
                pltpu.make_async_copy(
                    narrow.at[slot, side, at : at + count], to, narrow_sem.at[slot, j]
                )
                for j, (side, at, count, to) in enumerate(parts)
            ]
        for copy in going[slot]:
            copy.start()
        if i == 2:
            sides[3].wait()
            give = pltpu.make_async_copy(back_buf, back_out, side_sem.at[3])
            give.start()
        if i == 4:
            for copy in sides[:3]:
                copy.wait()
            for b in range(2 * B):
                turned = flips[b]

                def deliver(r, c):
                    at = pl.ds(pl.multiple_of(r * 64, 64), 64)
                    near_buf[b, at] = jnp.where(
                        turned == 1, far_buf[b, at].astype(F32), near_buf[b, at].astype(F32)
                    ).astype(BF16)
                    return c

                lax.fori_loop(0, L // 128, deliver, 0)
            hand = pltpu.make_async_copy(near_buf, result, side_sem.at[0])
            hand.start()
    for copies in going:
        for copy in copies:
            copy.wait()
    give.wait()
    hand.wait()


def on_device(
    nd,
    nq,
    inputs,
    shifts,
    flips,
    gain1,
    bias1,
    weight1,
    gain2,
    bias2,
    weight2,
    gain3,
    bias3,
    weight3,
    out_grad,
):
    sequences, L, C = inputs.shape
    H = weight3.shape[0]
    B, half = sequences // 2, L // 2
    rows = B * half
    dims = (C, H, L, B, nd, nq)
    anywhere = pl.BlockSpec(memory_space=pl.ANY)
    vmem = pl.BlockSpec(memory_space=pltpu.VMEM)
    smem = pl.BlockSpec(memory_space=pltpu.SMEM)
    peers = nd - 1 + nq - 1
    shape = jax.ShapeDtypeStruct
    dma = pltpu.SemaphoreType.DMA
    width = C // 2
    side = (3 * C * H + H * C) // width // 2
    first_blocks = side // BLOCK
    later_blocks = 5 * C // BLOCK
    depth = (nd.bit_length() - 1) + (nq.bit_length() - 1)

    def cube_scratch(blocks):
        return [
            dma((blocks,)),
            dma((blocks,)),
            dma((blocks, depth)),
            dma((blocks, halvings(depth))),
            dma((blocks,)),
        ]

    taps, grads, result, first, back, *vectors = pl.pallas_call(
        functools.partial(chain_kernel, dims),
        name="chain",
        out_shape=(
            shape((rows, 6 * C), BF16),
            shape((2, rows, C), BF16),
            shape((2, B, half, width), BF16),
            shape((2, first_blocks, BLOCK, width), BF16),
            shape((2 * B, L, width), BF16),
        )
        + (shape((C,), F32),) * 4
        + (shape((H,), F32),) * 2,
        in_specs=[
            anywhere,
            anywhere,
            smem,
            smem,
            vmem,
            vmem,
            anywhere,
            vmem,
            vmem,
            anywhere,
            vmem,
            vmem,
            anywhere,
        ],
        out_specs=[anywhere] * 5 + [vmem] * 6,
        scratch_shapes=[
            pltpu.VMEM((B, L + 4 * EDGE, C), BF16),
            pltpu.VMEM((B, 2, half + EDGE, C), BF16),
            pltpu.VMEM((half + 2 * EDGE, C), F32),
            pltpu.VMEM((rows, 6 * C), BF16),
            pltpu.VMEM((5 * C, C), BF16),
            pltpu.VMEM((3 * C, H), BF16),
            pltpu.VMEM((H, C), BF16),
            pltpu.VMEM((half, C // 3), F32),
            pltpu.VMEM((half, C // 3), F32),
            pltpu.VMEM((rows, C), F32),
            pltpu.VMEM((B, half + 2 * EDGE, C), BF16),
            pltpu.VMEM((4, 2, B, 2, EDGE, C), BF16),
            pltpu.VMEM((4, 2, B, 2, EDGE, C), BF16),
            pltpu.VMEM((rows, 3 * C), BF16),
            pltpu.VMEM((rows, H), F32),
            pltpu.VMEM((B, half, C), BF16),
            pltpu.VMEM((B, half, C), BF16),
            pltpu.VMEM((rows, H), F32),
            pltpu.VMEM((rows, H), BF16),
            pltpu.VMEM((B, half + 2 * EDGE, H), BF16),
            pltpu.VMEM((rows, 3 * H), BF16),
            pltpu.VMEM((rows, C), F32),
            pltpu.VMEM((2 * first_blocks, BLOCK, width), F32),
            pltpu.VMEM((2 * first_blocks, BLOCK, width), BF16),
            pltpu.VMEM((first_blocks, BLOCK, width), BF16),
            pltpu.VMEM((first_blocks, region(depth), width), BF16),
            pltpu.VMEM((2, first_blocks, BLOCK, width), BF16),
            pltpu.VMEM((2, rows, C), BF16),
            pltpu.VMEM((2, B, half, width), BF16),
            pltpu.VMEM((2, rows, C), F32),
            pltpu.VMEM((2, B, L, width), BF16),
            pltpu.VMEM((B, L, width), BF16),
            pltpu.VMEM((2, 8, C), F32),
            pltpu.VMEM((6 * B, nd, 2, C), F32),
            pltpu.VMEM((6 * B, nq, 2, C), F32),
            dma((6,)),
            dma((4 * B,)),
            dma((2 * B, peers)),
            dma((2 * B, peers)),
            dma((5, B, 2)),
            dma((5, B, 2)),
            dma((B, 4)),
            dma((B, 4)),
            dma((B + 1,)),
            dma((B + 1,)),
        ]
        + cube_scratch(first_blocks),
        compiler_params=pltpu.CompilerParams(
            collective_id=0, has_side_effects=True, vmem_limit_bytes=60 * 2**20
        ),
    )(
        inputs,
        out_grad,
        shifts,
        flips,
        gain1,
        bias1,
        weight1.reshape(5 * C, C),
        gain2,
        bias2,
        weight2.reshape(3 * C, H),
        gain3,
        bias3,
        weight3,
    )
    later, near, far = pl.pallas_call(
        functools.partial(sum_kernel, dims),
        name="weight_sum",
        out_shape=(
            shape((2, later_blocks, BLOCK, width), BF16),
            shape((B, half, width), BF16),
            shape((2 * B, half, width), BF16),
        ),
        in_specs=[anywhere] * 3,
        out_specs=[anywhere] * 3,
        scratch_shapes=[
            pltpu.VMEM((later_blocks, BLOCK, width), F32),
            pltpu.VMEM((later_blocks, BLOCK, width), BF16),
            pltpu.VMEM((later_blocks, BLOCK, width), BF16),
            pltpu.VMEM((later_blocks, region(depth), width), BF16),
            pltpu.VMEM((2, later_blocks, BLOCK, width), BF16),
            pltpu.VMEM((BLOCK, C), F32),
            pltpu.VMEM((rows, 6 * C), BF16),
            pltpu.VMEM((2, rows, C), BF16),
            dma((7,)),
            dma((1 + 2 * B,)),
            dma((1 + 2 * B,)),
        ]
        + cube_scratch(later_blocks),
        compiler_params=pltpu.CompilerParams(
            collective_id=1, has_side_effects=True, vmem_limit_bytes=60 * 2**20
        ),
    )(taps, grads, result)
    blocks = first_blocks + later_blocks
    slots = 6
    conv1, conv2, conv3, result, back, *vectors = pl.pallas_call(
        functools.partial(finish_kernel, dims),
        name="widen",
        out_shape=(
            shape((5 * C, C), F32),
            shape((3 * C, H), F32),
            shape((H, C), F32),
            shape((2 * B, half, width), BF16),
            shape((2 * B, L, width), BF16),
        )
        + (shape((C,), F32),) * 4
        + (shape((H,), F32),) * 2,
        in_specs=[anywhere] * 6 + [smem] + [vmem] * 6,
        out_specs=[anywhere] * 5 + [vmem] * 6,
        scratch_shapes=[
            pltpu.VMEM((blocks, 2, BLOCK, width), BF16),
            pltpu.VMEM((slots, BLOCK, C), F32),
            pltpu.VMEM((slots, 2, BLOCK, width), F32),
            pltpu.VMEM((2 * B, half, width), BF16),
            pltpu.VMEM((2 * B, half, width), BF16),
            pltpu.VMEM((2 * B, L, width), BF16),
            dma((blocks,)),
            dma((slots,)),
            dma((slots, 4)),
            dma((4,)),
        ],
        compiler_params=pltpu.CompilerParams(vmem_limit_bytes=60 * 2**20),
    )(first, later, result, near, far, back, flips, *vectors)
    return (
        result,
        back,
        conv1.reshape(5, C, C),
        vectors[0],
        vectors[1],
        conv2.reshape(3, C, H),
        vectors[2],
        vectors[3],
        conv3,
        vectors[4],
        vectors[5],
    )


def solution(mesh):
    whole = P()
    split = P("dp", "seq", None)
    return jax.shard_map(
        functools.partial(on_device, mesh.shape["dp"], mesh.shape["seq"]),
        mesh=mesh,
        in_specs=(split, P("dp"), P("dp")) + (whole,) * 9 + (split,),
        out_specs=(P("dp", "seq", "section"),) * 2 + (whole,) * 9,
        check_vma=False,
    )
```

```python
import functools

import jax
import jax.numpy as jnp
from jax import lax
from jax.experimental import pallas as pl
from jax.experimental.pallas import tpu as pltpu
from jax.sharding import PartitionSpec as P

DILATION_SIZE = 11
EPSILON = 0.001
EDGE = 16
MESH = pl.DeviceIdType.MESH
F32 = jnp.float32
BF16 = jnp.bfloat16
SCALE = 0.7978845608028654
CUBIC = 0.044715
TN = (((0,), (0,)), ((), ()))
NT = (((1,), (1,)), ((), ()))


def gelu(u):
    return 0.5 * u * (1.0 + jnp.tanh(SCALE * u * (1.0 + CUBIC * (u * u))))


def gelu_slope(u):
    square = u * u
    t = jnp.tanh(SCALE * u * (1.0 + CUBIC * square))
    return 0.5 * (1.0 + t) + (0.5 * SCALE) * u * (1.0 - t * t) * (1.0 + (3.0 * CUBIC) * square)


def chunks(count, body, carry=0, unroll=2):
    def step(i, carry):
        return body(pl.multiple_of(i * EDGE, EDGE), carry)

    return lax.fori_loop(0, count // EDGE, step, carry, unroll=unroll)


def eight(row):
    return jnp.broadcast_to(row, (8, row.shape[-1]))


def halves(block):
    return block.reshape(block.shape[0] // 8, 8, block.shape[1])


def flat(block):
    return block.reshape(block.shape[0] * 8, block.shape[2])


def row_sum(block):
    return jnp.sum(block, axis=0, keepdims=True)


class Place:
    def __init__(self, nd, nq):
        self.nd, self.nq = nd, nq
        self.s, self.d, self.q = (lax.axis_index(a) for a in ("section", "dp", "seq"))
        self.mirror = nq - 1 - self.q
        self.next = lax.rem(self.q + 1, nq)
        self.prev = lax.rem(self.q + nq - 1, nq)
        self.partner = (1 - self.s, self.d, self.q)

    def plane(self):
        return [(self.s, lax.rem(self.d + i, self.nd), self.q) for i in range(1, self.nd)]

    def line(self):
        return [(self.s, self.d, lax.rem(self.q + i, self.nq)) for i in range(1, self.nq)]

    def greet(self, devices):
        barrier = pltpu.get_barrier_semaphore()
        for device in devices:
            pl.semaphore_signal(barrier, inc=1, device_id=device, device_id_type=MESH)
        return lambda: pl.semaphore_wait(barrier, len(devices))


def remote(src, dst, send_sem, recv_sem, device):
    return pltpu.make_async_remote_copy(
        src_ref=src,
        dst_ref=dst,
        send_sem=send_sem,
        recv_sem=recv_sem,
        device_id=device,
        device_id_type=MESH,
    )


class Exchange:
    def __init__(self, place, number, sems, plane_buf, line_buf, send_sem, recv_sem):
        self.place = place
        self.plane_buf, self.line_buf = plane_buf.at[number], line_buf.at[number]
        self.send_sem, self.recv_sem = send_sem.at[sems], recv_sem.at[sems]

    def _start(self, buf, slot, rows, devices, base):
        for at, row in enumerate(rows):
            buf[slot, at : at + 1, 0 : row.shape[1]] = row
        self.copies = [
            remote(
                buf.at[slot],
                buf.at[slot],
                self.send_sem.at[base + i],
                self.recv_sem.at[base + i],
                device,
            )
            for i, device in enumerate(devices)
        ]
        for copy in self.copies:
            copy.start()

    def _finish(self, buf, count, n_rows, width):
        for copy in self.copies:
            copy.wait()
        return [[buf[j, at : at + 1, 0:width] for at in range(n_rows)] for j in range(count)]

    def start(self, rows):
        self.n_rows, self.width = len(rows), rows[0].shape[1]
        self._start(self.plane_buf, self.place.d, rows, self.place.plane(), 0)

    def relay(self, join):
        parts = self._finish(self.plane_buf, self.place.nd, self.n_rows, self.width)
        self._start(
            self.line_buf, self.place.q, join(parts), self.place.line(), self.place.nd - 1
        )

    def finish(self, join):
        return join(self._finish(self.line_buf, self.place.nq, self.n_rows, self.width))


def join_sums(parts):
    totals = parts[0]
    for part in parts[1:]:
        totals = [total + row for total, row in zip(totals, part)]
    return totals


def join_moments(count):
    def join(parts):
        n = len(parts[0]) // 2
        totals = join_sums(parts)
        means = [total * (1.0 / len(parts)) for total in totals[:n]]
        squares = totals[n:]
        for part in parts:
            squares = [
                square + count * (row - mean) * (row - mean)
                for square, row, mean in zip(squares, part[:n], means)
            ]
        return means + squares

    return join


class Norm:
    def __init__(self, mean, inv, gain, bias):
        self.mean, self.inv = eight(mean), eight(inv)
        self.gain, self.bias = (
            eight(vector[...].reshape(1, vector.shape[0])) for vector in (gain, bias)
        )

    def normed(self, block):
        return (block - self.mean[None]) * self.inv[None]

    def pre(self, normed):
        return normed * self.gain[None] + self.bias[None]


def chain_kernel(
    dims,
    inputs,
    out_grad,
    shifts,
    flips,
    gain1,
    bias1,
    weight1,
    gain2,
    bias2,
    weight2,
    gain3,
    bias3,
    weight3,
    taps_out,
    grad_out,
    result_out,
    summed_out,
    back_out,
    gain1_out,
    bias1_out,
    gain2_out,
    bias2_out,
    gain3_out,
    bias3_out,
    window,
    placed,
    act,
    taps,
    w1,
    w2,
    w3,
    even,
    odd,
    share,
    pooled,
    edges,
    edges_in,
    second,
    narrow,
    own_grad,
    far_grad,
    third_in,
    third,
    narrow_grad,
    narrow_taps,
    second_grad,
    block_grad,
    block_send,
    inbox,
    relayed,
    summed,
    wide_grad,
    ours,
    act_grad,
    placed_back,
    final,
    sums,
    plane_buf,
    line_buf,
    local_sem,
    load_sem,
    exchange_send,
    exchange_recv,
    halo_send,
    halo_recv,
    far_send,
    far_recv,
    core_send,
    core_recv,
    *cube_sems,
):
    C, H, L, B, nd, nq = dims
    half = L // 2
    width = C // 2
    tall = half + EDGE
    long = half + 2 * EDGE
    place = Place(nd, nq)
    s, q = place.s, place.q
    blocks = inbox.shape[0]
    cube = Cube(place, blocks, s * blocks, (block_grad, inbox, relayed, summed, summed_out) + cube_sems)
    for i in range(blocks):
        cube.sources[i] = block_send.at[(1 - s) * blocks + i]
    place.greet(place.plane() + place.line() + [place.partner])()
    flip = [flips[s * B + b] for b in range(B)]
    shift = [shifts[s * B + b] for b in range(B)]
    block_at = [flip[b] * (nq - 1 - q) + (1 - flip[b]) * q for b in range(B)]

    load = [
        pltpu.make_async_copy(
            inputs.at[s * B + b], window.at[b, EDGE : EDGE + L], load_sem.at[b]
        )
        for b in range(B)
    ]
    load_w1 = pltpu.make_async_copy(weight1, w1, local_sem.at[0])
    load_w2 = pltpu.make_async_copy(weight2, w2, local_sem.at[1])
    load_w3 = pltpu.make_async_copy(weight3, w3, local_sem.at[2])
    load_grad = pltpu.make_async_copy(out_grad.at[pl.ds(s * B, B)], own_grad, local_sem.at[3])

    def pair(number, b, to_next, to_prev, from_prev, from_next):
        return [
            remote(
                to_next,
                from_prev,
                halo_send.at[number, b, 0],
                halo_recv.at[number, b, 0],
                (s, place.d, place.next),
            ),
            remote(
                to_prev,
                from_next,
                halo_send.at[number, b, 1],
                halo_recv.at[number, b, 1],
                (s, place.d, place.prev),
            ),
        ]

    rings = [
        pair(
            4,
            b,
            inputs.at[s * B + b, L - EDGE : L],
            inputs.at[s * B + b, 0:EDGE],
            window.at[b, 0:EDGE],
            window.at[b, EDGE + L : 2 * EDGE + L],
        )
        for b in range(B)
    ]
    for b in range(B):
        load[b].start()
        for copy in rings[b]:
            copy.start()
    for copy in (load_w1, load_w2, load_w3, load_grad):
        copy.start()

    quarter = half // 4
    mirrored = [
        [
            remote(
                out_grad.at[s * B + b, i * quarter : (i + 1) * quarter],
                far_grad.at[b, i * quarter : (i + 1) * quarter],
                far_send.at[b, i],
                far_recv.at[b, i],
                (s, place.d, place.mirror),
            )
            for i in range(4)
        ]
        for b in range(B)
    ]
    letters = [copy for copies in mirrored for copy in copies]

    def post(count):
        for copy in letters[:count]:
            copy.start()
        del letters[:count]

    def send_edges(number, b, first, last, size, wrap=False):
        turned = flip[b] == 1
        for at, (head, tail) in enumerate(zip(first, last)):
            head, tail = head.astype(F32), tail.astype(F32)
            edges[number, 0, b, at, :, 0:size] = jnp.where(turned, head, tail).astype(BF16)
            edges[number, 1, b, at, :, 0:size] = jnp.where(turned, tail, head).astype(BF16)
        n = len(first)
        copies = pair(
            number,
            b,
            edges.at[number, 0, b, 0:n, :, 0:size],
            edges.at[number, 1, b, 0:n, :, 0:size],
            edges_in.at[number, 0, b, 0:n, :, 0:size],
            edges_in.at[number, 1, b, 0:n, :, 0:size],
        )
        for copy in copies:
            copy.start()
        return copies

    def take_edges(number, b, at, size, wrap=False):
        from_prev = edges_in[number, 0, b, at, :, 0:size].astype(F32)
        from_next = edges_in[number, 1, b, at, :, 0:size].astype(F32)
        turned = flip[b] == 1
        before = jnp.where(turned, from_next, from_prev)
        after = jnp.where(turned, from_prev, from_next)
        if not wrap:
            before = jnp.where(block_at[b] > 0, before, 0.0)
            after = jnp.where(block_at[b] < nq - 1, after, 0.0)
        return before.astype(BF16), after.astype(BF16)

    def moments(read, count, size):
        none = jnp.zeros((8, size), F32)
        total = chunks(count, lambda r, t: t + jnp.sum(halves(read(r)), axis=0), none, 2)
        mean = row_sum(total) * (1.0 / count)
        mean8 = eight(mean)

        def deviations(r, t):
            away = halves(read(r)) - mean8[None]
            return t + jnp.sum(away * away, axis=0)

        return [mean, row_sum(chunks(count, deviations, none, 2))]

    def norm_of(step, count, gain, bias):
        mean, square = step.finish(join_moments(float(count * nd)))
        return Norm(mean, lax.rsqrt(square * (1.0 / (count * nd * nq)) + EPSILON), gain, bias)

    def gradients(norm, back, count):
        scale = 1.0 / (count * nd * nq)
        bias_mean, gain_mean = eight(back[0] * scale), eight(back[1] * scale)
        factor = norm.gain * norm.inv

        def value(grad, normed):
            return factor[None] * (grad - bias_mean[None] - normed * gain_mean[None])

        return value

    def tally(row, b, back):
        for at, total in ((row, back[1]), (row + 1, back[0])):
            to = sums.at[0, at : at + 1, 0 : total.shape[1]]
            if b == 0:
                to[...] = total
            else:
                to[...] = to[...] + total

    def gather(b, first, value):
        at = slice(first // BLOCK, (first + value.shape[0]) // BLOCK)
        value = value.reshape(value.shape[0] // BLOCK, BLOCK, width)
        if b > 0:
            value = value + block_grad[at]
        block_grad[at] = value
        if b == B - 1:
            block_send[at] = value.astype(BF16)

    saved = []

    def save(src, dst, sem):
        copy = pltpu.make_async_copy(src, dst, sem)
        copy.start()
        saved.append(copy)
        return copy

    zero = jnp.zeros((8, C), F32)
    none = jnp.zeros((8, H), F32)
    tap_saves = [None] * B
    swap = remote(sums.at[0], sums.at[1], core_send.at[B], core_recv.at[B], place.partner)
    last = []

    def chain(b):
        low, high = b * half, (b + 1) * half
        turned = flip[b] == 1

        def exchange(number):
            return Exchange(
                place,
                b * 6 + number,
                b * 2 + number % 2,
                plane_buf,
                line_buf,
                exchange_send,
                exchange_recv,
            )

        load[b].wait()
        step = exchange(0)
        step.start(moments(lambda r: window[b, pl.ds(EDGE + r, EDGE)].astype(F32), L, C))
        yield
        for copy in rings[b]:
            copy.wait()
        for parity in range(2):
            shape = (tall, L + 2 * EDGE)
            at = 2 * (lax.broadcasted_iota(jnp.int32, shape, 0) - 8) + parity
            source = flip[b] * (L - 1) + (1 - 2 * flip[b]) * at - shift[b] + EDGE
            pick = jnp.where(lax.broadcasted_iota(jnp.int32, shape, 1) == source, 1.0, 0.0)
            placed[b, parity] = jnp.dot(
                pick.astype(BF16), window[b, 0 : L + 2 * EDGE], preferred_element_type=F32
            ).astype(BF16)
        step.relay(join_moments(float(L)))
        post(2)
        yield
        norm1 = norm_of(step, L, gain1, bias1)
        for parity in range(2):

            def activate(r, c):
                block = halves(placed[b, parity, pl.ds(r, EDGE)].astype(F32))
                value = flat(gelu(norm1.pre(norm1.normed(block))))
                at = lax.broadcasted_iota(jnp.int32, value.shape, 0) + (r - 8)
                at = 2 * at + (parity + block_at[b] * L)
                act[pl.ds(r, EDGE)] = jnp.where((at >= 0) & (at < nq * L), value, 0.0)
                return c

            chunks(tall, activate)

            def spread(r, c):
                values = act[pl.ds(r, 2 * EDGE)]
                for off in range(3):
                    at = (2 * off + parity) * C
                    taps[pl.ds(low + r, EDGE), at : at + C] = values[
                        7 + off : 7 + off + EDGE
                    ].astype(BF16)
                return c

            chunks(half, spread)
        tap_saves[b] = save(taps.at[low:high], taps_out.at[low:high], load_sem.at[B + b])
        yield
        if b == 0:
            load_w1.wait()
        tile = even.shape[1]

        def convolve(j, c):
            cols = pl.ds(pl.multiple_of(j * tile, tile), tile)
            even[...] = jnp.dot(
                taps[low:high, 0 : 5 * C], w1[:, cols], preferred_element_type=F32
            )
            odd[...] = jnp.dot(
                taps[low:high, C : 6 * C], w1[:, cols], preferred_element_type=F32
            )

            def pool(r, c):
                at = pl.ds(r, EDGE)
                left, right = even[at, :], odd[at, :]
                away = left - right
                small = jnp.exp(-jnp.abs(away))
                pooled[b, pl.ds(EDGE + r, EDGE), cols] = (
                    jnp.maximum(left, right) + jnp.log(1.0 + small)
                ).astype(BF16)
                part = 1.0 / (1.0 + small)
                share[pl.ds(low + r, EDGE), cols] = jnp.where(away >= 0, part, small * part)
                return c

            chunks(half, pool, 0, 2)
            return c

        lax.fori_loop(0, C // tile, convolve, 0)
        step = exchange(1)
        step.start(moments(lambda r: pooled[b, pl.ds(EDGE + r, EDGE)].astype(F32), half, C))
        ring = send_edges(
            0, b, [pooled[b, EDGE : 2 * EDGE]], [pooled[b, half : half + EDGE]], C
        )
        yield
        step.relay(join_moments(float(half)))
        post(2)
        yield
        norm2 = norm_of(step, half, gain2, bias2)
        for copy in ring:
            copy.wait()
        pooled[b, 0:EDGE], pooled[b, EDGE + half : long] = take_edges(0, b, 0, C)

        def activate(r, c):
            block = halves(pooled[b, pl.ds(r, EDGE)].astype(F32))
            value = flat(gelu(norm2.pre(norm2.normed(block))))
            at = lax.broadcasted_iota(jnp.int32, value.shape, 0) + (r - EDGE + block_at[b] * half)
            act[pl.ds(r, EDGE)] = jnp.where((at >= 0) & (at < nq * half), value, 0.0)
            return c

        chunks(long, activate)

        def spread(r, c):
            values = act[pl.ds(r, 3 * EDGE)]
            for k in range(3):
                at = EDGE + (k - 1) * DILATION_SIZE
                second[pl.ds(low + r, EDGE), k * C : (k + 1) * C] = values[
                    at : at + EDGE
                ].astype(BF16)
            return c

        chunks(half, spread)
        if b == 0:
            load_w2.wait()
        narrow[low:high] = jnp.dot(second[low:high], w2[...], preferred_element_type=F32)
        step = exchange(2)
        step.start(moments(lambda r: narrow[pl.ds(low + r, EDGE)], half, H))
        yield
        step.relay(join_moments(float(half)))
        if b == 0:
            load_w3.wait()
            load_grad.wait()
        for copy in mirrored[b]:
            copy.wait()

        def choose(r, c):
            at = pl.ds(r, EDGE)
            own_grad[b, at] = jnp.where(
                turned, far_grad[b, at].astype(F32), own_grad[b, at].astype(F32)
            ).astype(BF16)
            return c

        chunks(half, choose)
        third_in[low:high] = lax.dot_general(
            own_grad[b], w3[...], NT, preferred_element_type=F32
        )
        yield
        norm3 = norm_of(step, half, gain3, bias3)

        def activate(r, carry):
            at = pl.ds(low + r, EDGE)
            normed = norm3.normed(halves(narrow[at]))
            pre = norm3.pre(normed)
            third[at] = flat(gelu(pre)).astype(BF16)
            grad = halves(third_in[at]) * gelu_slope(pre)
            third_in[at] = flat(grad)
            return carry[0] + jnp.sum(grad, axis=0), carry[1] + jnp.sum(grad * normed, axis=0)

        step = exchange(3)
        step.start([row_sum(t) for t in chunks(half, activate, (none, none))])
        for side in range(2):
            cols = slice(side * width, (side + 1) * width)
            ours[side, b] = (
                pooled[b, EDGE : EDGE + half, cols].astype(F32)
                + jnp.dot(third[low:high], w3[:, cols], preferred_element_type=F32)
            ).astype(BF16)
        if b == B - 1:
            save(ours, result_out, local_sem.at[4])
        yield
        step.relay(join_sums)
        value = lax.dot_general(third[low:high], own_grad[b], TN, preferred_element_type=F32)
        gather(b, 3 * C, jnp.concatenate([value[:, 0:width], value[:, width:]], axis=0))
        yield
        back = step.finish(join_sums)
        tally(4, b, back)
        gradient = gradients(norm3, back, half)

        def input_grad(r, c):
            at = pl.ds(low + r, EDGE)
            value = gradient(halves(third_in[at]), norm3.normed(halves(narrow[at])))
            narrow_grad[b, pl.ds(EDGE + r, EDGE)] = flat(value).astype(BF16)
            return c

        chunks(half, input_grad)
        ring = send_edges(
            1, b, [narrow_grad[b, EDGE : 2 * EDGE]], [narrow_grad[b, half : half + EDGE]], H
        )
        for k in range(3):
            gather(
                b,
                k * C,
                lax.dot_general(
                    second[low:high, k * C : (k + 1) * C],
                    narrow_grad[b, EDGE : EDGE + half],
                    TN,
                    preferred_element_type=F32,
                ),
            )
        yield
        for copy in ring:
            copy.wait()
        narrow_grad[b, 0:EDGE], narrow_grad[b, EDGE + half : long] = take_edges(1, b, 0, H)

        def spread(r, c):
            values = narrow_grad[b, pl.ds(r, 3 * EDGE)].astype(F32)
            for k in range(3):
                at = EDGE - (k - 1) * DILATION_SIZE
                narrow_taps[pl.ds(low + r, EDGE), k * H : (k + 1) * H] = values[
                    at : at + EDGE
                ].astype(BF16)
            return c

        chunks(half, spread)
        second_grad[low:high] = sum(
            lax.dot_general(
                narrow_taps[low:high, k * H : (k + 1) * H],
                w2[k * C : (k + 1) * C],
                NT,
                preferred_element_type=F32,
            )
            for k in range(3)
        )

        def slope(r, carry):
            at = pl.ds(low + r, EDGE)
            normed = norm2.normed(halves(pooled[b, pl.ds(EDGE + r, EDGE)].astype(F32)))
            grad = halves(second_grad[at]) * gelu_slope(norm2.pre(normed))
            second_grad[at] = flat(grad)
            return carry[0] + jnp.sum(grad, axis=0), carry[1] + jnp.sum(grad * normed, axis=0)

        step = exchange(4)
        step.start([row_sum(t) for t in chunks(half, slope, (zero, zero))])
        yield
        step.relay(join_sums)
        yield
        back = step.finish(join_sums)
        tally(2, b, back)
        gradient = gradients(norm2, back, half)

        def unpool(r, c):
            at = pl.ds(low + r, EDGE)
            normed = norm2.normed(halves(pooled[b, pl.ds(EDGE + r, EDGE)].astype(F32)))
            value = flat(gradient(halves(second_grad[at]), normed))
            value = value + own_grad[b, pl.ds(r, EDGE)].astype(F32)
            value = value.astype(BF16).astype(F32)
            part = share[at]
            wide_grad[0, at] = (value * part).astype(BF16)
            wide_grad[1, at] = (value * (1.0 - part)).astype(BF16)
            return c

        chunks(half, unpool)
        ring = send_edges(
            2,
            b,
            [wide_grad[p, low : low + EDGE] for p in range(2)],
            [wide_grad[p, high - EDGE : high] for p in range(2)],
            C,
        )
        if b == B - 1:
            save(wide_grad, grad_out, local_sem.at[5])
        tap_saves[b].wait()
        saved.remove(tap_saves[b])

        def put(parity, r, values):
            for at in range(3):
                lanes = (1 - parity + 2 * at) * C
                taps[pl.ds(low + r, EDGE), lanes : lanes + C] = values[
                    EDGE + 1 - at : 2 * EDGE + 1 - at
                ].astype(BF16)

        for parity in range(2):

            def spread(i, c):
                r = pl.multiple_of(i * EDGE, EDGE)
                values = wide_grad[parity, pl.ds(low + r - EDGE, 3 * EDGE)].astype(F32)
                put(parity, r, values)
                return c

            lax.fori_loop(1, half // EDGE - 1, spread, 0)
        yield
        for copy in ring:
            copy.wait()
        for parity in range(2):
            before, after = take_edges(2, b, parity, C)
            put(
                parity,
                0,
                jnp.concatenate([before, wide_grad[parity, low : low + 2 * EDGE]], axis=0).astype(F32),
            )
            put(
                parity,
                half - EDGE,
                jnp.concatenate([wide_grad[parity, high - 2 * EDGE : high], after], axis=0).astype(F32),
            )
        carry = (zero, zero)
        for parity in range(2):
            if parity == 1:
                yield

            def convolve(j, c):
                at = pl.multiple_of(j * BLOCK, BLOCK)
                part = None
                for k in range(5):
                    lanes = (k + 1 - parity) * C
                    more = lax.dot_general(
                        taps[low:high, lanes : lanes + C],
                        w1[pl.ds(k * C + at, BLOCK), :],
                        NT,
                        preferred_element_type=F32,
                    )
                    part = more if part is None else part + more
                act_grad[parity, low:high, pl.ds(at, BLOCK)] = part
                return c

            lax.fori_loop(0, C // BLOCK, convolve, 0)

            def slope(r, carry):
                at = pl.ds(low + r, EDGE)
                values = placed[b, parity, pl.ds(r, 2 * EDGE)].astype(F32)[8 : 8 + EDGE]
                normed = norm1.normed(halves(values))
                grad = halves(act_grad[parity, at]) * gelu_slope(norm1.pre(normed))
                act_grad[parity, at] = flat(grad)
                return carry[0] + jnp.sum(grad, axis=0), carry[1] + jnp.sum(grad * normed, axis=0)

            carry = chunks(half, slope, carry)
        step = exchange(5)
        step.start([row_sum(t) for t in carry])
        yield
        step.relay(join_sums)
        yield
        back = step.finish(join_sums)
        tally(0, b, back)
        if b == B - 1:
            swap.start()
        gradient = gradients(norm1, back, L)
        for parity in range(2):

            def input_grad(r, c):
                values = placed[b, parity, pl.ds(r, 2 * EDGE)].astype(F32)[8 : 8 + EDGE]
                value = gradient(
                    halves(act_grad[parity, pl.ds(low + r, EDGE)]), norm1.normed(halves(values))
                )
                window[b, pl.ds(parity * long + EDGE + r, EDGE)] = flat(value).astype(BF16)
                return c

            chunks(half, input_grad)
        starts = [parity * long for parity in range(2)]
        ring = send_edges(
            3,
            b,
            [window[b, at + EDGE : at + 2 * EDGE] for at in starts],
            [window[b, at + half : at + half + EDGE] for at in starts],
            C,
        )
        yield
        for copy in ring:
            copy.wait()
        for parity, at in enumerate(starts):
            window[b, at : at + EDGE], window[b, at + EDGE + half : at + long] = take_edges(
                3, b, parity, C, True
            )
        shape = (L, 2 * long)
        at = lax.broadcasted_iota(jnp.int32, shape, 0) + shift[b]
        at = flip[b] * (L - 1) + (1 - 2 * flip[b]) * at
        source = (at & 1) * long + (at >> 1) + EDGE
        pick = jnp.where(lax.broadcasted_iota(jnp.int32, shape, 1) == source, 1.0, 0.0)
        pick = pick.astype(BF16)
        for side in range(2):
            cols = slice(side * width, (side + 1) * width)
            placed_back[side, b] = jnp.dot(
                pick, window[b, :, cols], preferred_element_type=F32
            ).astype(BF16)
        across = remote(
            placed_back.at[1 - s, b], final.at[b], core_send.at[b], core_recv.at[b], place.partner
        )
        across.start()
        save(placed_back.at[s, b], back_out.at[s * B + b], load_sem.at[2 * B + b])
        yield
        across.wait()
        save(final.at[b], back_out.at[(1 - s) * B + b], load_sem.at[3 * B + b])

    def adding():
        for stage in range(len(cube.events())):
            for block in range(blocks):
                cube.run(block, stage)
                if block % 3 == 2:
                    yield

    run_chains(chain, adding, B)
    cube.end()
    swap.wait()
    outs = (gain1_out, bias1_out, gain2_out, bias2_out, gain3_out, bias3_out)
    for i, to in enumerate(outs):
        count = to.shape[0]
        row = sums[0, i : i + 1, 0:count] + sums[1, i : i + 1, 0:count]
        to[...] = row.reshape(count)
    for copy in saved:
        copy.wait()


GRADS_STEP = 10


def run_chains(chain, adding, count):
    chains = [chain(b) for b in range(count)]
    taken = [0] * count
    extra = None

    def advance(b):
        taken[b] += 1
        return next(chains[b], "end") != "end"

    for b in range(count):
        advance(b)
    for b in range(count):
        advance(b)
    advance(0)
    live = list(range(count))
    while live:
        for b in list(live):
            if not advance(b):
                live.remove(b)
            if extra is None and taken[-1] >= GRADS_STEP:
                extra = adding()
            if extra is not None:
                next(extra, None)
    if extra is not None:
        for _ in extra:
            pass


class Cube:
    def __init__(self, place, blocks, base, refs):
        self.place, self.blocks, self.base = place, blocks, base
        self.total, self.inbox, self.relayed, self.summed, self.out = refs[:5]
        self.send_sem, self.core_recv, self.down_recv, self.up_recv, self.share_recv = refs[5:]
        self.sources = [None] * blocks
        self.axes = cube_axes(place)
        self.planar = place.nd.bit_length() - 1
        self.flight = [None] * blocks
        self.state = [None] * blocks

    def order(self, block):
        return [self.axes[i] for i in cube_order(block, self.planar, len(self.axes))]

    def events(self):
        depth = len(self.axes)
        return ["core"] + ["down"] * depth + ["up"] * halvings(depth) + ["share", "out"]

    def _add(self, block, incoming, first, count, send):
        total, inbox = self.total, self.inbox

        step = min(count, 4 * EDGE)
        for r in range(0, count, step):
            at = pl.ds(pl.multiple_of(first + r, EDGE), step)
            value = total[self.base + block, at] + incoming(r, step).astype(F32)
            total[self.base + block, at] = value
            if send:
                inbox[block, at] = value.astype(BF16)

    def run(self, block, stage):
        place, depth = self.place, len(self.axes)
        s = place.s
        last = depth + halvings(depth)
        if self.flight[block] is not None:
            self.flight[block].wait()
        if stage == 0:
            copy = remote(
                self.sources[block],
                self.inbox.at[block],
                self.send_sem.at[block],
                self.core_recv.at[block],
                place.partner,
            )
        elif stage <= depth:
            k = stage - 1
            partner, side = self.order(block)[k]
            size, first, past = sizes(k), [0], None
            if k > 0:
                first, past = self.state[block]
            offset = first[-1]
            if k == 0:
                incoming = lambda base: lambda r, n: self.inbox[
                    block, pl.ds(pl.multiple_of(base + r, EDGE), n)
                ]
                base_of = lambda at: at
            else:
                incoming = lambda base: lambda r, n: self.relayed[
                    block, pl.ds(pl.multiple_of(base + r, EDGE), n)
                ]
                base_of = lambda at: at - offset + region(k - 1)
            if size >= 2 * EDGE:
                small = size // 2
                give, hold = offset + (1 - side) * small, offset + side * small
                self._add(block, incoming(base_of(give)), give, small, True)
            else:
                small, give, hold = size, offset, offset
                self._add(block, incoming(base_of(give)), give, small, True)
                at = pl.ds(pl.multiple_of(give, EDGE), small)
                self.total[self.base + block, at] = self.inbox[block, at].astype(F32)
            copy = remote(
                self.inbox.at[block, pl.ds(pl.multiple_of(give, EDGE), small)],
                self.relayed.at[block, region(k) : region(k) + small],
                self.send_sem.at[block],
                self.down_recv.at[block, k],
                partner,
            )
            self.state[block] = (first + [hold], past)
        elif stage <= last:
            k = last - stage
            first, _ = self.state[block]
            partner, _ = self.order(block)[k]
            hold, small = first[k + 1], sizes(k + 1)
            at = pl.ds(pl.multiple_of(hold, EDGE), small)
            if stage == depth + 1:
                end = pl.ds(pl.multiple_of(first[-1], EDGE), sizes(depth))
                begin = region(depth - 1)
                self.summed[s, block, end] = (
                    self.total[self.base + block, end]
                    + self.relayed[block, begin : begin + sizes(depth)].astype(F32)
                ).astype(BF16)
            copy = remote(
                self.summed.at[s, block, at],
                self.summed.at[s, block, at],
                self.send_sem.at[block],
                self.up_recv.at[block, k],
                partner,
            )
        elif stage == last + 1:
            copy = remote(
                self.summed.at[s, block],
                self.summed.at[s, block],
                self.send_sem.at[block],
                self.share_recv.at[block],
                place.partner,
            )
        else:
            copy = pltpu.make_async_copy(
                self.summed.at[:, block], self.out.at[:, block], self.send_sem.at[block]
            )
        if stage > 0 and stage <= depth:
            copy.start()
            if size >= 2 * EDGE:
                self._add(block, incoming(base_of(hold)), hold, small, False)
        else:
            copy.start()
        self.flight[block] = copy

    def end(self):
        for copy in self.flight:
            copy.wait()


BLOCK = 256


def sizes(k):
    return max(BLOCK >> k, EDGE)


def region(k):
    return sum(sizes(i + 1) for i in range(k))


def halvings(depth):
    return sum(sizes(k) >= 2 * EDGE for k in range(depth))


def cube_axes(place):
    axes = []
    bit = 1
    while bit < place.nd:
        side = lax.rem(place.d // bit, 2)
        axes.append(((place.s, place.d + bit * (1 - 2 * side), place.q), side))
        bit *= 2
    bit = 1
    while bit < place.nq:
        side = lax.rem(place.q // bit, 2)
        axes.append(((place.s, place.d, place.q + bit * (1 - 2 * side)), side))
        bit *= 2
    return axes


def cube_order(block, planar, depth):
    kind = KINDS[block % len(KINDS)]
    order = [(kind + i) % planar for i in range(planar)] + list(range(planar, depth))
    if kind < 0:
        order.remove(planar)
        order = [planar] + order
    return order


def plan(planar, depth, blocks, pieces, events):
    rate, cost = 70e3, 0.15
    free = [0.0] * (depth + 1)
    ready = {}
    now, order, done = 0.0, [], 0.0
    pieces = list(pieces)

    def send(axis, size):
        if axis == depth:
            loads, speed, wait = [(depth, 1)], 6 * rate, 1.1
        elif axis > planar:
            loads, speed, wait = [(planar, 1), (axis, 2)], rate, 3.8
        else:
            loads, speed, wait = [(axis, 1)], rate, 3.2
        begin = max([now] + [free[i] for i, _ in loads])
        for i, times in loads:
            free[i] = begin + times * size / speed
        return max(free[i] for i, _ in loads) + wait

    while pieces or ready:
        able = sorted((t, b) for b, (t, _) in ready.items() if t <= now)
        if able:
            _, block = able[0]
            _, stage = ready.pop(block)
            order.append((block, stage))
            kind = events[stage]
            now += cost if kind == "down" else 0.05
            if stage + 1 < len(events):
                axes = cube_order(block, planar, depth)
                if kind in ("core", "share"):
                    axis, size = depth, BLOCK
                elif kind == "down":
                    axis, size = axes[stage - 1], sizes(stage)
                elif kind == "up":
                    k = depth + halvings(depth) - stage
                    axis, size = axes[k], sizes(k + 1)
                else:
                    axis, size = depth, 0
                ready[block] = (send(axis, 2 * size * 768), stage + 1)
        elif pieces and done + pieces[0][4] <= now:
            name, time, made, sends, _ = pieces.pop(0)
            order.append(name)
            now += time
            done = now
            for block in made:
                ready[block] = (now, 0)
            for axis, size in sends:
                send(axis, size)
        else:
            now = min([t for t, _ in ready.values()] + [done + p[4] for p in pieces[:1]])
    return order


def sum_kernel(
    dims,
    taps_in,
    grad_in,
    result_in,
    summed_out,
    near_out,
    far_out,
    total,
    inbox,
    sending,
    relayed,
    summed,
    product,
    taps,
    grads,
    load_sem,
    result_send,
    result_recv,
    *cube_sems,
):
    C, H, L, B, nd, nq = dims
    half = L // 2
    width = C // 2
    place = Place(nd, nq)
    s = place.s
    cross = (1 - s, place.d, place.mirror)
    mine = pl.ds(s * B, B)
    per_tap = C // BLOCK
    blocks = 5 * per_tap
    cube = Cube(place, blocks, 0, (total, inbox, relayed, summed, summed_out) + cube_sems)
    depth = len(cube.axes)
    load_grads = pltpu.make_async_copy(grad_in, grads, load_sem.at[6])
    load_taps = [
        pltpu.make_async_copy(
            taps_in.at[:, i * C : (i + 1) * C], taps.at[:, i * C : (i + 1) * C], load_sem.at[i]
        )
        for i in range(6)
    ]
    for copy in [load_grads] + load_taps:
        copy.start()
    meet = place.greet(place.plane() + place.line() + [place.partner, cross])
    for i in range(blocks):
        cube.sources[i] = sending.at[i]
    todo, pieces = {}, []

    def piece(name, time, made=(), sends=(), after=0.0):
        def keep(body):
            todo[name] = body
            pieces.append((name, time, made, sends, after))
            return body

        return keep

    across = remote(
        result_in.at[1 - s], near_out, result_send.at[0], result_recv.at[0], place.partner
    )
    away = [
        remote(
            result_in.at[side, b],
            far_out.at[s * B + b],
            result_send.at[1 + 2 * b + i],
            result_recv.at[1 + 2 * b + i],
            (side, place.d, place.mirror),
        )
        for b in range(B)
        for i, side in enumerate((s, 1 - s))
    ]

    def result_piece(i, after):
        @piece(("result", i), 0.05, (), [(depth - 1, 4 * half * width)], after)
        def _():
            away[i].start()

    def weight_piece(k):
        @piece(("weight", k), WEIGHT_TIME, range(k * per_tap, (k + 1) * per_tap))
        def _():
            if k == 0:
                load_grads.wait()
                load_taps[0].wait()
            load_taps[k + 1].wait()

            def tile(m, c):
                lanes = pl.multiple_of(k * C + m * BLOCK, BLOCK)
                product[...] = lax.dot_general(
                    taps[:, pl.ds(lanes, BLOCK)], grads[0], TN, preferred_element_type=F32
                ) + lax.dot_general(
                    taps[:, pl.ds(lanes + C, BLOCK)], grads[1], TN, preferred_element_type=F32
                )

                def split(r, c):
                    at = pl.ds(r, EDGE)
                    low = pl.ds(pl.multiple_of(s * width, width), width)
                    high = pl.ds(pl.multiple_of((1 - s) * width, width), width)
                    total[k * per_tap + m, at] = product[at, low]
                    sending[k * per_tap + m, at] = product[at, high].astype(BF16)
                    return c

                chunks(BLOCK, split)
                return c

            lax.fori_loop(0, per_tap, tile, 0)
            if k == 0:
                meet()
                across.start()

    early = len(away) // 2
    for k in range(5):
        weight_piece(k)
        if k < early:
            result_piece(k, 0.0)
    for i in range(early, len(away)):
        result_piece(i, LATE if i == early else 0.0)
    for item in plan(cube.planar, depth, blocks, pieces, cube.events()):
        if item in todo:
            todo[item]()
        else:
            cube.run(*item)
    cube.end()
    across.wait()
    for copy in away:
        copy.wait()


WEIGHT_TIME = 4.5
KINDS = (0, 1, 0, 1, 0, 1, 0, -1, 0, 1, 0, 0, 0, 1, 0)
LATE = 45.0


def finish_kernel(
    dims,
    first,
    later,
    mine,
    near,
    far,
    back,
    flips,
    *refs,
):
    vectors, outs, rest = refs[:6], refs[6:17], refs[17:]
    for src, dst in zip(vectors, outs[5:]):
        dst[...] = src[...]
    finish(dims, first, later, mine, near, far, back, flips, *outs[:5], *rest)


def finish(
    dims,
    first,
    later,
    mine,
    near,
    far,
    back,
    flips,
    conv1,
    conv2,
    conv3,
    result,
    back_out,
    held,
    wide,
    narrow,
    near_buf,
    far_buf,
    back_buf,
    in_sem,
    wide_sem,
    narrow_sem,
    side_sem,
):
    C, H, L, B, nd, nq = dims
    s = lax.axis_index("section")
    first_blocks = first.shape[1]
    blocks = first_blocks + later.shape[1]
    width = C // 2
    slots = wide.shape[0]

    def summed(block):
        return first.at[:, block] if block < first_blocks else later.at[:, block - first_blocks]

    order = list(range(first_blocks, blocks)) + list(range(first_blocks))
    loads = {
        block: pltpu.make_async_copy(summed(block), held.at[block], in_sem.at[block])
        for block in order
    }
    sides = [
        pltpu.make_async_copy(mine.at[s], near_buf.at[pl.ds(s * B, B)], side_sem.at[0]),
        pltpu.make_async_copy(near, near_buf.at[pl.ds((1 - s) * B, B)], side_sem.at[1]),
        pltpu.make_async_copy(far, far_buf, side_sem.at[2]),
        pltpu.make_async_copy(back, back_buf, side_sem.at[3]),
    ]
    for block in order[:4]:
        loads[block].start()
    for copy in sides:
        copy.start()
    for block in order[4:]:
        loads[block].start()
    bottom = 3 * C

    def targets(block, side):
        row = side * first_blocks * BLOCK + block * BLOCK
        if row < bottom:
            return [(0, BLOCK, conv2.at[row : row + BLOCK])]
        parts, at = [], 0
        while at < BLOCK:
            which, begin = (row - bottom + at) // H, (row - bottom + at) % H
            count = min(BLOCK - at, H - begin)
            cols = slice(which * width, (which + 1) * width)
            parts.append((at, count, conv3.at[begin : begin + count, cols]))
            at += count
        return parts

    going = [[] for _ in range(slots)]
    for i, block in enumerate(order):
        slot = i % slots
        for copy in going[slot]:
            copy.wait()
        loads[block].wait()
        for side in range(2):

            def widen(r, c):
                at = pl.ds(pl.multiple_of(r * 64, 64), 64)
                value = held[block, side, at].astype(F32)
                if block >= first_blocks:
                    wide[slot, at, side * width : (side + 1) * width] = value
                else:
                    narrow[slot, side, at] = value
                return c

            lax.fori_loop(0, BLOCK // 64, widen, 0)
        if block >= first_blocks:
            row = (block - first_blocks) * BLOCK
            going[slot] = [
                pltpu.make_async_copy(
                    wide.at[slot], conv1.at[row : row + BLOCK], wide_sem.at[slot]
                )
            ]
        else:
            parts = [(side, *part) for side in range(2) for part in targets(block, side)]
            going[slot] = [
                pltpu.make_async_copy(
                    narrow.at[slot, side, at : at + count], to, narrow_sem.at[slot, j]
                )
                for j, (side, at, count, to) in enumerate(parts)
            ]
        for copy in going[slot]:
            copy.start()
        if i == 2:
            sides[3].wait()
            give = pltpu.make_async_copy(back_buf, back_out, side_sem.at[3])
            give.start()
        if i == 4:
            for copy in sides[:3]:
                copy.wait()
            for b in range(2 * B):
                turned = flips[b]

                def deliver(r, c):
                    at = pl.ds(pl.multiple_of(r * 64, 64), 64)
                    near_buf[b, at] = jnp.where(
                        turned == 1, far_buf[b, at].astype(F32), near_buf[b, at].astype(F32)
                    ).astype(BF16)
                    return c

                lax.fori_loop(0, L // 128, deliver, 0)
            hand = pltpu.make_async_copy(near_buf, result, side_sem.at[0])
            hand.start()
    for copies in going:
        for copy in copies:
            copy.wait()
    give.wait()
    hand.wait()


def on_device(
    nd,
    nq,
    inputs,
    shifts,
    flips,
    gain1,
    bias1,
    weight1,
    gain2,
    bias2,
    weight2,
    gain3,
    bias3,
    weight3,
    out_grad,
):
    sequences, L, C = inputs.shape
    H = weight3.shape[0]
    B, half = sequences // 2, L // 2
    rows = B * half
    dims = (C, H, L, B, nd, nq)
    anywhere = pl.BlockSpec(memory_space=pl.ANY)
    vmem = pl.BlockSpec(memory_space=pltpu.VMEM)
    smem = pl.BlockSpec(memory_space=pltpu.SMEM)
    peers = nd - 1 + nq - 1
    shape = jax.ShapeDtypeStruct
    dma = pltpu.SemaphoreType.DMA
    width = C // 2
    side = (3 * C * H + H * C) // width // 2
    first_blocks = side // BLOCK
    later_blocks = 5 * C // BLOCK
    depth = (nd.bit_length() - 1) + (nq.bit_length() - 1)

    def cube_scratch(blocks):
        return [
            dma((blocks,)),
            dma((blocks,)),
            dma((blocks, depth)),
            dma((blocks, halvings(depth))),
            dma((blocks,)),
        ]

    taps, grads, result, first, back, *vectors = pl.pallas_call(
        functools.partial(chain_kernel, dims),
        name="chain",
        out_shape=(
            shape((rows, 6 * C), BF16),
            shape((2, rows, C), BF16),
            shape((2, B, half, width), BF16),
            shape((2, first_blocks, BLOCK, width), BF16),
            shape((2 * B, L, width), BF16),
        )
        + (shape((C,), F32),) * 4
        + (shape((H,), F32),) * 2,
        in_specs=[
            anywhere,
            anywhere,
            smem,
            smem,
            vmem,
            vmem,
            anywhere,
            vmem,
            vmem,
            anywhere,
            vmem,
            vmem,
            anywhere,
        ],
        out_specs=[anywhere] * 5 + [vmem] * 6,
        scratch_shapes=[
            pltpu.VMEM((B, L + 4 * EDGE, C), BF16),
            pltpu.VMEM((B, 2, half + EDGE, C), BF16),
            pltpu.VMEM((half + 2 * EDGE, C), F32),
            pltpu.VMEM((rows, 6 * C), BF16),
            pltpu.VMEM((5 * C, C), BF16),
            pltpu.VMEM((3 * C, H), BF16),
            pltpu.VMEM((H, C), BF16),
            pltpu.VMEM((half, C // 3), F32),
            pltpu.VMEM((half, C // 3), F32),
            pltpu.VMEM((rows, C), F32),
            pltpu.VMEM((B, half + 2 * EDGE, C), BF16),
            pltpu.VMEM((4, 2, B, 2, EDGE, C), BF16),
            pltpu.VMEM((4, 2, B, 2, EDGE, C), BF16),
            pltpu.VMEM((rows, 3 * C), BF16),
            pltpu.VMEM((rows, H), F32),
            pltpu.VMEM((B, half, C), BF16),
            pltpu.VMEM((B, half, C), BF16),
            pltpu.VMEM((rows, H), F32),
            pltpu.VMEM((rows, H), BF16),
            pltpu.VMEM((B, half + 2 * EDGE, H), BF16),
            pltpu.VMEM((rows, 3 * H), BF16),
            pltpu.VMEM((rows, C), F32),
            pltpu.VMEM((2 * first_blocks, BLOCK, width), F32),
            pltpu.VMEM((2 * first_blocks, BLOCK, width), BF16),
            pltpu.VMEM((first_blocks, BLOCK, width), BF16),
            pltpu.VMEM((first_blocks, region(depth), width), BF16),
            pltpu.VMEM((2, first_blocks, BLOCK, width), BF16),
            pltpu.VMEM((2, rows, C), BF16),
            pltpu.VMEM((2, B, half, width), BF16),
            pltpu.VMEM((2, rows, C), F32),
            pltpu.VMEM((2, B, L, width), BF16),
            pltpu.VMEM((B, L, width), BF16),
            pltpu.VMEM((2, 8, C), F32),
            pltpu.VMEM((6 * B, nd, 2, C), F32),
            pltpu.VMEM((6 * B, nq, 2, C), F32),
            dma((6,)),
            dma((4 * B,)),
            dma((2 * B, peers)),
            dma((2 * B, peers)),
            dma((5, B, 2)),
            dma((5, B, 2)),
            dma((B, 4)),
            dma((B, 4)),
            dma((B + 1,)),
            dma((B + 1,)),
        ]
        + cube_scratch(first_blocks),
        compiler_params=pltpu.CompilerParams(
            collective_id=0, has_side_effects=True, vmem_limit_bytes=60 * 2**20
        ),
    )(
        inputs,
        out_grad,
        shifts,
        flips,
        gain1,
        bias1,
        weight1.reshape(5 * C, C),
        gain2,
        bias2,
        weight2.reshape(3 * C, H),
        gain3,
        bias3,
        weight3,
    )
    later, near, far = pl.pallas_call(
        functools.partial(sum_kernel, dims),
        name="weight_sum",
        out_shape=(
            shape((2, later_blocks, BLOCK, width), BF16),
            shape((B, half, width), BF16),
            shape((2 * B, half, width), BF16),
        ),
        in_specs=[anywhere] * 3,
        out_specs=[anywhere] * 3,
        scratch_shapes=[
            pltpu.VMEM((later_blocks, BLOCK, width), F32),
            pltpu.VMEM((later_blocks, BLOCK, width), BF16),
            pltpu.VMEM((later_blocks, BLOCK, width), BF16),
            pltpu.VMEM((later_blocks, region(depth), width), BF16),
            pltpu.VMEM((2, later_blocks, BLOCK, width), BF16),
            pltpu.VMEM((BLOCK, C), F32),
            pltpu.VMEM((rows, 6 * C), BF16),
            pltpu.VMEM((2, rows, C), BF16),
            dma((7,)),
            dma((1 + 2 * B,)),
            dma((1 + 2 * B,)),
        ]
        + cube_scratch(later_blocks),
        compiler_params=pltpu.CompilerParams(
            collective_id=1, has_side_effects=True, vmem_limit_bytes=60 * 2**20
        ),
    )(taps, grads, result)
    blocks = first_blocks + later_blocks
    slots = 6
    conv1, conv2, conv3, result, back, *vectors = pl.pallas_call(
        functools.partial(finish_kernel, dims),
        name="widen",
        out_shape=(
            shape((5 * C, C), F32),
            shape((3 * C, H), F32),
            shape((H, C), F32),
            shape((2 * B, half, width), BF16),
            shape((2 * B, L, width), BF16),
        )
        + (shape((C,), F32),) * 4
        + (shape((H,), F32),) * 2,
        in_specs=[anywhere] * 6 + [smem] + [vmem] * 6,
        out_specs=[anywhere] * 5 + [vmem] * 6,
        scratch_shapes=[
            pltpu.VMEM((blocks, 2, BLOCK, width), BF16),
            pltpu.VMEM((slots, BLOCK, C), F32),
            pltpu.VMEM((slots, 2, BLOCK, width), F32),
            pltpu.VMEM((2 * B, half, width), BF16),
            pltpu.VMEM((2 * B, half, width), BF16),
            pltpu.VMEM((2 * B, L, width), BF16),
            dma((blocks,)),
            dma((slots,)),
            dma((slots, 4)),
            dma((4,)),
        ],
        compiler_params=pltpu.CompilerParams(vmem_limit_bytes=60 * 2**20),
    )(first, later, result, near, far, back, flips, *vectors)
    return (
        result,
        back,
        conv1.reshape(5, C, C),
        vectors[0],
        vectors[1],
        conv2.reshape(3, C, H),
        vectors[2],
        vectors[3],
        conv3,
        vectors[4],
        vectors[5],
    )


def solution(mesh):
    whole = P()
    split = P("dp", "seq", None)
    return jax.shard_map(
        functools.partial(on_device, mesh.shape["dp"], mesh.shape["seq"]),
        mesh=mesh,
        in_specs=(split, P("dp"), P("dp")) + (whole,) * 9 + (split,),
        out_specs=(P("dp", "seq", "section"),) * 2 + (whole,) * 9,
        check_vma=False,
    )
```

```python
import functools

import jax
import jax.numpy as jnp
from jax import lax
from jax.experimental import pallas as pl
from jax.experimental.pallas import tpu as pltpu
from jax.sharding import PartitionSpec as P

DILATION_SIZE = 11
EPSILON = 0.001
EDGE = 16
MESH = pl.DeviceIdType.MESH
F32 = jnp.float32
BF16 = jnp.bfloat16
SCALE = 0.7978845608028654
CUBIC = 0.044715
TN = (((0,), (0,)), ((), ()))
NT = (((1,), (1,)), ((), ()))


def gelu(u):
    return 0.5 * u * (1.0 + jnp.tanh(SCALE * u * (1.0 + CUBIC * (u * u))))


def gelu_slope(u):
    square = u * u
    t = jnp.tanh(SCALE * u * (1.0 + CUBIC * square))
    return 0.5 * (1.0 + t) + (0.5 * SCALE) * u * (1.0 - t * t) * (1.0 + (3.0 * CUBIC) * square)


def chunks(count, body, carry=0, unroll=2):
    def step(i, carry):
        return body(pl.multiple_of(i * EDGE, EDGE), carry)

    return lax.fori_loop(0, count // EDGE, step, carry, unroll=unroll)


def eight(row):
    return jnp.broadcast_to(row, (8, row.shape[-1]))


def halves(block):
    return block.reshape(block.shape[0] // 8, 8, block.shape[1])


def flat(block):
    return block.reshape(block.shape[0] * 8, block.shape[2])


def row_sum(block):
    return jnp.sum(block, axis=0, keepdims=True)


class Place:
    def __init__(self, nd, nq):
        self.nd, self.nq = nd, nq
        self.s, self.d, self.q = (lax.axis_index(a) for a in ("section", "dp", "seq"))
        self.mirror = nq - 1 - self.q
        self.next = lax.rem(self.q + 1, nq)
        self.prev = lax.rem(self.q + nq - 1, nq)
        self.partner = (1 - self.s, self.d, self.q)

    def plane(self):
        return [(self.s, lax.rem(self.d + i, self.nd), self.q) for i in range(1, self.nd)]

    def line(self):
        return [(self.s, self.d, lax.rem(self.q + i, self.nq)) for i in range(1, self.nq)]

    def greet(self, devices):
        barrier = pltpu.get_barrier_semaphore()
        for device in devices:
            pl.semaphore_signal(barrier, inc=1, device_id=device, device_id_type=MESH)
        return lambda: pl.semaphore_wait(barrier, len(devices))


def remote(src, dst, send_sem, recv_sem, device):
    return pltpu.make_async_remote_copy(
        src_ref=src,
        dst_ref=dst,
        send_sem=send_sem,
        recv_sem=recv_sem,
        device_id=device,
        device_id_type=MESH,
    )


class Exchange:
    def __init__(self, place, number, sems, plane_buf, line_buf, send_sem, recv_sem):
        self.place = place
        self.plane_buf, self.line_buf = plane_buf.at[number], line_buf.at[number]
        self.send_sem, self.recv_sem = send_sem.at[sems], recv_sem.at[sems]

    def _start(self, buf, slot, rows, devices, base):
        for at, row in enumerate(rows):
            buf[slot, at : at + 1, 0 : row.shape[1]] = row
        self.copies = [
            remote(
                buf.at[slot],
                buf.at[slot],
                self.send_sem.at[base + i],
                self.recv_sem.at[base + i],
                device,
            )
            for i, device in enumerate(devices)
        ]
        for copy in self.copies:
            copy.start()

    def _finish(self, buf, count, n_rows, width):
        for copy in self.copies:
            copy.wait()
        return [[buf[j, at : at + 1, 0:width] for at in range(n_rows)] for j in range(count)]

    def start(self, rows):
        self.n_rows, self.width = len(rows), rows[0].shape[1]
        self._start(self.plane_buf, self.place.d, rows, self.place.plane(), 0)

    def relay(self, join):
        parts = self._finish(self.plane_buf, self.place.nd, self.n_rows, self.width)
        self._start(
            self.line_buf, self.place.q, join(parts), self.place.line(), self.place.nd - 1
        )

    def finish(self, join):
        return join(self._finish(self.line_buf, self.place.nq, self.n_rows, self.width))


def join_sums(parts):
    totals = parts[0]
    for part in parts[1:]:
        totals = [total + row for total, row in zip(totals, part)]
    return totals


def join_moments(count):
    def join(parts):
        n = len(parts[0]) // 2
        totals = join_sums(parts)
        means = [total * (1.0 / len(parts)) for total in totals[:n]]
        squares = totals[n:]
        for part in parts:
            squares = [
                square + count * (row - mean) * (row - mean)
                for square, row, mean in zip(squares, part[:n], means)
            ]
        return means + squares

    return join


class Norm:
    def __init__(self, mean, inv, gain, bias):
        self.mean, self.inv = eight(mean), eight(inv)
        self.gain, self.bias = (
            eight(vector[...].reshape(1, vector.shape[0])) for vector in (gain, bias)
        )

    def normed(self, block):
        return (block - self.mean[None]) * self.inv[None]

    def pre(self, normed):
        return normed * self.gain[None] + self.bias[None]


def chain_kernel(
    dims,
    inputs,
    out_grad,
    shifts,
    flips,
    gain1,
    bias1,
    weight1,
    gain2,
    bias2,
    weight2,
    gain3,
    bias3,
    weight3,
    taps_out,
    grad_out,
    result_out,
    summed_out,
    back_out,
    gain1_out,
    bias1_out,
    gain2_out,
    bias2_out,
    gain3_out,
    bias3_out,
    window,
    placed,
    act,
    taps,
    w1,
    w2,
    w3,
    even,
    odd,
    share,
    pooled,
    edges,
    edges_in,
    second,
    narrow,
    own_grad,
    far_grad,
    third_in,
    third,
    narrow_grad,
    narrow_taps,
    second_grad,
    block_grad,
    block_send,
    inbox,
    relayed,
    summed,
    wide_grad,
    ours,
    act_grad,
    placed_back,
    final,
    sums,
    plane_buf,
    line_buf,
    local_sem,
    load_sem,
    exchange_send,
    exchange_recv,
    halo_send,
    halo_recv,
    far_send,
    far_recv,
    core_send,
    core_recv,
    *cube_sems,
):
    C, H, L, B, nd, nq = dims
    half = L // 2
    width = C // 2
    tall = half + EDGE
    long = half + 2 * EDGE
    place = Place(nd, nq)
    s, q = place.s, place.q
    blocks = inbox.shape[0]
    cube = Cube(place, blocks, s * blocks, (block_grad, inbox, relayed, summed, summed_out) + cube_sems)
    for i in range(blocks):
        cube.sources[i] = block_send.at[(1 - s) * blocks + i]
    place.greet(place.plane() + place.line() + [place.partner])()
    flip = [flips[s * B + b] for b in range(B)]
    shift = [shifts[s * B + b] for b in range(B)]
    block_at = [flip[b] * (nq - 1 - q) + (1 - flip[b]) * q for b in range(B)]

    load = [
        pltpu.make_async_copy(
            inputs.at[s * B + b], window.at[b, EDGE : EDGE + L], load_sem.at[b]
        )
        for b in range(B)
    ]
    load_w1 = pltpu.make_async_copy(weight1, w1, local_sem.at[0])
    load_w2 = pltpu.make_async_copy(weight2, w2, local_sem.at[1])
    load_w3 = pltpu.make_async_copy(weight3, w3, local_sem.at[2])
    load_grad = pltpu.make_async_copy(out_grad.at[pl.ds(s * B, B)], own_grad, local_sem.at[3])

    def pair(number, b, to_next, to_prev, from_prev, from_next):
        return [
            remote(
                to_next,
                from_prev,
                halo_send.at[number, b, 0],
                halo_recv.at[number, b, 0],
                (s, place.d, place.next),
            ),
            remote(
                to_prev,
                from_next,
                halo_send.at[number, b, 1],
                halo_recv.at[number, b, 1],
                (s, place.d, place.prev),
            ),
        ]

    rings = [
        pair(
            4,
            b,
            inputs.at[s * B + b, L - EDGE : L],
            inputs.at[s * B + b, 0:EDGE],
            window.at[b, 0:EDGE],
            window.at[b, EDGE + L : 2 * EDGE + L],
        )
        for b in range(B)
    ]
    for b in range(B):
        load[b].start()
        for copy in rings[b]:
            copy.start()
    for copy in (load_w1, load_w2, load_w3, load_grad):
        copy.start()

    quarter = half // 4
    mirrored = [
        [
            remote(
                out_grad.at[s * B + b, i * quarter : (i + 1) * quarter],
                far_grad.at[b, i * quarter : (i + 1) * quarter],
                far_send.at[b, i],
                far_recv.at[b, i],
                (s, place.d, place.mirror),
            )
            for i in range(4)
        ]
        for b in range(B)
    ]
    letters = [copy for copies in mirrored for copy in copies]

    def post(count):
        for copy in letters[:count]:
            copy.start()
        del letters[:count]

    def send_edges(number, b, first, last, size, wrap=False):
        turned = flip[b] == 1
        for at, (head, tail) in enumerate(zip(first, last)):
            head, tail = head.astype(F32), tail.astype(F32)
            edges[number, 0, b, at, :, 0:size] = jnp.where(turned, head, tail).astype(BF16)
            edges[number, 1, b, at, :, 0:size] = jnp.where(turned, tail, head).astype(BF16)
        n = len(first)
        copies = pair(
            number,
            b,
            edges.at[number, 0, b, 0:n, :, 0:size],
            edges.at[number, 1, b, 0:n, :, 0:size],
            edges_in.at[number, 0, b, 0:n, :, 0:size],
            edges_in.at[number, 1, b, 0:n, :, 0:size],
        )
        for copy in copies:
            copy.start()
        return copies

    def take_edges(number, b, at, size, wrap=False):
        from_prev = edges_in[number, 0, b, at, :, 0:size].astype(F32)
        from_next = edges_in[number, 1, b, at, :, 0:size].astype(F32)
        turned = flip[b] == 1
        before = jnp.where(turned, from_next, from_prev)
        after = jnp.where(turned, from_prev, from_next)
        if not wrap:
            before = jnp.where(block_at[b] > 0, before, 0.0)
            after = jnp.where(block_at[b] < nq - 1, after, 0.0)
        return before.astype(BF16), after.astype(BF16)

    def moments(read, count, size):
        none = jnp.zeros((8, size), F32)
        total = chunks(count, lambda r, t: t + jnp.sum(halves(read(r)), axis=0), none, 2)
        mean = row_sum(total) * (1.0 / count)
        mean8 = eight(mean)

        def deviations(r, t):
            away = halves(read(r)) - mean8[None]
            return t + jnp.sum(away * away, axis=0)

        return [mean, row_sum(chunks(count, deviations, none, 2))]

    def norm_of(step, count, gain, bias):
        mean, square = step.finish(join_moments(float(count * nd)))
        return Norm(mean, lax.rsqrt(square * (1.0 / (count * nd * nq)) + EPSILON), gain, bias)

    def gradients(norm, back, count):
        scale = 1.0 / (count * nd * nq)
        bias_mean, gain_mean = eight(back[0] * scale), eight(back[1] * scale)
        factor = norm.gain * norm.inv

        def value(grad, normed):
            return factor[None] * (grad - bias_mean[None] - normed * gain_mean[None])

        return value

    def tally(row, b, back):
        for at, total in ((row, back[1]), (row + 1, back[0])):
            to = sums.at[0, at : at + 1, 0 : total.shape[1]]
            if b == 0:
                to[...] = total
            else:
                to[...] = to[...] + total

    def gather(b, first, value):
        at = slice(first // BLOCK, (first + value.shape[0]) // BLOCK)
        value = value.reshape(value.shape[0] // BLOCK, BLOCK, width)
        if b > 0:
            value = value + block_grad[at]
        block_grad[at] = value
        if b == B - 1:
            block_send[at] = value.astype(BF16)

    saved = []

    def save(src, dst, sem):
        copy = pltpu.make_async_copy(src, dst, sem)
        copy.start()
        saved.append(copy)
        return copy

    zero = jnp.zeros((8, C), F32)
    none = jnp.zeros((8, H), F32)
    tap_saves = [None] * B
    swap = remote(sums.at[0], sums.at[1], core_send.at[B], core_recv.at[B], place.partner)
    last = []

    def chain(b):
        low, high = b * half, (b + 1) * half
        turned = flip[b] == 1

        def exchange(number):
            return Exchange(
                place,
                b * 6 + number,
                b * 2 + number % 2,
                plane_buf,
                line_buf,
                exchange_send,
                exchange_recv,
            )

        load[b].wait()
        step = exchange(0)
        step.start(moments(lambda r: window[b, pl.ds(EDGE + r, EDGE)].astype(F32), L, C))
        post(1)
        yield
        for copy in rings[b]:
            copy.wait()
        for parity in range(2):
            shape = (tall, L + 2 * EDGE)
            at = 2 * (lax.broadcasted_iota(jnp.int32, shape, 0) - 8) + parity
            source = flip[b] * (L - 1) + (1 - 2 * flip[b]) * at - shift[b] + EDGE
            pick = jnp.where(lax.broadcasted_iota(jnp.int32, shape, 1) == source, 1.0, 0.0)
            placed[b, parity] = jnp.dot(
                pick.astype(BF16), window[b, 0 : L + 2 * EDGE], preferred_element_type=F32
            ).astype(BF16)
        step.relay(join_moments(float(L)))
        post(2)
        yield
        norm1 = norm_of(step, L, gain1, bias1)
        for parity in range(2):

            def activate(r, c):
                block = halves(placed[b, parity, pl.ds(r, EDGE)].astype(F32))
                value = flat(gelu(norm1.pre(norm1.normed(block))))
                at = lax.broadcasted_iota(jnp.int32, value.shape, 0) + (r - 8)
                at = 2 * at + (parity + block_at[b] * L)
                act[pl.ds(r, EDGE)] = jnp.where((at >= 0) & (at < nq * L), value, 0.0)
                return c

            chunks(tall, activate)

            def spread(r, c):
                values = act[pl.ds(r, 2 * EDGE)]
                for off in range(3):
                    at = (2 * off + parity) * C
                    taps[pl.ds(low + r, EDGE), at : at + C] = values[
                        7 + off : 7 + off + EDGE
                    ].astype(BF16)
                return c

            chunks(half, spread)
        tap_saves[b] = save(taps.at[low:high], taps_out.at[low:high], load_sem.at[B + b])
        yield
        if b == 0:
            load_w1.wait()
        tile = even.shape[1]

        def convolve(j, c):
            cols = pl.ds(pl.multiple_of(j * tile, tile), tile)
            even[...] = jnp.dot(
                taps[low:high, 0 : 5 * C], w1[:, cols], preferred_element_type=F32
            )
            odd[...] = jnp.dot(
                taps[low:high, C : 6 * C], w1[:, cols], preferred_element_type=F32
            )

            def pool(r, c):
                at = pl.ds(r, EDGE)
                left, right = even[at, :], odd[at, :]
                away = left - right
                small = jnp.exp(-jnp.abs(away))
                pooled[b, pl.ds(EDGE + r, EDGE), cols] = (
                    jnp.maximum(left, right) + jnp.log(1.0 + small)
                ).astype(BF16)
                part = 1.0 / (1.0 + small)
                share[pl.ds(low + r, EDGE), cols] = jnp.where(away >= 0, part, small * part)
                return c

            chunks(half, pool, 0, 2)
            return c

        lax.fori_loop(0, C // tile, convolve, 0)
        step = exchange(1)
        step.start(moments(lambda r: pooled[b, pl.ds(EDGE + r, EDGE)].astype(F32), half, C))
        ring = send_edges(
            0, b, [pooled[b, EDGE : 2 * EDGE]], [pooled[b, half : half + EDGE]], C
        )
        yield
        step.relay(join_moments(float(half)))
        post(1)
        yield
        norm2 = norm_of(step, half, gain2, bias2)
        for copy in ring:
            copy.wait()
        pooled[b, 0:EDGE], pooled[b, EDGE + half : long] = take_edges(0, b, 0, C)

        def activate(r, c):
            block = halves(pooled[b, pl.ds(r, EDGE)].astype(F32))
            value = flat(gelu(norm2.pre(norm2.normed(block))))
            at = lax.broadcasted_iota(jnp.int32, value.shape, 0) + (r - EDGE + block_at[b] * half)
            act[pl.ds(r, EDGE)] = jnp.where((at >= 0) & (at < nq * half), value, 0.0)
            return c

        chunks(long, activate)

        def spread(r, c):
            values = act[pl.ds(r, 3 * EDGE)]
            for k in range(3):
                at = EDGE + (k - 1) * DILATION_SIZE
                second[pl.ds(low + r, EDGE), k * C : (k + 1) * C] = values[
                    at : at + EDGE
                ].astype(BF16)
            return c

        chunks(half, spread)
        if b == 0:
            load_w2.wait()
        narrow[low:high] = jnp.dot(second[low:high], w2[...], preferred_element_type=F32)
        step = exchange(2)
        step.start(moments(lambda r: narrow[pl.ds(low + r, EDGE)], half, H))
        yield
        step.relay(join_moments(float(half)))
        if b == 0:
            load_w3.wait()
            load_grad.wait()
        for copy in mirrored[b]:
            copy.wait()

        def choose(r, c):
            at = pl.ds(r, EDGE)
            own_grad[b, at] = jnp.where(
                turned, far_grad[b, at].astype(F32), own_grad[b, at].astype(F32)
            ).astype(BF16)
            return c

        chunks(half, choose)
        third_in[low:high] = lax.dot_general(
            own_grad[b], w3[...], NT, preferred_element_type=F32
        )
        yield
        norm3 = norm_of(step, half, gain3, bias3)

        def activate(r, carry):
            at = pl.ds(low + r, EDGE)
            normed = norm3.normed(halves(narrow[at]))
            pre = norm3.pre(normed)
            third[at] = flat(gelu(pre)).astype(BF16)
            grad = halves(third_in[at]) * gelu_slope(pre)
            third_in[at] = flat(grad)
            return carry[0] + jnp.sum(grad, axis=0), carry[1] + jnp.sum(grad * normed, axis=0)

        step = exchange(3)
        step.start([row_sum(t) for t in chunks(half, activate, (none, none))])
        for side in range(2):
            cols = slice(side * width, (side + 1) * width)
            ours[side, b] = (
                pooled[b, EDGE : EDGE + half, cols].astype(F32)
                + jnp.dot(third[low:high], w3[:, cols], preferred_element_type=F32)
            ).astype(BF16)
        if b == B - 1:
            save(ours, result_out, local_sem.at[4])
        yield
        step.relay(join_sums)
        value = lax.dot_general(third[low:high], own_grad[b], TN, preferred_element_type=F32)
        gather(b, 3 * C, jnp.concatenate([value[:, 0:width], value[:, width:]], axis=0))
        yield
        back = step.finish(join_sums)
        tally(4, b, back)
        gradient = gradients(norm3, back, half)

        def input_grad(r, c):
            at = pl.ds(low + r, EDGE)
            value = gradient(halves(third_in[at]), norm3.normed(halves(narrow[at])))
            narrow_grad[b, pl.ds(EDGE + r, EDGE)] = flat(value).astype(BF16)
            return c

        chunks(half, input_grad)
        ring = send_edges(
            1, b, [narrow_grad[b, EDGE : 2 * EDGE]], [narrow_grad[b, half : half + EDGE]], H
        )
        for k in range(3):
            gather(
                b,
                k * C,
                lax.dot_general(
                    second[low:high, k * C : (k + 1) * C],
                    narrow_grad[b, EDGE : EDGE + half],
                    TN,
                    preferred_element_type=F32,
                ),
            )
        yield
        for copy in ring:
            copy.wait()
        narrow_grad[b, 0:EDGE], narrow_grad[b, EDGE + half : long] = take_edges(1, b, 0, H)

        def spread(r, c):
            values = narrow_grad[b, pl.ds(r, 3 * EDGE)].astype(F32)
            for k in range(3):
                at = EDGE - (k - 1) * DILATION_SIZE
                narrow_taps[pl.ds(low + r, EDGE), k * H : (k + 1) * H] = values[
                    at : at + EDGE
                ].astype(BF16)
            return c

        chunks(half, spread)
        second_grad[low:high] = sum(
            lax.dot_general(
                narrow_taps[low:high, k * H : (k + 1) * H],
                w2[k * C : (k + 1) * C],
                NT,
                preferred_element_type=F32,
            )
            for k in range(3)
        )

        def slope(r, carry):
            at = pl.ds(low + r, EDGE)
            normed = norm2.normed(halves(pooled[b, pl.ds(EDGE + r, EDGE)].astype(F32)))
            grad = halves(second_grad[at]) * gelu_slope(norm2.pre(normed))
            second_grad[at] = flat(grad)
            return carry[0] + jnp.sum(grad, axis=0), carry[1] + jnp.sum(grad * normed, axis=0)

        step = exchange(4)
        step.start([row_sum(t) for t in chunks(half, slope, (zero, zero))])
        yield
        step.relay(join_sums)
        yield
        back = step.finish(join_sums)
        tally(2, b, back)
        gradient = gradients(norm2, back, half)

        def unpool(r, c):
            at = pl.ds(low + r, EDGE)
            normed = norm2.normed(halves(pooled[b, pl.ds(EDGE + r, EDGE)].astype(F32)))
            value = flat(gradient(halves(second_grad[at]), normed))
            value = value + own_grad[b, pl.ds(r, EDGE)].astype(F32)
            value = value.astype(BF16).astype(F32)
            part = share[at]
            wide_grad[0, at] = (value * part).astype(BF16)
            wide_grad[1, at] = (value * (1.0 - part)).astype(BF16)
            return c

        chunks(half, unpool)
        ring = send_edges(
            2,
            b,
            [wide_grad[p, low : low + EDGE] for p in range(2)],
            [wide_grad[p, high - EDGE : high] for p in range(2)],
            C,
        )
        if b == B - 1:
            save(wide_grad, grad_out, local_sem.at[5])
        tap_saves[b].wait()
        saved.remove(tap_saves[b])

        def put(parity, r, values):
            for at in range(3):
                lanes = (1 - parity + 2 * at) * C
                taps[pl.ds(low + r, EDGE), lanes : lanes + C] = values[
                    EDGE + 1 - at : 2 * EDGE + 1 - at
                ].astype(BF16)

        for parity in range(2):

            def spread(i, c):
                r = pl.multiple_of(i * EDGE, EDGE)
                values = wide_grad[parity, pl.ds(low + r - EDGE, 3 * EDGE)].astype(F32)
                put(parity, r, values)
                return c

            lax.fori_loop(1, half // EDGE - 1, spread, 0)
        yield
        for copy in ring:
            copy.wait()
        for parity in range(2):
            before, after = take_edges(2, b, parity, C)
            put(
                parity,
                0,
                jnp.concatenate([before, wide_grad[parity, low : low + 2 * EDGE]], axis=0).astype(F32),
            )
            put(
                parity,
                half - EDGE,
                jnp.concatenate([wide_grad[parity, high - 2 * EDGE : high], after], axis=0).astype(F32),
            )
        carry = (zero, zero)
        for parity in range(2):
            if parity == 1:
                yield

            def convolve(j, c):
                at = pl.multiple_of(j * BLOCK, BLOCK)
                part = None
                for k in range(5):
                    lanes = (k + 1 - parity) * C
                    more = lax.dot_general(
                        taps[low:high, lanes : lanes + C],
                        w1[pl.ds(k * C + at, BLOCK), :],
                        NT,
                        preferred_element_type=F32,
                    )
                    part = more if part is None else part + more
                act_grad[parity, low:high, pl.ds(at, BLOCK)] = part
                return c

            lax.fori_loop(0, C // BLOCK, convolve, 0)

            def slope(r, carry):
                at = pl.ds(low + r, EDGE)
                values = placed[b, parity, pl.ds(r, 2 * EDGE)].astype(F32)[8 : 8 + EDGE]
                normed = norm1.normed(halves(values))
                grad = halves(act_grad[parity, at]) * gelu_slope(norm1.pre(normed))
                act_grad[parity, at] = flat(grad)
                return carry[0] + jnp.sum(grad, axis=0), carry[1] + jnp.sum(grad * normed, axis=0)

            carry = chunks(half, slope, carry)
        step = exchange(5)
        step.start([row_sum(t) for t in carry])
        yield
        step.relay(join_sums)
        yield
        back = step.finish(join_sums)
        tally(0, b, back)
        if b == B - 1:
            swap.start()
        gradient = gradients(norm1, back, L)
        for parity in range(2):

            def input_grad(r, c):
                values = placed[b, parity, pl.ds(r, 2 * EDGE)].astype(F32)[8 : 8 + EDGE]
                value = gradient(
                    halves(act_grad[parity, pl.ds(low + r, EDGE)]), norm1.normed(halves(values))
                )
                window[b, pl.ds(parity * long + EDGE + r, EDGE)] = flat(value).astype(BF16)
                return c

            chunks(half, input_grad)
        starts = [parity * long for parity in range(2)]
        ring = send_edges(
            3,
            b,
            [window[b, at + EDGE : at + 2 * EDGE] for at in starts],
            [window[b, at + half : at + half + EDGE] for at in starts],
            C,
        )
        yield
        for copy in ring:
            copy.wait()
        for parity, at in enumerate(starts):
            window[b, at : at + EDGE], window[b, at + EDGE + half : at + long] = take_edges(
                3, b, parity, C, True
            )
        shape = (L, 2 * long)
        at = lax.broadcasted_iota(jnp.int32, shape, 0) + shift[b]
        at = flip[b] * (L - 1) + (1 - 2 * flip[b]) * at
        source = (at & 1) * long + (at >> 1) + EDGE
        pick = jnp.where(lax.broadcasted_iota(jnp.int32, shape, 1) == source, 1.0, 0.0)
        pick = pick.astype(BF16)
        for side in range(2):
            cols = slice(side * width, (side + 1) * width)
            placed_back[side, b] = jnp.dot(
                pick, window[b, :, cols], preferred_element_type=F32
            ).astype(BF16)
        across = remote(
            placed_back.at[1 - s, b], final.at[b], core_send.at[b], core_recv.at[b], place.partner
        )
        across.start()
        save(placed_back.at[s, b], back_out.at[s * B + b], load_sem.at[2 * B + b])
        yield
        across.wait()
        save(final.at[b], back_out.at[(1 - s) * B + b], load_sem.at[3 * B + b])

    def adding():
        for stage in range(len(cube.events())):
            for block in range(blocks):
                cube.run(block, stage)
                if block % 3 == 2:
                    yield

    run_chains(chain, adding, B)
    cube.end()
    swap.wait()
    outs = (gain1_out, bias1_out, gain2_out, bias2_out, gain3_out, bias3_out)
    for i, to in enumerate(outs):
        count = to.shape[0]
        row = sums[0, i : i + 1, 0:count] + sums[1, i : i + 1, 0:count]
        to[...] = row.reshape(count)
    for copy in saved:
        copy.wait()


GRADS_STEP = 10


def run_chains(chain, adding, count):
    chains = [chain(b) for b in range(count)]
    taken = [0] * count
    extra = None

    def advance(b):
        taken[b] += 1
        return next(chains[b], "end") != "end"

    for b in range(count):
        advance(b)
    for b in range(count):
        advance(b)
    advance(0)
    live = list(range(count))
    while live:
        for b in list(live):
            if not advance(b):
                live.remove(b)
            if extra is None and taken[-1] >= GRADS_STEP:
                extra = adding()
            if extra is not None:
                next(extra, None)
    if extra is not None:
        for _ in extra:
            pass


class Cube:
    def __init__(self, place, blocks, base, refs):
        self.place, self.blocks, self.base = place, blocks, base
        self.total, self.inbox, self.relayed, self.summed, self.out = refs[:5]
        self.send_sem, self.core_recv, self.down_recv, self.up_recv, self.share_recv = refs[5:]
        self.sources = [None] * blocks
        self.axes = cube_axes(place)
        self.planar = place.nd.bit_length() - 1
        self.flight = [None] * blocks
        self.state = [None] * blocks

    def order(self, block):
        return [self.axes[i] for i in cube_order(block, self.planar, len(self.axes))]

    def events(self):
        depth = len(self.axes)
        return ["core"] + ["down"] * depth + ["up"] * halvings(depth) + ["share", "out"]

    def _add(self, block, incoming, first, count, send):
        total, inbox = self.total, self.inbox

        step = min(count, 4 * EDGE)
        for r in range(0, count, step):
            at = pl.ds(pl.multiple_of(first + r, EDGE), step)
            value = total[self.base + block, at] + incoming(r, step).astype(F32)
            total[self.base + block, at] = value
            if send:
                inbox[block, at] = value.astype(BF16)

    def run(self, block, stage):
        place, depth = self.place, len(self.axes)
        s = place.s
        last = depth + halvings(depth)
        if self.flight[block] is not None:
            self.flight[block].wait()
        if stage == 0:
            copy = remote(
                self.sources[block],
                self.inbox.at[block],
                self.send_sem.at[block],
                self.core_recv.at[block],
                place.partner,
            )
        elif stage <= depth:
            k = stage - 1
            partner, side = self.order(block)[k]
            size, first, past = sizes(k), [0], None
            if k > 0:
                first, past = self.state[block]
            offset = first[-1]
            if k == 0:
                incoming = lambda base: lambda r, n: self.inbox[
                    block, pl.ds(pl.multiple_of(base + r, EDGE), n)
                ]
                base_of = lambda at: at
            else:
                incoming = lambda base: lambda r, n: self.relayed[
                    block, pl.ds(pl.multiple_of(base + r, EDGE), n)
                ]
                base_of = lambda at: at - offset + region(k - 1)
            if size >= 2 * EDGE:
                small = size // 2
                give, hold = offset + (1 - side) * small, offset + side * small
                self._add(block, incoming(base_of(give)), give, small, True)
            else:
                small, give, hold = size, offset, offset
                self._add(block, incoming(base_of(give)), give, small, True)
                at = pl.ds(pl.multiple_of(give, EDGE), small)
                self.total[self.base + block, at] = self.inbox[block, at].astype(F32)
            copy = remote(
                self.inbox.at[block, pl.ds(pl.multiple_of(give, EDGE), small)],
                self.relayed.at[block, region(k) : region(k) + small],
                self.send_sem.at[block],
                self.down_recv.at[block, k],
                partner,
            )
            self.state[block] = (first + [hold], past)
        elif stage <= last:
            k = last - stage
            first, _ = self.state[block]
            partner, _ = self.order(block)[k]
            hold, small = first[k + 1], sizes(k + 1)
            at = pl.ds(pl.multiple_of(hold, EDGE), small)
            if stage == depth + 1:
                end = pl.ds(pl.multiple_of(first[-1], EDGE), sizes(depth))
                begin = region(depth - 1)
                self.summed[s, block, end] = (
                    self.total[self.base + block, end]
                    + self.relayed[block, begin : begin + sizes(depth)].astype(F32)
                ).astype(BF16)
            copy = remote(
                self.summed.at[s, block, at],
                self.summed.at[s, block, at],
                self.send_sem.at[block],
                self.up_recv.at[block, k],
                partner,
            )
        elif stage == last + 1:
            copy = remote(
                self.summed.at[s, block],
                self.summed.at[s, block],
                self.send_sem.at[block],
                self.share_recv.at[block],
                place.partner,
            )
        else:
            copy = pltpu.make_async_copy(
                self.summed.at[:, block], self.out.at[:, block], self.send_sem.at[block]
            )
        if stage > 0 and stage <= depth:
            copy.start()
            if size >= 2 * EDGE:
                self._add(block, incoming(base_of(hold)), hold, small, False)
        else:
            copy.start()
        self.flight[block] = copy

    def end(self):
        for copy in self.flight:
            copy.wait()


BLOCK = 256


def sizes(k):
    return max(BLOCK >> k, EDGE)


def region(k):
    return sum(sizes(i + 1) for i in range(k))


def halvings(depth):
    return sum(sizes(k) >= 2 * EDGE for k in range(depth))


def cube_axes(place):
    axes = []
    bit = 1
    while bit < place.nd:
        side = lax.rem(place.d // bit, 2)
        axes.append(((place.s, place.d + bit * (1 - 2 * side), place.q), side))
        bit *= 2
    bit = 1
    while bit < place.nq:
        side = lax.rem(place.q // bit, 2)
        axes.append(((place.s, place.d, place.q + bit * (1 - 2 * side)), side))
        bit *= 2
    return axes


def cube_order(block, planar, depth):
    kind = KINDS[block % len(KINDS)]
    order = [(kind + i) % planar for i in range(planar)] + list(range(planar, depth))
    if kind < 0:
        order.remove(planar)
        order = [planar] + order
    return order


def plan(planar, depth, blocks, pieces, events):
    rate, cost = 70e3, 0.15
    free = [0.0] * (depth + 1)
    ready = {}
    now, order, done = 0.0, [], 0.0
    pieces = list(pieces)

    def send(axis, size):
        if axis == depth:
            loads, speed, wait = [(depth, 1)], 6 * rate, 1.1
        elif axis > planar:
            loads, speed, wait = [(planar, 1), (axis, 2)], rate, 3.8
        else:
            loads, speed, wait = [(axis, 1)], rate, 3.2
        begin = max([now] + [free[i] for i, _ in loads])
        for i, times in loads:
            free[i] = begin + times * size / speed
        return max(free[i] for i, _ in loads) + wait

    while pieces or ready:
        able = sorted((t, b) for b, (t, _) in ready.items() if t <= now)
        if able:
            _, block = able[0]
            _, stage = ready.pop(block)
            order.append((block, stage))
            kind = events[stage]
            now += cost if kind == "down" else 0.05
            if stage + 1 < len(events):
                axes = cube_order(block, planar, depth)
                if kind in ("core", "share"):
                    axis, size = depth, BLOCK
                elif kind == "down":
                    axis, size = axes[stage - 1], sizes(stage)
                elif kind == "up":
                    k = depth + halvings(depth) - stage
                    axis, size = axes[k], sizes(k + 1)
                else:
                    axis, size = depth, 0
                ready[block] = (send(axis, 2 * size * 768), stage + 1)
        elif pieces and done + pieces[0][4] <= now:
            name, time, made, sends, _ = pieces.pop(0)
            order.append(name)
            now += time
            done = now
            for block in made:
                ready[block] = (now, 0)
            for axis, size in sends:
                send(axis, size)
        else:
            now = min([t for t, _ in ready.values()] + [done + p[4] for p in pieces[:1]])
    return order


def sum_kernel(
    dims,
    taps_in,
    grad_in,
    result_in,
    summed_out,
    near_out,
    far_out,
    total,
    inbox,
    sending,
    relayed,
    summed,
    product,
    taps,
    grads,
    load_sem,
    result_send,
    result_recv,
    *cube_sems,
):
    C, H, L, B, nd, nq = dims
    half = L // 2
    width = C // 2
    place = Place(nd, nq)
    s = place.s
    cross = (1 - s, place.d, place.mirror)
    mine = pl.ds(s * B, B)
    per_tap = C // BLOCK
    blocks = 5 * per_tap
    cube = Cube(place, blocks, 0, (total, inbox, relayed, summed, summed_out) + cube_sems)
    depth = len(cube.axes)
    load_grads = pltpu.make_async_copy(grad_in, grads, load_sem.at[6])
    load_taps = [
        pltpu.make_async_copy(
            taps_in.at[:, i * C : (i + 1) * C], taps.at[:, i * C : (i + 1) * C], load_sem.at[i]
        )
        for i in range(6)
    ]
    for copy in [load_grads] + load_taps:
        copy.start()
    meet = place.greet(place.plane() + place.line() + [place.partner, cross])
    for i in range(blocks):
        cube.sources[i] = sending.at[i]
    todo, pieces = {}, []

    def piece(name, time, made=(), sends=(), after=0.0):
        def keep(body):
            todo[name] = body
            pieces.append((name, time, made, sends, after))
            return body

        return keep

    across = remote(
        result_in.at[1 - s], near_out, result_send.at[0], result_recv.at[0], place.partner
    )
    away = [
        remote(
            result_in.at[side, b],
            far_out.at[s * B + b],
            result_send.at[1 + 2 * b + i],
            result_recv.at[1 + 2 * b + i],
            (side, place.d, place.mirror),
        )
        for b in range(B)
        for i, side in enumerate((s, 1 - s))
    ]

    def result_piece(i, after):
        @piece(("result", i), 0.05, (), [(depth - 1, 4 * half * width)], after)
        def _():
            away[i].start()

    def weight_piece(k):
        @piece(("weight", k), WEIGHT_TIME, range(k * per_tap, (k + 1) * per_tap))
        def _():
            if k == 0:
                load_grads.wait()
                load_taps[0].wait()
            load_taps[k + 1].wait()

            def tile(m, c):
                lanes = pl.multiple_of(k * C + m * BLOCK, BLOCK)
                product[...] = lax.dot_general(
                    taps[:, pl.ds(lanes, BLOCK)], grads[0], TN, preferred_element_type=F32
                ) + lax.dot_general(
                    taps[:, pl.ds(lanes + C, BLOCK)], grads[1], TN, preferred_element_type=F32
                )

                def split(r, c):
                    at = pl.ds(r, EDGE)
                    low = pl.ds(pl.multiple_of(s * width, width), width)
                    high = pl.ds(pl.multiple_of((1 - s) * width, width), width)
                    total[k * per_tap + m, at] = product[at, low]
                    sending[k * per_tap + m, at] = product[at, high].astype(BF16)
                    return c

                chunks(BLOCK, split)
                return c

            lax.fori_loop(0, per_tap, tile, 0)
            if k == 0:
                meet()
                across.start()

    early = len(away) // 2
    for k in range(5):
        weight_piece(k)
        if k < early:
            result_piece(k, 0.0)
    for i in range(early, len(away)):
        result_piece(i, LATE if i == early else 0.0)
    for item in plan(cube.planar, depth, blocks, pieces, cube.events()):
        if item in todo:
            todo[item]()
        else:
            cube.run(*item)
    cube.end()
    across.wait()
    for copy in away:
        copy.wait()


WEIGHT_TIME = 4.5
KINDS = (0, 1, 0, 1, 0, 1, 0, -1, 0, 1, 0, 0, 0, 1, 0)
LATE = 45.0


def finish_kernel(
    dims,
    first,
    later,
    mine,
    near,
    far,
    back,
    flips,
    *refs,
):
    vectors, outs, rest = refs[:6], refs[6:17], refs[17:]
    for src, dst in zip(vectors, outs[5:]):
        dst[...] = src[...]
    finish(dims, first, later, mine, near, far, back, flips, *outs[:5], *rest)


def finish(
    dims,
    first,
    later,
    mine,
    near,
    far,
    back,
    flips,
    conv1,
    conv2,
    conv3,
    result,
    back_out,
    held,
    wide,
    narrow,
    near_buf,
    far_buf,
    back_buf,
    in_sem,
    wide_sem,
    narrow_sem,
    side_sem,
):
    C, H, L, B, nd, nq = dims
    s = lax.axis_index("section")
    first_blocks = first.shape[1]
    blocks = first_blocks + later.shape[1]
    width = C // 2
    slots = wide.shape[0]

    def summed(block):
        return first.at[:, block] if block < first_blocks else later.at[:, block - first_blocks]

    order = list(range(first_blocks, blocks)) + list(range(first_blocks))
    loads = {
        block: pltpu.make_async_copy(summed(block), held.at[block], in_sem.at[block])
        for block in order
    }
    sides = [
        pltpu.make_async_copy(mine.at[s], near_buf.at[pl.ds(s * B, B)], side_sem.at[0]),
        pltpu.make_async_copy(near, near_buf.at[pl.ds((1 - s) * B, B)], side_sem.at[1]),
        pltpu.make_async_copy(far, far_buf, side_sem.at[2]),
        pltpu.make_async_copy(back, back_buf, side_sem.at[3]),
    ]
    for block in order[:4]:
        loads[block].start()
    for copy in sides:
        copy.start()
    for block in order[4:]:
        loads[block].start()
    bottom = 3 * C

    def targets(block, side):
        row = side * first_blocks * BLOCK + block * BLOCK
        if row < bottom:
            return [(0, BLOCK, conv2.at[row : row + BLOCK])]
        parts, at = [], 0
        while at < BLOCK:
            which, begin = (row - bottom + at) // H, (row - bottom + at) % H
            count = min(BLOCK - at, H - begin)
            cols = slice(which * width, (which + 1) * width)
            parts.append((at, count, conv3.at[begin : begin + count, cols]))
            at += count
        return parts

    going = [[] for _ in range(slots)]
    for i, block in enumerate(order):
        slot = i % slots
        for copy in going[slot]:
            copy.wait()
        loads[block].wait()
        for side in range(2):

            def widen(r, c):
                at = pl.ds(pl.multiple_of(r * 64, 64), 64)
                value = held[block, side, at].astype(F32)
                if block >= first_blocks:
                    wide[slot, at, side * width : (side + 1) * width] = value
                else:
                    narrow[slot, side, at] = value
                return c

            lax.fori_loop(0, BLOCK // 64, widen, 0, unroll=True)
        if block >= first_blocks:
            row = (block - first_blocks) * BLOCK
            going[slot] = [
                pltpu.make_async_copy(
                    wide.at[slot], conv1.at[row : row + BLOCK], wide_sem.at[slot]
                )
            ]
        else:
            parts = [(side, *part) for side in range(2) for part in targets(block, side)]
            going[slot] = [
                pltpu.make_async_copy(
                    narrow.at[slot, side, at : at + count], to, narrow_sem.at[slot, j]
                )
                for j, (side, at, count, to) in enumerate(parts)
            ]
        for copy in going[slot]:
            copy.start()
        if i == 2:
            sides[3].wait()
            give = pltpu.make_async_copy(back_buf, back_out, side_sem.at[3])
            give.start()
        if i == 4:
            for copy in sides[:3]:
                copy.wait()
            for b in range(2 * B):
                turned = flips[b]

                def deliver(r, c):
                    at = pl.ds(pl.multiple_of(r * 64, 64), 64)
                    near_buf[b, at] = jnp.where(
                        turned == 1, far_buf[b, at].astype(F32), near_buf[b, at].astype(F32)
                    ).astype(BF16)
                    return c

                lax.fori_loop(0, L // 128, deliver, 0)
            hand = pltpu.make_async_copy(near_buf, result, side_sem.at[0])
            hand.start()
    for copies in going:
        for copy in copies:
            copy.wait()
    give.wait()
    hand.wait()


def on_device(
    nd,
    nq,
    inputs,
    shifts,
    flips,
    gain1,
    bias1,
    weight1,
    gain2,
    bias2,
    weight2,
    gain3,
    bias3,
    weight3,
    out_grad,
):
    sequences, L, C = inputs.shape
    H = weight3.shape[0]
    B, half = sequences // 2, L // 2
    rows = B * half
    dims = (C, H, L, B, nd, nq)
    anywhere = pl.BlockSpec(memory_space=pl.ANY)
    vmem = pl.BlockSpec(memory_space=pltpu.VMEM)
    smem = pl.BlockSpec(memory_space=pltpu.SMEM)
    peers = nd - 1 + nq - 1
    shape = jax.ShapeDtypeStruct
    dma = pltpu.SemaphoreType.DMA
    width = C // 2
    side = (3 * C * H + H * C) // width // 2
    first_blocks = side // BLOCK
    later_blocks = 5 * C // BLOCK
    depth = (nd.bit_length() - 1) + (nq.bit_length() - 1)

    def cube_scratch(blocks):
        return [
            dma((blocks,)),
            dma((blocks,)),
            dma((blocks, depth)),
            dma((blocks, halvings(depth))),
            dma((blocks,)),
        ]

    taps, grads, result, first, back, *vectors = pl.pallas_call(
        functools.partial(chain_kernel, dims),
        name="chain",
        out_shape=(
            shape((rows, 6 * C), BF16),
            shape((2, rows, C), BF16),
            shape((2, B, half, width), BF16),
            shape((2, first_blocks, BLOCK, width), BF16),
            shape((2 * B, L, width), BF16),
        )
        + (shape((C,), F32),) * 4
        + (shape((H,), F32),) * 2,
        in_specs=[
            anywhere,
            anywhere,
            smem,
            smem,
            vmem,
            vmem,
            anywhere,
            vmem,
            vmem,
            anywhere,
            vmem,
            vmem,
            anywhere,
        ],
        out_specs=[anywhere] * 5 + [vmem] * 6,
        scratch_shapes=[
            pltpu.VMEM((B, L + 4 * EDGE, C), BF16),
            pltpu.VMEM((B, 2, half + EDGE, C), BF16),
            pltpu.VMEM((half + 2 * EDGE, C), F32),
            pltpu.VMEM((rows, 6 * C), BF16),
            pltpu.VMEM((5 * C, C), BF16),
            pltpu.VMEM((3 * C, H), BF16),
            pltpu.VMEM((H, C), BF16),
            pltpu.VMEM((half, C // 3), F32),
            pltpu.VMEM((half, C // 3), F32),
            pltpu.VMEM((rows, C), F32),
            pltpu.VMEM((B, half + 2 * EDGE, C), BF16),
            pltpu.VMEM((4, 2, B, 2, EDGE, C), BF16),
            pltpu.VMEM((4, 2, B, 2, EDGE, C), BF16),
            pltpu.VMEM((rows, 3 * C), BF16),
            pltpu.VMEM((rows, H), F32),
            pltpu.VMEM((B, half, C), BF16),
            pltpu.VMEM((B, half, C), BF16),
            pltpu.VMEM((rows, H), F32),
            pltpu.VMEM((rows, H), BF16),
            pltpu.VMEM((B, half + 2 * EDGE, H), BF16),
            pltpu.VMEM((rows, 3 * H), BF16),
            pltpu.VMEM((rows, C), F32),
            pltpu.VMEM((2 * first_blocks, BLOCK, width), F32),
            pltpu.VMEM((2 * first_blocks, BLOCK, width), BF16),
            pltpu.VMEM((first_blocks, BLOCK, width), BF16),
            pltpu.VMEM((first_blocks, region(depth), width), BF16),
            pltpu.VMEM((2, first_blocks, BLOCK, width), BF16),
            pltpu.VMEM((2, rows, C), BF16),
            pltpu.VMEM((2, B, half, width), BF16),
            pltpu.VMEM((2, rows, C), F32),
            pltpu.VMEM((2, B, L, width), BF16),
            pltpu.VMEM((B, L, width), BF16),
            pltpu.VMEM((2, 8, C), F32),
            pltpu.VMEM((6 * B, nd, 2, C), F32),
            pltpu.VMEM((6 * B, nq, 2, C), F32),
            dma((6,)),
            dma((4 * B,)),
            dma((2 * B, peers)),
            dma((2 * B, peers)),
            dma((5, B, 2)),
            dma((5, B, 2)),
            dma((B, 4)),
            dma((B, 4)),
            dma((B + 1,)),
            dma((B + 1,)),
        ]
        + cube_scratch(first_blocks),
        compiler_params=pltpu.CompilerParams(
            collective_id=0, has_side_effects=True, vmem_limit_bytes=60 * 2**20
        ),
    )(
        inputs,
        out_grad,
        shifts,
        flips,
        gain1,
        bias1,
        weight1.reshape(5 * C, C),
        gain2,
        bias2,
        weight2.reshape(3 * C, H),
        gain3,
        bias3,
        weight3,
    )
    later, near, far = pl.pallas_call(
        functools.partial(sum_kernel, dims),
        name="weight_sum",
        out_shape=(
            shape((2, later_blocks, BLOCK, width), BF16),
            shape((B, half, width), BF16),
            shape((2 * B, half, width), BF16),
        ),
        in_specs=[anywhere] * 3,
        out_specs=[anywhere] * 3,
        scratch_shapes=[
            pltpu.VMEM((later_blocks, BLOCK, width), F32),
            pltpu.VMEM((later_blocks, BLOCK, width), BF16),
            pltpu.VMEM((later_blocks, BLOCK, width), BF16),
            pltpu.VMEM((later_blocks, region(depth), width), BF16),
            pltpu.VMEM((2, later_blocks, BLOCK, width), BF16),
            pltpu.VMEM((BLOCK, C), F32),
            pltpu.VMEM((rows, 6 * C), BF16),
            pltpu.VMEM((2, rows, C), BF16),
            dma((7,)),
            dma((1 + 2 * B,)),
            dma((1 + 2 * B,)),
        ]
        + cube_scratch(later_blocks),
        compiler_params=pltpu.CompilerParams(
            collective_id=1, has_side_effects=True, vmem_limit_bytes=60 * 2**20
        ),
    )(taps, grads, result)
    blocks = first_blocks + later_blocks
    slots = 6
    conv1, conv2, conv3, result, back, *vectors = pl.pallas_call(
        functools.partial(finish_kernel, dims),
        name="widen",
        out_shape=(
            shape((5 * C, C), F32),
            shape((3 * C, H), F32),
            shape((H, C), F32),
            shape((2 * B, half, width), BF16),
            shape((2 * B, L, width), BF16),
        )
        + (shape((C,), F32),) * 4
        + (shape((H,), F32),) * 2,
        in_specs=[anywhere] * 6 + [smem] + [vmem] * 6,
        out_specs=[anywhere] * 5 + [vmem] * 6,
        scratch_shapes=[
            pltpu.VMEM((blocks, 2, BLOCK, width), BF16),
            pltpu.VMEM((slots, BLOCK, C), F32),
            pltpu.VMEM((slots, 2, BLOCK, width), F32),
            pltpu.VMEM((2 * B, half, width), BF16),
            pltpu.VMEM((2 * B, half, width), BF16),
            pltpu.VMEM((2 * B, L, width), BF16),
            dma((blocks,)),
            dma((slots,)),
            dma((slots, 4)),
            dma((4,)),
        ],
        compiler_params=pltpu.CompilerParams(vmem_limit_bytes=60 * 2**20),
    )(first, later, result, near, far, back, flips, *vectors)
    return (
        result,
        back,
        conv1.reshape(5, C, C),
        vectors[0],
        vectors[1],
        conv2.reshape(3, C, H),
        vectors[2],
        vectors[3],
        conv3,
        vectors[4],
        vectors[5],
    )


def solution(mesh):
    whole = P()
    split = P("dp", "seq", None)
    return jax.shard_map(
        functools.partial(on_device, mesh.shape["dp"], mesh.shape["seq"]),
        mesh=mesh,
        in_specs=(split, P("dp"), P("dp")) + (whole,) * 9 + (split,),
        out_specs=(P("dp", "seq", "section"),) * 2 + (whole,) * 9,
        check_vma=False,
    )
```
